32 devices in a mesh: dp: 8 (over z, core), tensor: 4 (over y, x).
Axes of the slice: x: 2, y: 2, z: 4, core: 2. Of those that a mesh axis runs over, the one named last changes fastest.
Arguments:
- features: bfloat16 [4096, 6144], P('tensor', 'dp'), may hold values from -6 to 6
- cotangent: bfloat16 [4096, 6144], P('tensor', 'dp'), may hold values from -6 to 6
- up_blocks: bfloat16 [16, 256, 1024], P('tensor'), may hold values from -0.375 to 0.375
- down_blocks: bfloat16 [16, 1024, 256], P('tensor'), may hold values from -0.1875 to 0.1875
Outputs:
- outputs: bfloat16 [4096, 6144], P('tensor', 'dp')
- feature_grads: bfloat16 [4096, 6144], P('tensor', 'dp')
- up_grads: float32 [16, 256, 1024], P('tensor', 'dp')
- down_grads: float32 [16, 1024, 256], P('tensor', 'dp')
The draws below stay inside these ranges and needn't reach their ends.
All inputs are finite; a program needn't handle non-finite values.
Results may differ from the reference program's by a relative error of at most 0.015.
Values may be sent and summed in bfloat16 or wider, within the bound.
No kernel may reach another device: no remote copies, remote signals or barrier semaphores. Data moves between devices by JAX's collectives and lax.ppermute only.
A program may use at most 64 MiB of HBM per device.

```python
import math
import jax
import jax.numpy as jnp
from jax import lax

D = 4096
BLOCKS = 16
TOK_DEV = 768
TOKENS = 6144
DB = 256
FB = 1024
SUB = 64
N_DP = 8


def steps_of(key, dims, cuts, least, top_value):
    gain = 1.0
    for axis_at, parts in cuts:
        heights = jax.random.uniform(jax.random.fold_in(jax.random.fold_in(key, 6), axis_at), (parts,), jnp.float32, least / len(cuts), top_value / len(cuts))
        gain = gain * jnp.repeat(jnp.exp(heights), dims[axis_at] // parts).reshape((-1,) + (1,) * (len(dims) - 1 - axis_at))
    return gain


def normal_values(rng, shape, width, bound, shards=(), kind=jnp.bfloat16):
    loudness = steps_of(rng, shape, shards, -0.22, 0.18) if shards else 1.0
    entries = jax.random.normal(rng, shape, jnp.float32) * width * loudness
    return jnp.minimum(jnp.maximum(entries, -bound), bound).astype(kind)


def setup_inputs(seed: int = 0) -> dict:
    keys = jax.random.split(jax.random.key(seed), 5)
    features = normal_values(keys[0], (D, TOKENS), 1.0, 6.0, ((0, 4), (1, 8)))
    cotangent = normal_values(keys[1], (D, TOKENS), 1.0, 6.0, ((0, 4), (1, 8)))
    up_blocks = normal_values(keys[2], (BLOCKS, DB, FB), DB ** -0.5, 0.375, ((0, 4),))
    down_blocks = normal_values(keys[3], (BLOCKS, FB, DB), FB ** -0.5, 0.1875, ((0, 4),))
    return dict(features=features, cotangent=cotangent, up_blocks=up_blocks, down_blocks=down_blocks)


INV_ROOT2 = 0.7071067811865476
INV_ROOT2PI = 0.3989422804014327

def gelu_value(value):
    return 0.5 * value * (1.0 + lax.erf(value * INV_ROOT2))

def gelu_slope(value):
    return 0.5 * (1.0 + lax.erf(value * INV_ROOT2)) + value * jnp.exp(-0.5 * value * value) * INV_ROOT2PI

def rounded(value):
    return lax.optimization_barrier(value.astype(jnp.bfloat16)).astype(jnp.float32)

def reference(features, cotangent, up_blocks, down_blocks):
    up_wide = up_blocks.astype(jnp.float32)
    down_wide = down_blocks.astype(jnp.float32).reshape(BLOCKS, BLOCKS, SUB, DB)

    def step(carry, index):
        grad_up, grad_down = carry
        begin = (index * TOK_DEV).astype(jnp.int32)
        x_block = lax.dynamic_slice_in_dim(features, begin, TOK_DEV, 1).astype(jnp.float32).reshape(BLOCKS, DB, TOK_DEV)
        dy_block = lax.dynamic_slice_in_dim(cotangent, begin, TOK_DEV, 1).astype(jnp.float32).reshape(BLOCKS, DB, TOK_DEV)
        preact = rounded(jnp.einsum('bdn,bdf->bfn', x_block, up_wide))
        hidden = rounded(gelu_value(preact)).reshape(BLOCKS, BLOCKS, SUB, TOK_DEV)
        out_block = jnp.einsum('ijsn,jise->jen', hidden, down_wide).astype(jnp.bfloat16).reshape(D, TOK_DEV)
        back = rounded(jnp.einsum('jen,jise->ijsn', dy_block, down_wide)).reshape(BLOCKS, FB, TOK_DEV)
        slope = rounded(back * gelu_slope(preact))
        dx_block = jnp.einsum('bfn,bdf->bdn', slope, up_wide).astype(jnp.bfloat16).reshape(D, TOK_DEV)
        grad_up = grad_up + jnp.einsum('bdn,bfn->bdf', x_block, slope)
        grad_down = grad_down + jnp.einsum('ijsn,jen->jise', hidden, dy_block).reshape(BLOCKS, FB, DB)
        return ((grad_up, grad_down), (out_block, dx_block))
    start_up = jnp.zeros((BLOCKS, DB, FB), jnp.float32)
    start_down = jnp.zeros((BLOCKS, FB, DB), jnp.float32)
    (grad_up, grad_down), (outs, dxs) = lax.scan(step, (start_up, start_down), jnp.arange(N_DP, dtype=jnp.int32))
    outputs = jnp.transpose(outs, (1, 0, 2)).reshape(D, TOKENS)
    feature_grads = jnp.transpose(dxs, (1, 0, 2)).reshape(D, TOKENS)
    factor = 1.0 / math.sqrt(TOKENS)
    return (outputs, feature_grads, grad_up * factor, grad_down * factor)
```

```python
import functools
import math

import jax
import jax.numpy as jnp
from jax import lax
from jax.experimental import pallas as pl
from jax.experimental.pallas import tpu as pltpu
from jax.sharding import PartitionSpec as P

BF16 = jnp.bfloat16
F32 = jnp.float32
INV_ROOT2 = 0.7071067811865476
INV_ROOT2PI = 0.3989422804014327
MIB = 1024 * 1024


def gelu_value(value):
    return 0.5 * value * (1.0 + lax.erf(value * INV_ROOT2))


def gelu_slope(value):
    return (
        0.5 * (1.0 + lax.erf(value * INV_ROOT2))
        + value * jnp.exp(-0.5 * value * value) * INV_ROOT2PI
    )


def generic_device(features, cotangent, up_blocks, down_blocks):
    local_blocks, block_feat, block_hidden = up_blocks.shape
    blocks = local_blocks * lax.axis_size("tensor")
    sub = block_hidden // blocks
    tokens_here = features.shape[1]
    factor = 1.0 / math.sqrt(tokens_here * lax.axis_size("dp"))
    x_local = features.reshape(local_blocks, block_feat, tokens_here)
    dy_local = cotangent.reshape(local_blocks, block_feat, tokens_here)
    down_four = down_blocks.reshape(local_blocks, blocks, sub, block_feat)
    preact = jnp.einsum("bdn,bdf->bfn", x_local, up_blocks, preferred_element_type=F32)
    pre_wide = preact.astype(BF16).astype(F32)
    hidden = gelu_value(pre_wide).astype(BF16).reshape(local_blocks, blocks, sub, tokens_here)
    mixed = lax.all_to_all(hidden, "tensor", split_axis=1, concat_axis=0, tiled=True)
    out_three = jnp.einsum("ijsn,jise->jen", mixed, down_four, preferred_element_type=F32)
    outputs = out_three.astype(BF16).reshape(local_blocks * block_feat, tokens_here)
    down_term = jnp.einsum("ijsn,jen->isje", mixed, dy_local, preferred_element_type=F32)
    down_term = down_term.reshape(block_hidden, local_blocks, block_feat)
    back = jnp.einsum("jen,jise->ijsn", dy_local, down_four, preferred_element_type=F32)
    back_home = lax.all_to_all(
        back.astype(BF16), "tensor", split_axis=0, concat_axis=1, tiled=True
    ).reshape(local_blocks, block_hidden, tokens_here)
    slope = (back_home.astype(F32) * gelu_slope(pre_wide)).astype(BF16)
    up_term = jnp.einsum("bdn,bfn->dbf", x_local, slope, preferred_element_type=F32)
    up_share = lax.psum_scatter(up_term, "dp", scatter_dimension=0, tiled=True)
    down_share = lax.psum_scatter(down_term, "dp", scatter_dimension=0, tiled=True)
    dx_three = jnp.einsum("bfn,bdf->bdn", slope, up_blocks, preferred_element_type=F32)
    feature_grads = dx_three.astype(BF16).reshape(local_blocks * block_feat, tokens_here)
    up_grads = jnp.transpose(up_share, (1, 0, 2)) * factor
    down_grads = jnp.transpose(down_share, (1, 0, 2)) * factor
    return (outputs, feature_grads, up_grads, down_grads)


def dot_tn(a, b):
    return lax.dot_general(a, b, (((0,), (0,)), ((), ())), preferred_element_type=F32)


def dot_nn(a, b):
    return lax.dot_general(a, b, (((1,), (0,)), ((), ())), preferred_element_type=F32)


def dot_nt(a, b):
    return lax.dot_general(a, b, (((1,), (1,)), ((), ())), preferred_element_type=F32)


def call(body, place, grid, ins, outs, mib, scratch=(), span=0.0):
    return pl.pallas_call(
        body,
        grid_spec=pltpu.PrefetchScalarGridSpec(
            num_scalar_prefetch=1,
            grid=grid,
            in_specs=[pl.BlockSpec(b, m) for _, b, m in ins],
            out_specs=[pl.BlockSpec(b, m) for _, _, b, m in outs],
            scratch_shapes=list(scratch),
        ),
        out_shape=[jax.ShapeDtypeStruct(s, d) for s, d, _, _ in outs],
        compiler_params=pltpu.CompilerParams(vmem_limit_bytes=mib * MIB),
        cost_estimate=pl.CostEstimate(
            flops=int(span * 1e9), bytes_accessed=0, transcendentals=0
        ),
    )(place, *[a for a, _, _ in ins])


def block_of(ref, block, where):
    at = []
    for size, extent, index in zip(block, ref.shape, where):
        if size == extent:
            at.append(slice(None))
        elif isinstance(index, int):
            at.append(slice(index * size, (index + 1) * size))
        else:
            at.append(pl.ds(pl.multiple_of(index * size, size), size))
    return ref.at[tuple(at)]


def call_once(body, place, steps, ins, outs, mib, scratch=(), span=0.0):
    def every_step(place, *refs):
        blocks = [(b, m) for _, b, m in ins] + [(b, m) for _, _, b, m in outs]
        held, rest = refs[: len(blocks)], refs[len(blocks) :]
        for step in range(steps):
            views = [block_of(ref, b, m(step, place)) for ref, (b, m) in zip(held, blocks)]
            body(step, steps, place, *views, *rest)

    return call(
        every_step,
        place,
        (1,),
        [whole(a) for a, _, _ in ins],
        [whole_out(s, d) for s, d, _, _ in outs],
        mib,
        scratch=scratch,
        span=span,
    )


def by_grid(body):
    return lambda place, *refs: body(pl.program_id(0), pl.num_programs(0), place, *refs)


def whole(array):
    rank = array.ndim
    return (array, array.shape, lambda *at: (0,) * rank)


def whole_out(shape, kind):
    rank = len(shape)
    return (shape, kind, shape, lambda *at: (0,) * rank)


def after(values, *earlier):
    return lax.optimization_barrier((tuple(values), earlier))[0]


def square(ref):
    block = ref[...]
    width = block.shape[-1]
    return block.reshape(block.size // width, width)


def hidden_body(place, x_ref, up_ref, hidden_ref, gate_ref):
    pre = dot_tn(square(up_ref), square(x_ref)).astype(BF16).astype(F32)
    half_cdf = 0.5 + 0.5 * lax.erf(pre * INV_ROOT2)
    gate = half_cdf + pre * jnp.exp(-0.5 * pre * pre) * INV_ROOT2PI
    hidden_ref[...] = (pre * half_cdf).astype(BF16).reshape(hidden_ref.shape)
    gate_ref[...] = gate.astype(BF16).reshape(gate_ref.shape)


def weights_body(place, *refs):
    low, core, out_ref = place[1] % 2, place[2], refs[-1]
    for at in range(2):
        out_ref[:, :, :, core * 2 + (low ^ at)] = refs[at][...]
        out_ref[:, :, :, (1 - core) * 2 + (low ^ at)] = refs[2 + at][...]


def halves(step, steps, work, lo, hi):
    if isinstance(step, int):
        work(*(lo if step < steps // 2 else hi))
        return
    pl.when(step < steps // 2)(functools.partial(work, *lo))
    pl.when(step >= steps // 2)(functools.partial(work, *hi))


def put_slope(cot, down_ref, gate_ref, slope_ref):
    back = dot_nn(square(down_ref), cot).astype(BF16).astype(F32)
    slope = (back * square(gate_ref).astype(F32)).astype(BF16)
    slope_ref[...] = slope.reshape(slope_ref.shape)


def slope_body(step, steps, place, cot_ref, down_ref, gate_ref, slope_ref):
    put_slope(square(cot_ref), down_ref, gate_ref, slope_ref)


def late_slopes_body(step, steps, place, own_ref, near_lo, near_hi, *refs):
    downs, gates, slopes = refs[:4], refs[4:8], refs[8:]
    put_slope(square(own_ref), downs[3], gates[3], slopes[3])

    def work(near_ref):
        for at in range(3):
            put_slope(square(near_ref), downs[at], gates[at], slopes[at])

    halves(step, steps, work, (near_lo,), (near_hi,))


def own_terms_body(step, steps, place, cot_ref, hid_ref, x_ref, slope_ref, give_ref, keep_ref, down_s, up_s):
    core = place[2]
    up_s[...] = dot_nt(square(x_ref), square(slope_ref)).astype(BF16).reshape(up_s.shape)
    count = up_s.shape[2]
    strip = slice(step * count, (step + 1) * count)
    give_ref[0, :, strip] = up_s[:, 1 - core]
    keep_ref[0, :, strip] = up_s[:, core]
    down_s[...] = dot_nt(square(hid_ref), square(cot_ref)).astype(BF16).reshape(down_s.shape)
    give_ref[1, step] = down_s[1 - core]
    keep_ref[1, step] = down_s[core]


def down_terms_body(step, steps, place, own_ref, near_lo, near_hi, sn, ns_lo, ns_hi, nn_lo, nn_hi, give_own, give_near, keep_ref, term_s):
    core = place[2]

    def put(pair, lo, hi, cot, give):
        term_s[0], term_s[1] = (dot_nt(v, cot).astype(BF16) for v in (lo, hi))
        give[...] = term_s[1 - core].reshape(give.shape)
        keep_ref[pair, 0] = term_s[core]

    def work(near_ref):
        own, near = square(own_ref), square(near_ref)
        mixed = square(sn)
        part = mixed.shape[0] // 2
        put(0, mixed[:part], mixed[part:], near, give_own)
        put(1, square(ns_lo), square(ns_hi), own, give_near.at[0])
        put(2, square(nn_lo), square(nn_hi), near, give_near.at[1])

    halves(step, steps, work, (near_lo,), (near_hi,))


def put_up_term(pair, core, x, slope_ref, give_ref, keep_ref, term_s):
    term_s[...] = dot_nt(x, square(slope_ref)).astype(BF16).reshape(term_s.shape)
    give_ref[pair] = term_s[:, 1 - core]
    keep_ref[pair] = term_s[:, core]


def up_terms_body(step, steps, place, x_ref, x_lo, x_hi, sn, lo_s, lo_n, hi_s, hi_n, give_lo, give_hi, keep_ref, term_s):
    def work(x_near, from_own, from_near, give_ref):
        near = square(x_near)
        for pair, (x, ref) in enumerate(((square(x_ref), sn), (near, from_own), (near, from_near))):
            put_up_term(pair, place[2], x, ref, give_ref, keep_ref, term_s)

    lo, hi = (x_lo, lo_s, lo_n, give_lo), (x_hi, hi_s, hi_n, give_hi)
    halves(step, steps, work, lo, hi)


def outputs_body(step, steps, place, d_own, d_lo, d_hi, hid_ref, lo_ref, hi_ref, *rest):
    total = dot_tn(square(d_own), square(hid_ref))
    total = total + dot_tn(square(d_lo), square(lo_ref))
    total = total + dot_tn(square(d_hi), square(hi_ref))
    for ref in rest[:-1]:
        total = total + ref[0].astype(F32)
    rest[-1][0] = total.astype(BF16)


def near_grads_body(step, steps, place, up_own, up_near, lo_s, lo_n, hi_s, hi_n, out_ref):
    def work(slope_own, slope_near):
        total = dot_nn(square(up_own), square(slope_own))
        total = total + dot_nn(square(up_near), square(slope_near))
        out_ref[0] = total.astype(BF16)

    halves(step, steps, work, (lo_s, lo_n), (hi_s, hi_n))


def grads_body(step, steps, place, up_own, up_near, slope_own, slope_near, add_ref, out_ref):
    total = dot_nn(square(up_own), square(slope_own)) + dot_nn(square(up_near), square(slope_near))
    out_ref[0] = (total + add_ref[0].astype(F32)).astype(BF16)


def down_meet_body(place, first, first_got, keep_ref, got_own, got_near, send_ref, mine_ref, total_s):
    stay = (place[0] ^ place[1]) & 1
    total_s[0, 0] = first[1].astype(F32) + first_got[1].astype(F32)
    total_s[0, 1] = keep_ref[0].astype(F32) + got_own[...].astype(F32)
    total_s[1] = keep_ref[1:].astype(F32) + got_near[...].astype(F32)
    mine_ref[...] = total_s[stay]
    send_ref[...] = total_s[1 - stay].astype(BF16)


def down_again_body(place, mine_ref, got_ref, send_ref, own_ref):
    stay = (place[0] // 2) ^ (place[1] // 2)
    own_ref[...] = mine_ref[stay] + got_ref[stay].astype(F32)
    send_ref[...] = (mine_ref[1 - stay] + got_ref[1 - stay].astype(F32)).astype(BF16)


def down_sum_body(factor, place, own_ref, got_ref, out_ref):
    out_ref[...] = ((own_ref[...] + got_ref[...].astype(F32)) * factor).astype(BF16)


def up_meet_body(parts, place, keep_ref, *refs):
    gots, sends, mine_ref = refs[:parts], refs[parts:-1], refs[-1]
    rows = gots[0].shape[2]
    for hop in range(4):
        there = place[1] ^ hop
        for at, got_ref in enumerate(gots):
            strip = slice(at * rows, (at + 1) * rows)
            total = keep_ref[:, there, strip].astype(F32) + got_ref[:, there].astype(F32)
            if hop % 2:
                sends[hop // 2][:, strip] = total.astype(BF16)
            else:
                mine_ref[hop // 2, :, strip] = total


def up_again_body(place, mine_ref, got_ref, got_far, send_ref, own_ref):
    send_ref[...] = (mine_ref[1] + got_far[...].astype(F32)).astype(BF16)
    own_ref[...] = mine_ref[0] + got_ref[...].astype(F32)


def up_sum_body(factor, place, first_ref, first_got, own_ref, got_ref, send_ref, mine_ref):
    mine_ref[0] = (first_ref[0] + first_got[0].astype(F32)) * factor
    total = (own_ref[...] + got_ref[...].astype(F32)) * factor
    mine_ref[1] = total[0]
    send_ref[...] = total[1:].astype(BF16)


def place_body(place, mine_ref, got_ref, down_in, up_ref, down_ref):
    down_ref[...] = down_in[...].astype(F32)
    width = mine_ref.shape[-1]
    for ref, side in ((mine_ref, 0), (got_ref, 1)):
        for at in range(2):
            where = place[0] ^ side ^ (2 * at)
            lanes = pl.ds(pl.multiple_of(where * width, width), width)
            up_ref[:, :, lanes] = ref[at].astype(F32).reshape(*up_ref.shape[:2], width)


def square_device(features, cotangent, up_blocks, down_blocks):
    local, feat, block_hidden = up_blocks.shape
    tokens = features.shape[1]
    n_dp, n_tensor = lax.axis_size("dp"), lax.axis_size("tensor")
    sub = block_hidden // (local * n_tensor)
    rows = local * sub
    half, part = local // 2, rows // 2
    factor = 1.0 / math.sqrt(tokens * n_dp)
    me = lax.axis_index("tensor").astype(jnp.int32)
    rank = lax.axis_index("dp").astype(jnp.int32)
    z, core = rank >> 1, rank & 1
    place = jnp.stack([me, z, core])
    x = features.reshape(local, feat, tokens)
    cot = cotangent.reshape(local, feat, tokens)
    one = (1, feat, tokens)
    blocks = (local, feat, tokens)
    every = lambda i, p: (i, 0, 0)
    least = lambda a, b: min(a, b) if isinstance(a, int) else jnp.minimum(a, b)
    most = lambda a, b: max(a, b) if isinstance(a, int) else jnp.maximum(a, b)
    low = lambda i, p: (least(i, half - 1), 0, 0)
    high = lambda i, p: (most(i - half, 0), 0, 0)

    def send(value, hop):
        return lax.ppermute(value, "tensor", [(t, t ^ hop) for t in range(n_tensor)])

    def send_z(value, hop):
        return lax.ppermute(value, "dp", [(d, d ^ (2 * hop)) for d in range(n_dp)])

    def send_core(value):
        return lax.ppermute(value, "dp", [(d, d ^ 1) for d in range(n_dp)])

    quarter = rows // 4
    at = (core * 2 + (z & 1)) * quarter
    to_x = jnp.stack(
        [
            lax.dynamic_slice(up_blocks, (0, at, (me ^ k) * rows), (local, quarter, rows))
            for k in (1, 3)
        ]
    )
    to_y = jnp.stack(
        [
            lax.dynamic_slice(down_blocks, (0, (me ^ k) * rows + at, 0), (local, quarter, feat))
            for k in (2, 3)
        ]
    )
    from_x, from_y = send(to_x, 1), send(to_y, 2)
    firsts = after((x[:half], x[half:], cot[:half], cot[half:]), to_x, to_y)
    x_lo, cot_lo = send(firsts[0], 1), send(firsts[2], 2)
    x_hi, cot_hi = send(firsts[1], 1), send(firsts[3], 2)

    def hidden_of(source, count, up, span):
        unit = (2, local, count, sub, tokens)
        block = (1, local, 1, sub, tokens)
        where = lambda j, i, p: (j, 0, i, 0, 0)
        return call(
            hidden_body,
            place,
            (2, count),
            [(source, one, lambda j, i, p: (i, 0, 0)), up],
            [(unit, BF16, block, where), (unit, BF16, block, where)],
            16,
        )

    hid, gate = hidden_of(
        x, local, (up_blocks, (1, feat, rows), lambda j, i, p: (i, 0, p[0] ^ (2 * j))), 0.0
    )
    from_x, from_y = after((from_x, from_y), hid)
    share = jnp.stack([from_x, from_y])
    share_z = send_z(share, 1)

    def unit_of(array, j):
        return (array, (1, 1) + array.shape[2:], lambda i, p: (j, i, 0, 0, 0))

    def down_of(j, which):
        if j == 0:
            if which == 0:
                return (down_blocks, (1, rows, feat), lambda i, p: (i, p[0], 0))
            return (
                down_blocks,
                (1, part, feat),
                lambda i, p: (i, 2 * (p[0] ^ 1) + which - 1, 0),
            )
        if which == 0:
            return (weights, (1, 1, 1, rows, feat), lambda i, p: (1, 0, i, 0, 0))
        return (weights, (1, 1, 1, part, feat), lambda i, p: (1, 1, i, which - 1, 0))

    def own_slope(which, array):
        return call_once(
            slope_body,
            place,
            local,
            [(cot, one, every), down_of(0, which), unit_of(array, 0)],
            [(array.shape[1:], BF16, (1,) + array.shape[2:], lambda i, p: (i, 0, 0, 0))],
            20,
        )[0]

    slope_ss = own_slope(0, gate)
    at_i = lambda i, p: (0, i, 0, 0)
    strip = (local, 1, sub, tokens)
    shard_u = (n_dp // 2, local * feat // n_dp, rows)

    def up_terms(body, ins, count, gives, span):
        block = (count, n_dp // 2, feat // n_dp, rows)
        wide = (count,) + shard_u
        part_u = (count, n_dp // 2, shard_u[1] // len(gives), rows)
        return call_once(
            body,
            place,
            local,
            ins,
            [
                (part_u, BF16, block, functools.partial(lambda m, i, p: (0, 0, m(i), 0), m))
                for m in gives
            ]
            + [(wide, BF16, block, lambda i, p: (0, 0, i, 0))],
            20,
            scratch=[pltpu.VMEM((n_dp // 2, 2, feat // n_dp, rows), BF16)],
            span=span,
        )

    def up_meet(count, keep, gots):
        piece = (count,) + shard_u[1:]
        return call(
            functools.partial(up_meet_body, len(gots)),
            place,
            (1,),
            [(v, (count,) + v.shape[1:], lambda i, p: (0, 0, 0, 0)) for v in (keep, *gots)],
            [whole_out(piece, BF16)] * 2 + [whole_out((2,) + piece, F32)],
            16,
        )

    def up_again(mine, got, far):
        piece = mine.shape[1:]
        return call(
            up_again_body,
            place,
            (1,),
            [whole(mine), whole(got), whole(far)],
            [whole_out(piece, BF16), whole_out(piece, F32)],
            16,
        )

    give_e, keep_e = call_once(
        own_terms_body,
        place,
        local,
        [
            (cot, one, every),
            unit_of(hid, 0),
            (x, one, every),
            (slope_ss, strip, at_i),
        ],
        [whole_out((2,) + shard_u, BF16)] * 2,
        20,
        scratch=[
            pltpu.VMEM((2, part, feat), BF16),
            pltpu.VMEM((n_dp // 2, 2, feat // n_dp, rows), BF16),
        ],
    )
    share, share_z, x_lo, cot_lo = after((share, share_z, x_lo, cot_lo), give_e)
    core_parts = after((share, share_z), x_lo, cot_lo)
    weights = call(
        weights_body,
        place,
        (1,),
        [whole(v) for v in (share, share_z, *map(send_core, core_parts))],
        [whole_out((2, 2, local, 4, quarter, feat), BF16)],
        16,
    )[0].reshape(2, 2, local, rows, feat)

    def near_hidden(source, which):
        up = (
            weights,
            (1, 1, 1, feat, rows),
            lambda j, i, p: (0, j, which * half + i, 0, 0),
        )
        return hidden_of(source, half, up, 0.0)

    give_e = after((give_e,), x_lo, cot_lo)[0]
    first_got = send_core(give_e)
    send_e, far_e, mine_e = up_meet(1, keep_e, [first_got])
    got_e, far_e = send_z(send_e, 1), send_z(far_e, 1)
    x_lo = after((x_lo,), weights, send_e)[0]
    hid_lo, gate_lo = near_hidden(x_lo, 0)
    slope_lo_s = own_slope(1, gate_lo)

    got_e, far_e = after((got_e, far_e), slope_lo_s)
    send_e, mine_e = up_again(mine_e, got_e, far_e)
    got_e = send_z(send_e, 2)

    x_hi, cot_hi = after((x_hi, cot_hi), got_e)
    hid_hi, gate_hi = near_hidden(x_hi, 1)

    def outputs_of(j, hid, adds):
        run = functools.partial(call, by_grid(outputs_body), place, (local,))
        if not adds:
            run = functools.partial(call_once, outputs_body, place, local)
        return run(
            [down_of(j, which) for which in range(3)]
            + [unit_of(array, j) for array in (hid, hid_lo, hid_hi)]
            + [(a, one, every) for a in adds],
            [(blocks, BF16, one, every)],
            16,
        )[0]

    shard = (2, 2, local, part, feat)
    strip_d = (1, part, feat)
    give_own, give_near, keep_d = call_once(
        down_terms_body,
        place,
        local,
        [(cot, one, every), (cot_lo, one, low), (cot_hi, one, high)]
        + [unit_of(hid, 1)]
        + [unit_of(array, j) for j in (0, 1) for array in (hid_lo, hid_hi)],
        [
            (shard[2:], BF16, strip_d, every),
            (shard[1:], BF16, (2,) + strip_d, lambda i, p: (0, i, 0, 0)),
            ((3,) + shard[2:], BF16, (3,) + strip_d, lambda i, p: (0, i, 0, 0)),
        ],
        16,
        scratch=[pltpu.VMEM((2, part, feat), BF16)],
    )
    core_own, core_near = send_core(give_own), send_core(give_near)
    hid_b = after((hid,), give_own)[0]
    near_out = outputs_of(1, hid_b, [])
    got_out = send(near_out, 2)
    core_own, core_near = after((core_own, core_near), near_out)
    parts_d = (keep_e, first_got, keep_d, core_own, core_near)
    send_d, mine_d = call(
        down_meet_body,
        place,
        (1,),
        [whole(v) for v in parts_d],
        [whole_out(shard[1:], BF16), whole_out(shard[1:], F32)],
        16,
        scratch=[pltpu.VMEM(shard, F32)],
    )
    got_d = send_z(send_d, 1)
    cot_b, *near_b = after((cot, cot_lo, cot_hi), send_d)
    late = [(1, 0, gate), (1, 1, gate_lo), (1, 2, gate_hi), (0, 2, gate_hi)]
    slope_sn, slope_lo_n, slope_hi_n, slope_hi_s = call_once(
        late_slopes_body,
        place,
        local,
        [(cot_b, one, every), (near_b[0], one, low), (near_b[1], one, high)]
        + [down_of(j, which) for j, which, _ in late]
        + [unit_of(array, j) for j, _, array in late],
        [
            (array.shape[1:], BF16, (1,) + array.shape[2:], lambda i, p: (i, 0, 0, 0))
            for _, _, array in late
        ],
        20,
    )

    at_lo = lambda i, p: (0, least(i, half - 1), 0, 0)
    at_hi = lambda i, p: (0, most(i - half, 0), 0, 0)
    near_up = lambda j: (weights, (1, 1, 1, feat, rows), lambda i, p: (0, j, i, 0, 0))
    near_grads = call_once(
        near_grads_body,
        place,
        local,
        [
            near_up(0),
            near_up(1),
            (slope_lo_s, strip, at_lo),
            (slope_lo_n, strip, at_lo),
            (slope_hi_s, strip, at_hi),
            (slope_hi_n, strip, at_hi),
        ],
        [(blocks, BF16, one, every)],
        16,
    )[0]
    got_grads = send(near_grads, 1)

    x_b = after((x,), near_grads)[0]
    give_lo, give_hi, keep_u = up_terms(
        up_terms_body,
        [(x_b, one, every), (x_lo, one, low), (x_hi, one, high), (slope_sn, strip, at_i)]
        + [(slope_lo_s, strip, at_lo), (slope_lo_n, strip, at_lo)]
        + [(slope_hi_s, strip, at_hi), (slope_hi_n, strip, at_hi)],
        3,
        [lambda i: least(i, half - 1), lambda i: most(i - half, 0)],
        16.0,
    )
    send_u, far_u, mine_u = up_meet(3, keep_u, [send_core(give_lo), send_core(give_hi)])
    got_u, far_u = send_z(send_u, 1), send_z(far_u, 1)

    got_d = after((got_d,), send_u)[0]
    send_d, mine_d = call(
        down_again_body,
        place,
        (1,),
        [whole(mine_d), whole(got_d)],
        [whole_out(shard[2:], BF16), whole_out(shard[2:], F32)],
        16,
    )
    got_d = send_z(send_d, 2)

    got_u, far_u = after((got_u, far_u), send_d)
    send_u, mine_u = up_again(mine_u, got_u, far_u)
    got_u = send_z(send_u, 2)

    got_d = after((got_d,), send_u)[0]
    sum_d = call(
        functools.partial(down_sum_body, factor),
        place,
        (1,),
        [whole(mine_d), whole(got_d)],
        [whole_out(shard[2:], BF16)],
        8,
    )[0]
    swaps = []
    for device in range(n_dp * n_tensor):
        dp, t = device // n_tensor, device % n_tensor
        z_high, y = dp // 4, t // 2
        swaps.append((device, (y * 4 + dp % 4) * n_tensor + z_high * 2 + t % 2))
    home_d = lax.ppermute(sum_d, ("dp", "tensor"), swaps)

    got_out = after((got_out,), sum_d)[0]
    outputs = outputs_of(0, hid, [got_out])

    got_u = after((got_u,), outputs)[0]
    send_u, mine_u = call(
        functools.partial(up_sum_body, factor),
        place,
        (1,),
        [whole(v) for v in (mine_e, got_e, mine_u, got_u)],
        [whole_out((2,) + shard_u[1:], BF16), whole_out((2,) + shard_u[1:], F32)],
        8,
    )
    got_u = send(send_u, 1)

    got_grads = after((got_grads,), send_u)[0]
    feature_grads = call(
        by_grid(grads_body),
        place,
        (local,),
        [
            (up_blocks, (1, feat, rows), lambda i, p: (i, 0, p[0])),
            (up_blocks, (1, feat, rows), lambda i, p: (i, 0, p[0] ^ 2)),
            (slope_ss, strip, at_i),
            (slope_sn, strip, at_i),
            (got_grads, one, every),
        ],
        [(blocks, BF16, one, every)],
        16,
    )[0]

    got_u, home_d = after((got_u, home_d), feature_grads)
    up_grads, down_grads = call(
        place_body,
        place,
        (1,),
        [whole(mine_u), whole(got_u), whole(home_d)],
        [
            whole_out((local, feat // n_dp, block_hidden), F32),
            whole_out((local, part, feat), F32),
        ],
        8,
    )
    wide = (local * feat, tokens)
    return (outputs.reshape(wide), feature_grads.reshape(wide), up_grads, down_grads)


def solution(mesh):
    in_specs = (
        P("tensor", "dp"),
        P("tensor", "dp"),
        P("tensor", None, None),
        P("tensor", None, None),
    )
    out_specs = (
        P("tensor", "dp"),
        P("tensor", "dp"),
        P("tensor", "dp", None),
        P("tensor", "dp", None),
    )
    small = mesh.shape["tensor"] == 4 and mesh.shape["dp"] == 8
    return jax.shard_map(
        square_device if small else generic_device,
        mesh=mesh,
        in_specs=in_specs,
        out_specs=out_specs,
        check_vma=False,
    )
```

```python
import functools
import math

import jax
import jax.numpy as jnp
from jax import lax
from jax.experimental import pallas as pl
from jax.experimental.pallas import tpu as pltpu
from jax.sharding import PartitionSpec as P

BF16 = jnp.bfloat16
F32 = jnp.float32
INV_ROOT2 = 0.7071067811865476
INV_ROOT2PI = 0.3989422804014327
MIB = 1024 * 1024


def gelu_value(value):
    return 0.5 * value * (1.0 + lax.erf(value * INV_ROOT2))


def gelu_slope(value):
    return (
        0.5 * (1.0 + lax.erf(value * INV_ROOT2))
        + value * jnp.exp(-0.5 * value * value) * INV_ROOT2PI
    )


def generic_device(features, cotangent, up_blocks, down_blocks):
    local_blocks, block_feat, block_hidden = up_blocks.shape
    blocks = local_blocks * lax.axis_size("tensor")
    sub = block_hidden // blocks
    tokens_here = features.shape[1]
    factor = 1.0 / math.sqrt(tokens_here * lax.axis_size("dp"))
    x_local = features.reshape(local_blocks, block_feat, tokens_here)
    dy_local = cotangent.reshape(local_blocks, block_feat, tokens_here)
    down_four = down_blocks.reshape(local_blocks, blocks, sub, block_feat)
    preact = jnp.einsum("bdn,bdf->bfn", x_local, up_blocks, preferred_element_type=F32)
    pre_wide = preact.astype(BF16).astype(F32)
    hidden = gelu_value(pre_wide).astype(BF16).reshape(local_blocks, blocks, sub, tokens_here)
    mixed = lax.all_to_all(hidden, "tensor", split_axis=1, concat_axis=0, tiled=True)
    out_three = jnp.einsum("ijsn,jise->jen", mixed, down_four, preferred_element_type=F32)
    outputs = out_three.astype(BF16).reshape(local_blocks * block_feat, tokens_here)
    down_term = jnp.einsum("ijsn,jen->isje", mixed, dy_local, preferred_element_type=F32)
    down_term = down_term.reshape(block_hidden, local_blocks, block_feat)
    back = jnp.einsum("jen,jise->ijsn", dy_local, down_four, preferred_element_type=F32)
    back_home = lax.all_to_all(
        back.astype(BF16), "tensor", split_axis=0, concat_axis=1, tiled=True
    ).reshape(local_blocks, block_hidden, tokens_here)
    slope = (back_home.astype(F32) * gelu_slope(pre_wide)).astype(BF16)
    up_term = jnp.einsum("bdn,bfn->dbf", x_local, slope, preferred_element_type=F32)
    up_share = lax.psum_scatter(up_term, "dp", scatter_dimension=0, tiled=True)
    down_share = lax.psum_scatter(down_term, "dp", scatter_dimension=0, tiled=True)
    dx_three = jnp.einsum("bfn,bdf->bdn", slope, up_blocks, preferred_element_type=F32)
    feature_grads = dx_three.astype(BF16).reshape(local_blocks * block_feat, tokens_here)
    up_grads = jnp.transpose(up_share, (1, 0, 2)) * factor
    down_grads = jnp.transpose(down_share, (1, 0, 2)) * factor
    return (outputs, feature_grads, up_grads, down_grads)


def dot_tn(a, b):
    return lax.dot_general(a, b, (((0,), (0,)), ((), ())), preferred_element_type=F32)


def dot_nn(a, b):
    return lax.dot_general(a, b, (((1,), (0,)), ((), ())), preferred_element_type=F32)


def dot_nt(a, b):
    return lax.dot_general(a, b, (((1,), (1,)), ((), ())), preferred_element_type=F32)


def call(body, place, grid, ins, outs, mib, scratch=(), span=0.0):
    return pl.pallas_call(
        body,
        grid_spec=pltpu.PrefetchScalarGridSpec(
            num_scalar_prefetch=1,
            grid=grid,
            in_specs=[pl.BlockSpec(b, m) for _, b, m in ins],
            out_specs=[pl.BlockSpec(b, m) for _, _, b, m in outs],
            scratch_shapes=list(scratch),
        ),
        out_shape=[jax.ShapeDtypeStruct(s, d) for s, d, _, _ in outs],
        compiler_params=pltpu.CompilerParams(vmem_limit_bytes=mib * MIB),
        cost_estimate=pl.CostEstimate(
            flops=int(span * 1e9), bytes_accessed=0, transcendentals=0
        ),
    )(place, *[a for a, _, _ in ins])


def block_of(ref, block, where):
    at = []
    for size, extent, index in zip(block, ref.shape, where):
        if size == extent:
            at.append(slice(None))
        elif isinstance(index, int):
            at.append(slice(index * size, (index + 1) * size))
        else:
            at.append(pl.ds(pl.multiple_of(index * size, size), size))
    return ref.at[tuple(at)]


def call_once(body, place, steps, ins, outs, mib, scratch=(), span=0.0):
    def every_step(place, *refs):
        blocks = [(b, m) for _, b, m in ins] + [(b, m) for _, _, b, m in outs]
        held, rest = refs[: len(blocks)], refs[len(blocks) :]
        for step in range(steps):
            views = [block_of(ref, b, m(step, place)) for ref, (b, m) in zip(held, blocks)]
            body(step, steps, place, *views, *rest)

    return call(
        every_step,
        place,
        (1,),
        [whole(a) for a, _, _ in ins],
        [whole_out(s, d) for s, d, _, _ in outs],
        mib,
        scratch=scratch,
        span=span,
    )


def by_grid(body):
    return lambda place, *refs: body(pl.program_id(0), pl.num_programs(0), place, *refs)


def whole(array):
    rank = array.ndim
    return (array, array.shape, lambda *at: (0,) * rank)


def whole_out(shape, kind):
    rank = len(shape)
    return (shape, kind, shape, lambda *at: (0,) * rank)


def after(values, *earlier):
    return lax.optimization_barrier((tuple(values), earlier))[0]


def square(ref):
    block = ref[...]
    width = block.shape[-1]
    return block.reshape(block.size // width, width)


def hidden_body(place, x_ref, up_ref, hidden_ref, gate_ref):
    pre = dot_tn(square(up_ref), square(x_ref)).astype(BF16).astype(F32)
    half_cdf = 0.5 + 0.5 * lax.erf(pre * INV_ROOT2)
    gate = half_cdf + pre * jnp.exp(-0.5 * pre * pre) * INV_ROOT2PI
    hidden_ref[...] = (pre * half_cdf).astype(BF16).reshape(hidden_ref.shape)
    gate_ref[...] = gate.astype(BF16).reshape(gate_ref.shape)


def weights_body(place, *refs):
    low, core, out_ref = place[1] % 2, place[2], refs[-1]
    for at in range(2):
        out_ref[:, :, :, core * 2 + (low ^ at)] = refs[at][...]
        out_ref[:, :, :, (1 - core) * 2 + (low ^ at)] = refs[2 + at][...]


def halves(step, steps, work, lo, hi):
    if isinstance(step, int):
        work(*(lo if step < steps // 2 else hi))
        return
    pl.when(step < steps // 2)(functools.partial(work, *lo))
    pl.when(step >= steps // 2)(functools.partial(work, *hi))


def stacked(refs, axis=0):
    return jnp.concatenate([square(ref) for ref in refs], axis)


def put_slopes(cot, downs, gates, slopes):
    back = dot_nn(stacked(downs), cot).astype(BF16)
    base = 0
    for gate_ref, slope_ref in zip(gates, slopes):
        gate = square(gate_ref).astype(F32)
        mine = back[base : base + gate.shape[0]].astype(F32)
        slope_ref[...] = (mine * gate).astype(BF16).reshape(slope_ref.shape)
        base += gate.shape[0]


def slope_body(step, steps, place, cot_ref, down_ref, gate_ref, slope_ref):
    put_slopes(square(cot_ref), [down_ref], [gate_ref], [slope_ref])


def late_slopes_body(step, steps, place, own_ref, near_lo, near_hi, *refs):
    downs, gates, slopes = refs[:4], refs[4:8], refs[8:]
    put_slopes(square(own_ref), downs[3:], gates[3:], slopes[3:])

    def work(near_ref):
        put_slopes(square(near_ref), downs[:3], gates[:3], slopes[:3])

    halves(step, steps, work, (near_lo,), (near_hi,))


def own_terms_body(step, steps, place, cot_ref, hid_ref, x_ref, slope_ref, give_ref, keep_ref, down_s, up_s):
    core = place[2]
    up_s[...] = dot_nt(square(x_ref), square(slope_ref)).astype(BF16).reshape(up_s.shape)
    count = up_s.shape[2]
    strip = slice(step * count, (step + 1) * count)
    give_ref[0, :, strip] = up_s[:, 1 - core]
    keep_ref[0, :, strip] = up_s[:, core]
    down_s[...] = dot_nt(square(hid_ref), square(cot_ref)).astype(BF16).reshape(down_s.shape)
    give_ref[1, step] = down_s[1 - core]
    keep_ref[1, step] = down_s[core]


def down_terms_body(step, steps, place, own_ref, near_lo, near_hi, sn, ns_lo, ns_hi, nn_lo, nn_hi, give_own, give_near, keep_ref, term_s):
    core = place[2]

    def put(pair, terms, give):
        term_s[pair] = terms.astype(BF16).reshape(term_s.shape[1:])
        give[...] = term_s[pair, 1 - core].reshape(give.shape)
        keep_ref[pair, 0] = term_s[pair, core]

    def work(near_ref):
        rows = 2 * term_s.shape[2]
        mixed = dot_nt(stacked((sn, nn_lo, nn_hi)), square(near_ref))
        put(0, mixed[:rows], give_own)
        put(1, dot_nt(stacked((ns_lo, ns_hi)), square(own_ref)), give_near.at[0])
        put(2, mixed[rows:], give_near.at[1])

    halves(step, steps, work, (near_lo,), (near_hi,))


def put_up_term(pair, core, x, slope_ref, give_ref, keep_ref, term_s):
    term_s[...] = dot_nt(x, square(slope_ref)).astype(BF16).reshape(term_s.shape)
    give_ref[pair] = term_s[:, 1 - core]
    keep_ref[pair] = term_s[:, core]


def up_terms_body(step, steps, place, x_ref, x_lo, x_hi, sn, lo_s, lo_n, hi_s, hi_n, give_lo, give_hi, keep_ref, term_s):
    def work(x_near, from_own, from_near, give_ref):
        near = square(x_near)
        for pair, (x, ref) in enumerate(((square(x_ref), sn), (near, from_own), (near, from_near))):
            put_up_term(pair, place[2], x, ref, give_ref, keep_ref, term_s)

    lo, hi = (x_lo, lo_s, lo_n, give_lo), (x_hi, hi_s, hi_n, give_hi)
    halves(step, steps, work, lo, hi)


def outputs_body(step, steps, place, d_own, d_lo, d_hi, hid_ref, lo_ref, hi_ref, out_ref):
    total = dot_tn(stacked((d_own, d_lo, d_hi)), stacked((hid_ref, lo_ref, hi_ref)))
    out_ref[0] = total.astype(out_ref.dtype)


def near_grads_body(step, steps, place, up_own, up_near, lo_s, lo_n, hi_s, hi_n, out_ref):
    def work(*slopes):
        out_ref[0] = dot_nn(stacked((up_own, up_near), 1), stacked(slopes)).astype(BF16)

    halves(step, steps, work, (lo_s, lo_n), (hi_s, hi_n))


def grads_body(step, steps, place, up_own, up_near, slope_own, slope_near, out_ref):
    out_ref[0] = dot_nn(stacked((up_own, up_near), 1), stacked((slope_own, slope_near)))


def add_body(place, own_ref, got_ref, out_ref):
    out_ref[...] = (own_ref[...] + got_ref[...].astype(F32)).astype(BF16)


def down_meet_body(place, first, first_got, keep_ref, got_own, got_near, send_ref, mine_ref, total_s):
    stay = (place[0] ^ place[1]) & 1
    total_s[0, 0] = first[1].astype(F32) + first_got[1].astype(F32)
    total_s[0, 1] = keep_ref[0].astype(F32) + got_own[...].astype(F32)
    total_s[1] = keep_ref[1:].astype(F32) + got_near[...].astype(F32)
    mine_ref[...] = total_s[:, stay]
    send_ref[...] = total_s[:, 1 - stay].astype(BF16)


def down_again_body(place, mine_ref, got_ref, send_ref, own_ref):
    stay = (place[0] // 2) ^ (place[1] // 2)
    own_ref[...] = mine_ref[stay] + got_ref[stay].astype(F32)
    send_ref[...] = (mine_ref[1 - stay] + got_ref[1 - stay].astype(F32)).astype(BF16)


def down_sum_body(factor, place, own_ref, got_ref, out_ref):
    out_ref[...] = ((own_ref[...] + got_ref[...].astype(F32)) * factor).astype(BF16)


def up_meet_body(parts, place, keep_ref, *refs):
    gots, sends, mine_ref = refs[:parts], refs[parts:-1], refs[-1]
    rows = gots[0].shape[2]
    for hop in range(4):
        there = place[1] ^ hop
        for at, got_ref in enumerate(gots):
            strip = slice(at * rows, (at + 1) * rows)
            total = keep_ref[:, there, strip].astype(F32) + got_ref[:, there].astype(F32)
            if hop % 2:
                sends[hop // 2][:, strip] = total.astype(BF16)
            else:
                mine_ref[hop // 2, :, strip] = total


def up_again_body(place, mine_ref, far_ref, send_ref):
    send_ref[...] = (mine_ref[1] + far_ref[...].astype(F32)).astype(BF16)


def up_sum_body(factor, place, *refs):
    ins, (send_ref, mine_ref) = refs[:6], refs[6:]
    first, total = (
        (own[0] + near[...].astype(F32) + far[...].astype(F32)) * factor
        for own, near, far in (ins[:3], ins[3:])
    )
    mine_ref[0] = first[0]
    mine_ref[1] = total[0]
    send_ref[...] = total[1:].astype(BF16)


def place_body(place, mine_ref, got_ref, down_in, up_ref, down_ref):
    down_ref[...] = down_in[...].astype(F32)
    width = mine_ref.shape[-1]
    for ref, side in ((mine_ref, 0), (got_ref, 1)):
        for at in range(2):
            where = place[0] ^ (2 * side) ^ at
            lanes = pl.ds(pl.multiple_of(where * width, width), width)
            up_ref[:, :, lanes] = ref[at].astype(F32).reshape(*up_ref.shape[:2], width)


def square_device(features, cotangent, up_blocks, down_blocks):
    local, feat, block_hidden = up_blocks.shape
    tokens = features.shape[1]
    n_dp, n_tensor = lax.axis_size("dp"), lax.axis_size("tensor")
    sub = block_hidden // (local * n_tensor)
    rows = local * sub
    half, part = local // 2, rows // 2
    factor = 1.0 / math.sqrt(tokens * n_dp)
    me = lax.axis_index("tensor").astype(jnp.int32)
    rank = lax.axis_index("dp").astype(jnp.int32)
    z, core = rank >> 1, rank & 1
    place = jnp.stack([me, z, core])
    x = features.reshape(local, feat, tokens)
    cot = cotangent.reshape(local, feat, tokens)
    one = (1, feat, tokens)
    blocks = (local, feat, tokens)
    every = lambda i, p: (i, 0, 0)
    least = lambda a, b: min(a, b) if isinstance(a, int) else jnp.minimum(a, b)
    most = lambda a, b: max(a, b) if isinstance(a, int) else jnp.maximum(a, b)
    low = lambda i, p: (least(i, half - 1), 0, 0)
    high = lambda i, p: (most(i - half, 0), 0, 0)

    def send(value, hop):
        return lax.ppermute(value, "tensor", [(t, t ^ hop) for t in range(n_tensor)])

    def send_z(value, hop):
        return lax.ppermute(value, "dp", [(d, d ^ (2 * hop)) for d in range(n_dp)])

    def send_core(value):
        return lax.ppermute(value, "dp", [(d, d ^ 1) for d in range(n_dp)])

    quarter = rows // 4
    at = (core * 2 + (z & 1)) * quarter
    to_i = jnp.stack(
        [
            lax.dynamic_slice(up_blocks, (0, at, (me ^ k) * rows), (local, quarter, rows))
            for k in (2, 3)
        ]
    )
    to_j = jnp.stack(
        [
            lax.dynamic_slice(down_blocks, (0, (me ^ k) * rows + at, 0), (local, quarter, feat))
            for k in (1, 3)
        ]
    )
    from_i, from_j = send(to_i, 2), send(to_j, 1)
    firsts = after((x[:half], x[half:], cot[:half], cot[half:]), to_i, to_j)
    x_lo, cot_lo = send(firsts[0], 2), send(firsts[2], 1)
    x_hi, cot_hi = send(firsts[1], 2), send(firsts[3], 1)

    def hidden_of(source, count, up, span):
        unit = (2, local, count, sub, tokens)
        block = (1, local, 1, sub, tokens)
        where = lambda j, i, p: (j, 0, i, 0, 0)
        return call(
            hidden_body,
            place,
            (2, count),
            [(source, one, lambda j, i, p: (i, 0, 0)), up],
            [(unit, BF16, block, where), (unit, BF16, block, where)],
            16,
        )

    hid, gate = hidden_of(
        x, local, (up_blocks, (1, feat, rows), lambda j, i, p: (i, 0, p[0] ^ j)), 0.0
    )
    from_i, from_j = after((from_i, from_j), hid)
    share = jnp.stack([from_i, from_j])
    share_z = send_z(share, 1)

    def unit_of(array, j):
        return (array, (1, 1) + array.shape[2:], lambda i, p: (j, i, 0, 0, 0))

    def down_of(j, which):
        if j == 0:
            if which == 0:
                return (down_blocks, (1, rows, feat), lambda i, p: (i, p[0], 0))
            return (
                down_blocks,
                (1, part, feat),
                lambda i, p: (i, 2 * (p[0] ^ 2) + which - 1, 0),
            )
        if which == 0:
            return (weights, (1, 1, 1, rows, feat), lambda i, p: (1, 0, i, 0, 0))
        return (weights, (1, 1, 1, part, feat), lambda i, p: (1, 1, i, which - 1, 0))

    def own_slope(which, array):
        return call_once(
            slope_body,
            place,
            local,
            [(cot, one, every), down_of(0, which), unit_of(array, 0)],
            [(array.shape[1:], BF16, (1,) + array.shape[2:], lambda i, p: (i, 0, 0, 0))],
            20,
        )[0]

    slope_ss = own_slope(0, gate)
    at_i = lambda i, p: (0, i, 0, 0)
    strip = (local, 1, sub, tokens)
    shard_u = (n_dp // 2, local * feat // n_dp, rows)

    def up_terms(body, ins, count, gives, span):
        block = (count, n_dp // 2, feat // n_dp, rows)
        wide = (count,) + shard_u
        part_u = (count, n_dp // 2, shard_u[1] // len(gives), rows)
        return call_once(
            body,
            place,
            local,
            ins,
            [
                (part_u, BF16, block, functools.partial(lambda m, i, p: (0, 0, m(i), 0), m))
                for m in gives
            ]
            + [(wide, BF16, block, lambda i, p: (0, 0, i, 0))],
            20,
            scratch=[pltpu.VMEM((n_dp // 2, 2, feat // n_dp, rows), BF16)],
            span=span,
        )

    def up_meet(count, keep, gots):
        piece = (count,) + shard_u[1:]
        return call(
            functools.partial(up_meet_body, len(gots)),
            place,
            (1,),
            [(v, (count,) + v.shape[1:], lambda i, p: (0, 0, 0, 0)) for v in (keep, *gots)],
            [whole_out(piece, BF16)] * 2 + [whole_out((2,) + piece, F32)],
            16,
        )

    def up_again(mine, far):
        piece = mine.shape[1:]
        return call(
            up_again_body, place, (1,), [whole(mine), whole(far)], [whole_out(piece, BF16)], 16
        )[0]

    give_e, keep_e = call_once(
        own_terms_body,
        place,
        local,
        [
            (cot, one, every),
            unit_of(hid, 0),
            (x, one, every),
            (slope_ss, strip, at_i),
        ],
        [whole_out((2,) + shard_u, BF16)] * 2,
        20,
        scratch=[
            pltpu.VMEM((2, part, feat), BF16),
            pltpu.VMEM((n_dp // 2, 2, feat // n_dp, rows), BF16),
        ],
    )
    share, share_z, x_lo, cot_lo = after((share, share_z, x_lo, cot_lo), give_e)
    core_parts = after((share, share_z), x_lo, cot_lo)
    weights = call(
        weights_body,
        place,
        (1,),
        [whole(v) for v in (share, share_z, *map(send_core, core_parts))],
        [whole_out((2, 2, local, 4, quarter, feat), BF16)],
        16,
    )[0].reshape(2, 2, local, rows, feat)

    def near_hidden(source, which):
        up = (
            weights,
            (1, 1, 1, feat, rows),
            lambda j, i, p: (0, j, which * half + i, 0, 0),
        )
        return hidden_of(source, half, up, 0.0)

    give_e = after((give_e,), x_lo, cot_lo)[0]
    first_got = send_core(give_e)
    send_e, far_e, mine_e = up_meet(1, keep_e, [first_got])
    got_e, far_e = send_z(send_e, 1), send_z(far_e, 1)
    x_lo = after((x_lo,), weights, send_e)[0]
    hid_lo, gate_lo = near_hidden(x_lo, 0)
    slope_lo_s = own_slope(1, gate_lo)

    got_e, far_e = after((got_e, far_e), slope_lo_s)
    last_e = send_z(up_again(mine_e, far_e), 2)

    x_hi, cot_hi = after((x_hi, cot_hi), last_e)
    hid_hi, gate_hi = near_hidden(x_hi, 1)

    def outputs_of(j, hid, kind):
        return call_once(
            outputs_body,
            place,
            local,
            [down_of(j, which) for which in range(3)]
            + [unit_of(array, j) for array in (hid, hid_lo, hid_hi)],
            [(blocks, kind, one, every)],
            16,
        )[0]

    def added(own, got):
        pairs_at = lambda i, p: (i, 0, 0)
        two = (2, feat, tokens)
        return call(
            add_body,
            place,
            (local // 2,),
            [(own, two, pairs_at), (got, two, pairs_at)],
            [(blocks, BF16, two, pairs_at)],
            20,
        )[0]

    shard = (2, 2, local, part, feat)
    strip_d = (1, part, feat)
    give_own, give_near, keep_d = call_once(
        down_terms_body,
        place,
        local,
        [(cot, one, every), (cot_lo, one, low), (cot_hi, one, high)]
        + [unit_of(hid, 1)]
        + [unit_of(array, j) for j in (0, 1) for array in (hid_lo, hid_hi)],
        [
            (shard[2:], BF16, strip_d, every),
            (shard[1:], BF16, (2,) + strip_d, lambda i, p: (0, i, 0, 0)),
            ((3,) + shard[2:], BF16, (3,) + strip_d, lambda i, p: (0, i, 0, 0)),
        ],
        16,
        scratch=[pltpu.VMEM((3, 2, part, feat), BF16)],
    )
    core_own, core_near = send_core(give_own), send_core(give_near)
    hid_b = after((hid,), give_own)[0]
    near_out = outputs_of(1, hid_b, BF16)
    got_out = send(near_out, 1)
    core_own, core_near = after((core_own, core_near), near_out)
    parts_d = (keep_e, first_got, keep_d, core_own, core_near)
    send_d, mine_d = call(
        down_meet_body,
        place,
        (1,),
        [whole(v) for v in parts_d],
        [whole_out(shard[1:], BF16), whole_out(shard[1:], F32)],
        16,
        scratch=[pltpu.VMEM(shard, F32)],
    )
    got_d = send_z(send_d, 1)
    cot_b, *near_b = after((cot, cot_lo, cot_hi), send_d)
    late = [(1, 0, gate), (1, 1, gate_lo), (1, 2, gate_hi), (0, 2, gate_hi)]
    slope_sn, slope_lo_n, slope_hi_n, slope_hi_s = call_once(
        late_slopes_body,
        place,
        local,
        [(cot_b, one, every), (near_b[0], one, low), (near_b[1], one, high)]
        + [down_of(j, which) for j, which, _ in late]
        + [unit_of(array, j) for j, _, array in late],
        [
            (array.shape[1:], BF16, (1,) + array.shape[2:], lambda i, p: (i, 0, 0, 0))
            for _, _, array in late
        ],
        20,
    )

    at_lo = lambda i, p: (0, least(i, half - 1), 0, 0)
    at_hi = lambda i, p: (0, most(i - half, 0), 0, 0)
    near_up = lambda j: (weights, (1, 1, 1, feat, rows), lambda i, p: (0, j, i, 0, 0))
    near_grads = call_once(
        near_grads_body,
        place,
        local,
        [
            near_up(0),
            near_up(1),
            (slope_lo_s, strip, at_lo),
            (slope_lo_n, strip, at_lo),
            (slope_hi_s, strip, at_hi),
            (slope_hi_n, strip, at_hi),
        ],
        [(blocks, BF16, one, every)],
        16,
    )[0]
    got_grads = send(near_grads, 2)

    x_b = after((x,), near_grads)[0]
    give_lo, give_hi, keep_u = up_terms(
        up_terms_body,
        [(x_b, one, every), (x_lo, one, low), (x_hi, one, high), (slope_sn, strip, at_i)]
        + [(slope_lo_s, strip, at_lo), (slope_lo_n, strip, at_lo)]
        + [(slope_hi_s, strip, at_hi), (slope_hi_n, strip, at_hi)],
        3,
        [lambda i: least(i, half - 1), lambda i: most(i - half, 0)],
        16.0,
    )
    send_u, far_u, mine_u = up_meet(3, keep_u, [send_core(give_lo), send_core(give_hi)])
    got_u, far_u = send_z(send_u, 1), send_z(far_u, 1)

    got_d = after((got_d,), send_u)[0]
    send_d, mine_d = call(
        down_again_body,
        place,
        (1,),
        [whole(mine_d), whole(got_d)],
        [whole_out(shard[2:], BF16), whole_out(shard[2:], F32)],
        16,
    )
    got_d = send_z(send_d, 2)

    up_b = after((up_blocks,), send_d)[0]
    own_grads = call_once(
        grads_body,
        place,
        local,
        [
            (up_b, (1, feat, rows), lambda i, p: (i, 0, p[0])),
            (up_b, (1, feat, rows), lambda i, p: (i, 0, p[0] ^ 1)),
            (slope_ss, strip, at_i),
            (slope_sn, strip, at_i),
        ],
        [(blocks, F32, one, every)],
        16,
    )[0]

    own_out = outputs_of(0, after((hid,), own_grads)[0], F32)
    far_u = after((far_u,), own_out)[0]
    send_u = up_again(mine_u, far_u)
    last_u = send_z(send_u, 2)

    got_d = after((got_d,), send_u)[0]
    sum_d = call(
        functools.partial(down_sum_body, factor),
        place,
        (1,),
        [whole(mine_d), whole(got_d)],
        [whole_out(shard[2:], BF16)],
        8,
    )[0]
    swaps = []
    for device in range(n_dp * n_tensor):
        dp, t = device // n_tensor, device % n_tensor
        z_low, x_at = dp // 2 % 2, t % 2
        home = (dp // 4 * 4 + x_at * 2 + dp % 2) * n_tensor + t // 2 * 2 + z_low
        swaps.append((device, home))
    home_d = lax.ppermute(sum_d, ("dp", "tensor"), swaps)

    got_out = after((got_out,), sum_d)[0]
    outputs = added(own_out, got_out)

    got_u, last_u = after((got_u, last_u), outputs)
    send_u, mine_u = call(
        functools.partial(up_sum_body, factor),
        place,
        (1,),
        [whole(v) for v in (mine_e, got_e, last_e, mine_u, got_u, last_u)],
        [whole_out((2,) + shard_u[1:], BF16), whole_out((2,) + shard_u[1:], F32)],
        8,
    )
    got_u = send(send_u, 2)

    got_grads = after((got_grads,), send_u)[0]
    feature_grads = added(own_grads, got_grads)

    got_u, home_d = after((got_u, home_d), feature_grads)
    up_grads, down_grads = call(
        place_body,
        place,
        (1,),
        [whole(mine_u), whole(got_u), whole(home_d)],
        [
            whole_out((local, feat // n_dp, block_hidden), F32),
            whole_out((local, part, feat), F32),
        ],
        8,
    )
    wide = (local * feat, tokens)
    return (outputs.reshape(wide), feature_grads.reshape(wide), up_grads, down_grads)


def solution(mesh):
    in_specs = (
        P("tensor", "dp"),
        P("tensor", "dp"),
        P("tensor", None, None),
        P("tensor", None, None),
    )
    out_specs = (
        P("tensor", "dp"),
        P("tensor", "dp"),
        P("tensor", "dp", None),
        P("tensor", "dp", None),
    )
    small = mesh.shape["tensor"] == 4 and mesh.shape["dp"] == 8
    return jax.shard_map(
        square_device if small else generic_device,
        mesh=mesh,
        in_specs=in_specs,
        out_specs=out_specs,
        check_vma=False,
    )
```

```python
import functools
import math

import jax
import jax.numpy as jnp
from jax import lax
from jax.experimental import pallas as pl
from jax.experimental.pallas import tpu as pltpu
from jax.sharding import PartitionSpec as P

BF16 = jnp.bfloat16
F32 = jnp.float32
INV_ROOT2 = 0.7071067811865476
INV_ROOT2PI = 0.3989422804014327
MIB = 1024 * 1024


def gelu_value(value):
    return 0.5 * value * (1.0 + lax.erf(value * INV_ROOT2))


def gelu_slope(value):
    return (
        0.5 * (1.0 + lax.erf(value * INV_ROOT2))
        + value * jnp.exp(-0.5 * value * value) * INV_ROOT2PI
    )


def generic_device(features, cotangent, up_blocks, down_blocks):
    local_blocks, block_feat, block_hidden = up_blocks.shape
    blocks = local_blocks * lax.axis_size("tensor")
    sub = block_hidden // blocks
    tokens_here = features.shape[1]
    factor = 1.0 / math.sqrt(tokens_here * lax.axis_size("dp"))
    x_local = features.reshape(local_blocks, block_feat, tokens_here)
    dy_local = cotangent.reshape(local_blocks, block_feat, tokens_here)
    down_four = down_blocks.reshape(local_blocks, blocks, sub, block_feat)
    preact = jnp.einsum("bdn,bdf->bfn", x_local, up_blocks, preferred_element_type=F32)
    pre_wide = preact.astype(BF16).astype(F32)
    hidden = gelu_value(pre_wide).astype(BF16).reshape(local_blocks, blocks, sub, tokens_here)
    mixed = lax.all_to_all(hidden, "tensor", split_axis=1, concat_axis=0, tiled=True)
    out_three = jnp.einsum("ijsn,jise->jen", mixed, down_four, preferred_element_type=F32)
    outputs = out_three.astype(BF16).reshape(local_blocks * block_feat, tokens_here)
    down_term = jnp.einsum("ijsn,jen->isje", mixed, dy_local, preferred_element_type=F32)
    down_term = down_term.reshape(block_hidden, local_blocks, block_feat)
    back = jnp.einsum("jen,jise->ijsn", dy_local, down_four, preferred_element_type=F32)
    back_home = lax.all_to_all(
        back.astype(BF16), "tensor", split_axis=0, concat_axis=1, tiled=True
    ).reshape(local_blocks, block_hidden, tokens_here)
    slope = (back_home.astype(F32) * gelu_slope(pre_wide)).astype(BF16)
    up_term = jnp.einsum("bdn,bfn->dbf", x_local, slope, preferred_element_type=F32)
    up_share = lax.psum_scatter(up_term, "dp", scatter_dimension=0, tiled=True)
    down_share = lax.psum_scatter(down_term, "dp", scatter_dimension=0, tiled=True)
    dx_three = jnp.einsum("bfn,bdf->bdn", slope, up_blocks, preferred_element_type=F32)
    feature_grads = dx_three.astype(BF16).reshape(local_blocks * block_feat, tokens_here)
    up_grads = jnp.transpose(up_share, (1, 0, 2)) * factor
    down_grads = jnp.transpose(down_share, (1, 0, 2)) * factor
    return (outputs, feature_grads, up_grads, down_grads)


def dot_tn(a, b):
    return lax.dot_general(a, b, (((0,), (0,)), ((), ())), preferred_element_type=F32)


def dot_nn(a, b):
    return lax.dot_general(a, b, (((1,), (0,)), ((), ())), preferred_element_type=F32)


def dot_nt(a, b):
    return lax.dot_general(a, b, (((1,), (1,)), ((), ())), preferred_element_type=F32)


def call(body, place, grid, ins, outs, mib, scratch=(), span=0.0, alias=None):
    return pl.pallas_call(
        body,
        grid_spec=pltpu.PrefetchScalarGridSpec(
            num_scalar_prefetch=1,
            grid=grid,
            in_specs=[
                pl.BlockSpec(b, m) if b else pl.BlockSpec(memory_space=pl.ANY) for _, b, m in ins
            ],
            out_specs=[pl.BlockSpec(b, m) for _, _, b, m in outs],
            scratch_shapes=list(scratch),
        ),
        out_shape=[jax.ShapeDtypeStruct(s, d) for s, d, _, _ in outs],
        input_output_aliases=alias or {},
        compiler_params=pltpu.CompilerParams(vmem_limit_bytes=mib * MIB),
        cost_estimate=pl.CostEstimate(
            flops=int(span * 1e9), bytes_accessed=0, transcendentals=0
        ),
    )(place, *[a for a, _, _ in ins])


def block_of(ref, block, where):
    at = []
    for size, extent, index in zip(block, ref.shape, where):
        if size == extent:
            at.append(slice(None))
        elif isinstance(index, int):
            at.append(slice(index * size, (index + 1) * size))
        else:
            at.append(pl.ds(pl.multiple_of(index * size, size), size))
    return ref.at[tuple(at)]


def call_once(body, place, steps, ins, outs, mib, scratch=(), span=0.0):
    def every_step(place, *refs):
        blocks = [(b, m) for _, b, m in ins] + [(b, m) for _, _, b, m in outs]
        held, rest = refs[: len(blocks)], refs[len(blocks) :]
        for step in range(steps):
            views = [block_of(ref, b, m(step, place)) for ref, (b, m) in zip(held, blocks)]
            body(step, steps, place, *views, *rest)

    return call(
        every_step,
        place,
        (1,),
        [whole(a) for a, _, _ in ins],
        [whole_out(s, d) for s, d, _, _ in outs],
        mib,
        scratch=scratch,
        span=span,
    )


def by_grid(body):
    return lambda place, *refs: body(pl.program_id(0), pl.num_programs(0), place, *refs)


def whole(array):
    rank = array.ndim
    return (array, array.shape, lambda *at: (0,) * rank)


def whole_out(shape, kind):
    rank = len(shape)
    return (shape, kind, shape, lambda *at: (0,) * rank)


def after(values, *earlier):
    return lax.optimization_barrier((tuple(values), earlier))[0]


def square(ref):
    block = ref[...]
    width = block.shape[-1]
    return block.reshape(block.size // width, width)


def hidden_body(place, x_ref, up_ref, hidden_ref, gate_ref):
    pre = dot_tn(square(up_ref), square(x_ref)).astype(BF16).astype(F32)
    half_cdf = 0.5 + 0.5 * lax.erf(pre * INV_ROOT2)
    gate = half_cdf + pre * jnp.exp(-0.5 * pre * pre) * INV_ROOT2PI
    hidden_ref[...] = (pre * half_cdf).astype(BF16).reshape(hidden_ref.shape)
    gate_ref[...] = gate.astype(BF16).reshape(gate_ref.shape)


def weights_body(place, *refs):
    low, core, out_ref = place[1] % 2, place[2], refs[-1]
    for at in range(2):
        out_ref[:, :, :, core * 2 + (low ^ at)] = refs[at][...]
        out_ref[:, :, :, (1 - core) * 2 + (low ^ at)] = refs[2 + at][...]


def halves(step, steps, work, lo, hi):
    if isinstance(step, int):
        work(*(lo if step < steps // 2 else hi))
        return
    pl.when(step < steps // 2)(functools.partial(work, *lo))
    pl.when(step >= steps // 2)(functools.partial(work, *hi))


def stacked(refs, axis=0):
    return jnp.concatenate([square(ref) for ref in refs], axis)


def put_slopes(cot, downs, gates, slopes):
    back = dot_nn(stacked(downs), cot).astype(BF16)
    base = 0
    for gate_ref, slope_ref in zip(gates, slopes):
        gate = square(gate_ref).astype(F32)
        mine = back[base : base + gate.shape[0]].astype(F32)
        slope_ref[...] = (mine * gate).astype(BF16).reshape(slope_ref.shape)
        base += gate.shape[0]


def slope_body(step, steps, place, cot_ref, down_ref, gate_ref, slope_ref):
    put_slopes(square(cot_ref), [down_ref], [gate_ref], [slope_ref])


def late_slopes_body(step, steps, place, own_ref, near_lo, near_hi, *refs):
    downs, gates, slopes = refs[:4], refs[4:8], refs[8:]
    put_slopes(square(own_ref), downs[3:], gates[3:], slopes[3:])

    def work(near_ref):
        put_slopes(square(near_ref), downs[:3], gates[:3], slopes[:3])

    halves(step, steps, work, (near_lo,), (near_hi,))


def own_terms_body(step, steps, place, cot_ref, hid_ref, x_ref, slope_ref, give_ref, keep_ref, down_s, up_s):
    core = place[2]
    up_s[...] = dot_nt(square(x_ref), square(slope_ref)).astype(BF16).reshape(up_s.shape)
    count = up_s.shape[2]
    strip = slice(step * count, (step + 1) * count)
    give_ref[0, :, strip] = up_s[:, 1 - core]
    keep_ref[0, :, strip] = up_s[:, core]
    down_s[...] = dot_nt(square(hid_ref), square(cot_ref)).astype(BF16).reshape(down_s.shape)
    give_ref[1, step] = down_s[1 - core]
    keep_ref[1, step] = down_s[core]


def down_terms_body(step, steps, place, own_ref, near_lo, near_hi, sn, ns_lo, ns_hi, nn_lo, nn_hi, give_own, give_near, keep_ref, term_s):
    core = place[2]

    def put(pair, terms, give):
        term_s[pair] = terms.astype(BF16).reshape(term_s.shape[1:])
        give[...] = term_s[pair, 1 - core].reshape(give.shape)
        keep_ref[pair, 0] = term_s[pair, core]

    def work(near_ref):
        rows = 2 * term_s.shape[2]
        mixed = dot_nt(stacked((sn, nn_lo, nn_hi)), square(near_ref))
        put(0, mixed[:rows], give_own)
        put(1, dot_nt(stacked((ns_lo, ns_hi)), square(own_ref)), give_near.at[0])
        put(2, mixed[rows:], give_near.at[1])

    halves(step, steps, work, (near_lo,), (near_hi,))


def put_up_term(pair, core, x, slope_ref, give_ref, keep_ref, term_s):
    term_s[...] = dot_nt(x, square(slope_ref)).astype(BF16).reshape(term_s.shape)
    give_ref[pair] = term_s[:, 1 - core]
    keep_ref[pair] = term_s[:, core]


def up_terms_body(step, steps, place, x_ref, x_lo, x_hi, sn, lo_s, lo_n, hi_s, hi_n, give_lo, give_hi, keep_ref, term_s):
    def work(x_near, from_own, from_near, give_ref):
        near = square(x_near)
        for pair, (x, ref) in enumerate(((square(x_ref), sn), (near, from_own), (near, from_near))):
            put_up_term(pair, place[2], x, ref, give_ref, keep_ref, term_s)

    lo, hi = (x_lo, lo_s, lo_n, give_lo), (x_hi, hi_s, hi_n, give_hi)
    halves(step, steps, work, lo, hi)


def outputs_body(step, steps, place, d_own, d_lo, d_hi, hid_ref, lo_ref, hi_ref, out_ref):
    total = dot_tn(stacked((d_own, d_lo, d_hi)), stacked((hid_ref, lo_ref, hi_ref)))
    out_ref[0] = total.astype(out_ref.dtype)


def near_grads_body(step, steps, place, up_own, up_near, lo_s, lo_n, hi_s, hi_n, out_ref):
    def work(*slopes):
        out_ref[0] = dot_nn(stacked((up_own, up_near), 1), stacked(slopes)).astype(BF16)

    halves(step, steps, work, (lo_s, lo_n), (hi_s, hi_n))


def grads_body(step, steps, place, up_own, up_near, slope_own, slope_near, out_ref):
    out_ref[0] = dot_nn(stacked((up_own, up_near), 1), stacked((slope_own, slope_near)))


def add_body(place, own_ref, got_ref, out_ref):
    out_ref[...] = (own_ref[...] + got_ref[...].astype(F32)).astype(BF16)


def down_meet_body(place, first, first_got, keep_ref, got_own, got_near, send_ref, mine_ref, total_s):
    stay = (place[0] ^ place[1]) & 1
    total_s[0, 0] = first[1].astype(F32) + first_got[1].astype(F32)
    total_s[0, 1] = keep_ref[0].astype(F32) + got_own[...].astype(F32)
    total_s[1] = keep_ref[1:].astype(F32) + got_near[...].astype(F32)
    mine_ref[...] = total_s[:, stay]
    send_ref[...] = total_s[:, 1 - stay].astype(BF16)


def down_again_body(place, mine_ref, got_ref, send_ref, own_ref):
    stay = (place[0] // 2) ^ (place[1] // 2)
    own_ref[...] = mine_ref[stay] + got_ref[stay].astype(F32)
    send_ref[...] = (mine_ref[1 - stay] + got_ref[1 - stay].astype(F32)).astype(BF16)


def down_sum_body(factor, place, own_ref, got_ref, out_ref):
    out_ref[...] = ((own_ref[...] + got_ref[...].astype(F32)) * factor).astype(BF16)


def up_meet_body(parts, place, keep_ref, *refs):
    gots, sends, mine_ref = refs[:parts], refs[parts:-1], refs[-1]
    rows = gots[0].shape[2]
    for hop in range(4):
        there = place[1] ^ hop
        for at, got_ref in enumerate(gots):
            strip = slice(at * rows, (at + 1) * rows)
            total = keep_ref[:, there, strip].astype(F32) + got_ref[:, there].astype(F32)
            if hop % 2:
                sends[hop // 2][:, strip] = total.astype(BF16)
            else:
                mine_ref[hop // 2, :, strip] = total


def up_again_body(place, mine_ref, far_ref, send_ref):
    send_ref[...] = (mine_ref[1] + far_ref[...].astype(F32)).astype(BF16)


def up_sum_body(factor, place, *refs):
    ins, (send_ref, mine_ref) = refs[:6], refs[6:]
    first, total = (
        (own[0] + near[...].astype(F32) + far[...].astype(F32)) * factor
        for own, near, far in (ins[:3], ins[3:])
    )
    mine_ref[0] = first[0]
    mine_ref[1] = total[0]
    send_ref[...] = total[1:].astype(BF16)


def place_own_body(place, mine_ref, down_in, up_ref, down_ref):
    down_ref[...] = down_in[...].astype(F32)
    width = mine_ref.shape[-1]
    for at in range(2):
        lanes = pl.ds(pl.multiple_of((place[0] ^ at) * width, width), width)
        up_ref[:, :, lanes] = mine_ref[at].reshape(*up_ref.shape[:2], width)


def place_near_body(place, got_ref, held_ref, up_ref):
    up_ref[...] = got_ref[0].astype(F32).reshape(up_ref.shape)


def square_device(features, cotangent, up_blocks, down_blocks):
    local, feat, block_hidden = up_blocks.shape
    tokens = features.shape[1]
    n_dp, n_tensor = lax.axis_size("dp"), lax.axis_size("tensor")
    sub = block_hidden // (local * n_tensor)
    rows = local * sub
    half, part = local // 2, rows // 2
    factor = 1.0 / math.sqrt(tokens * n_dp)
    me = lax.axis_index("tensor").astype(jnp.int32)
    rank = lax.axis_index("dp").astype(jnp.int32)
    z, core = rank >> 1, rank & 1
    place = jnp.stack([me, z, core])
    x = features.reshape(local, feat, tokens)
    cot = cotangent.reshape(local, feat, tokens)
    one = (1, feat, tokens)
    blocks = (local, feat, tokens)
    every = lambda i, p: (i, 0, 0)
    least = lambda a, b: min(a, b) if isinstance(a, int) else jnp.minimum(a, b)
    most = lambda a, b: max(a, b) if isinstance(a, int) else jnp.maximum(a, b)
    low = lambda i, p: (least(i, half - 1), 0, 0)
    high = lambda i, p: (most(i - half, 0), 0, 0)

    def send(value, hop):
        return lax.ppermute(value, "tensor", [(t, t ^ hop) for t in range(n_tensor)])

    def send_z(value, hop):
        return lax.ppermute(value, "dp", [(d, d ^ (2 * hop)) for d in range(n_dp)])

    def send_core(value):
        return lax.ppermute(value, "dp", [(d, d ^ 1) for d in range(n_dp)])

    quarter = rows // 4
    at = (core * 2 + (z & 1)) * quarter
    to_i = jnp.stack(
        [
            lax.dynamic_slice(up_blocks, (0, at, (me ^ k) * rows), (local, quarter, rows))
            for k in (2, 3)
        ]
    )
    down_b = after((down_blocks,), to_i)[0]
    to_j = jnp.stack(
        [
            lax.dynamic_slice(down_b, (0, (me ^ k) * rows + at, 0), (local, quarter, feat))
            for k in (1, 3)
        ]
    )
    from_i, from_j = send(to_i, 2), send(to_j, 1)
    firsts = after((x[:half], x[half:], cot[:half], cot[half:]), to_i, to_j)
    x_lo, cot_lo = send(firsts[0], 2), send(firsts[2], 1)
    x_hi, cot_hi = send(firsts[1], 2), send(firsts[3], 1)

    def hidden_of(source, count, up, span):
        unit = (2, local, count, sub, tokens)
        block = (1, local, 1, sub, tokens)
        where = lambda j, i, p: (j, 0, i, 0, 0)
        return call(
            hidden_body,
            place,
            (2, count),
            [(source, one, lambda j, i, p: (i, 0, 0)), up],
            [(unit, BF16, block, where), (unit, BF16, block, where)],
            16,
        )

    hid, gate = hidden_of(
        x, local, (up_blocks, (1, feat, rows), lambda j, i, p: (i, 0, p[0] ^ j)), 0.0
    )
    from_i, from_j = after((from_i, from_j), hid)
    share = jnp.stack([from_i, from_j])
    share_z = send_z(share, 1)

    def unit_of(array, j):
        return (array, (1, 1) + array.shape[2:], lambda i, p: (j, i, 0, 0, 0))

    def down_of(j, which):
        if j == 0:
            if which == 0:
                return (down_blocks, (1, rows, feat), lambda i, p: (i, p[0], 0))
            return (
                down_blocks,
                (1, part, feat),
                lambda i, p: (i, 2 * (p[0] ^ 2) + which - 1, 0),
            )
        if which == 0:
            return (weights, (1, 1, 1, rows, feat), lambda i, p: (1, 0, i, 0, 0))
        return (weights, (1, 1, 1, part, feat), lambda i, p: (1, 1, i, which - 1, 0))

    def own_slope(which, array):
        return call_once(
            slope_body,
            place,
            local,
            [(cot, one, every), down_of(0, which), unit_of(array, 0)],
            [(array.shape[1:], BF16, (1,) + array.shape[2:], lambda i, p: (i, 0, 0, 0))],
            20,
        )[0]

    slope_ss = own_slope(0, gate)
    at_i = lambda i, p: (0, i, 0, 0)
    strip = (local, 1, sub, tokens)
    shard_u = (n_dp // 2, local * feat // n_dp, rows)

    def up_terms(body, ins, count, gives, span):
        block = (count, n_dp // 2, feat // n_dp, rows)
        wide = (count,) + shard_u
        part_u = (count, n_dp // 2, shard_u[1] // len(gives), rows)
        return call_once(
            body,
            place,
            local,
            ins,
            [
                (part_u, BF16, block, functools.partial(lambda m, i, p: (0, 0, m(i), 0), m))
                for m in gives
            ]
            + [(wide, BF16, block, lambda i, p: (0, 0, i, 0))],
            20,
            scratch=[pltpu.VMEM((n_dp // 2, 2, feat // n_dp, rows), BF16)],
            span=span,
        )

    def up_meet(count, keep, gots):
        piece = (count,) + shard_u[1:]
        return call(
            functools.partial(up_meet_body, len(gots)),
            place,
            (1,),
            [(v, (count,) + v.shape[1:], lambda i, p: (0, 0, 0, 0)) for v in (keep, *gots)],
            [whole_out(piece, BF16)] * 2 + [whole_out((2,) + piece, F32)],
            16,
        )

    def up_again(mine, far):
        piece = mine.shape[1:]
        return call(
            up_again_body, place, (1,), [whole(mine), whole(far)], [whole_out(piece, BF16)], 16
        )[0]

    give_e, keep_e = call_once(
        own_terms_body,
        place,
        local,
        [
            (cot, one, every),
            unit_of(hid, 0),
            (x, one, every),
            (slope_ss, strip, at_i),
        ],
        [whole_out((2,) + shard_u, BF16)] * 2,
        20,
        scratch=[
            pltpu.VMEM((2, part, feat), BF16),
            pltpu.VMEM((n_dp // 2, 2, feat // n_dp, rows), BF16),
        ],
    )
    share, share_z, x_lo, cot_lo = after((share, share_z, x_lo, cot_lo), give_e)
    core_parts = after((share, share_z), x_lo, cot_lo)
    weights = call(
        weights_body,
        place,
        (1,),
        [whole(v) for v in (share, share_z, *map(send_core, core_parts))],
        [whole_out((2, 2, local, 4, quarter, feat), BF16)],
        16,
    )[0].reshape(2, 2, local, rows, feat)

    def near_hidden(source, which):
        up = (
            weights,
            (1, 1, 1, feat, rows),
            lambda j, i, p: (0, j, which * half + i, 0, 0),
        )
        return hidden_of(source, half, up, 0.0)

    give_e = after((give_e,), x_lo, cot_lo)[0]
    first_got = send_core(give_e)
    send_e, far_e, mine_e = up_meet(1, keep_e, [first_got])
    got_e, far_e = send_z(send_e, 1), send_z(far_e, 1)
    x_lo = after((x_lo,), weights, send_e)[0]
    hid_lo, gate_lo = near_hidden(x_lo, 0)
    slope_lo_s = own_slope(1, gate_lo)

    got_e, far_e = after((got_e, far_e), slope_lo_s)
    send_e = up_again(mine_e, far_e)
    last_e = send_z(send_e, 2)

    x_hi = after((x_hi,), send_e)[0]
    hid_hi, gate_hi = near_hidden(x_hi, 1)
    cot_hi, last_e = after((cot_hi, last_e), hid_hi)

    def outputs_of(j, hid, kind):
        return call_once(
            outputs_body,
            place,
            local,
            [down_of(j, which) for which in range(3)]
            + [unit_of(array, j) for array in (hid, hid_lo, hid_hi)],
            [(blocks, kind, one, every)],
            16,
        )[0]

    def added(own, got):
        pairs_at = lambda i, p: (i, 0, 0)
        two = (2, feat, tokens)
        return call(
            add_body,
            place,
            (local // 2,),
            [(own, two, pairs_at), (got, two, pairs_at)],
            [(blocks, BF16, two, pairs_at)],
            20,
        )[0]

    shard = (2, 2, local, part, feat)
    strip_d = (1, part, feat)
    give_own, give_near, keep_d = call_once(
        down_terms_body,
        place,
        local,
        [(cot, one, every), (cot_lo, one, low), (cot_hi, one, high)]
        + [unit_of(hid, 1)]
        + [unit_of(array, j) for j in (0, 1) for array in (hid_lo, hid_hi)],
        [
            (shard[2:], BF16, strip_d, every),
            (shard[1:], BF16, (2,) + strip_d, lambda i, p: (0, i, 0, 0)),
            ((3,) + shard[2:], BF16, (3,) + strip_d, lambda i, p: (0, i, 0, 0)),
        ],
        16,
        scratch=[pltpu.VMEM((3, 2, part, feat), BF16)],
    )
    core_own, core_near = send_core(give_own), send_core(give_near)
    hid_b = after((hid,), give_own)[0]
    near_out = outputs_of(1, hid_b, BF16)
    got_out = send(near_out, 1)
    core_own, core_near = after((core_own, core_near), near_out)
    parts_d = (keep_e, first_got, keep_d, core_own, core_near)
    send_d, mine_d = call(
        down_meet_body,
        place,
        (1,),
        [whole(v) for v in parts_d],
        [whole_out(shard[1:], BF16), whole_out(shard[1:], F32)],
        16,
        scratch=[pltpu.VMEM(shard, F32)],
    )
    got_d = send_z(send_d, 1)
    cot_b, *near_b = after((cot, cot_lo, cot_hi), send_d)
    late = [(1, 0, gate), (1, 1, gate_lo), (1, 2, gate_hi), (0, 2, gate_hi)]
    slope_sn, slope_lo_n, slope_hi_n, slope_hi_s = call_once(
        late_slopes_body,
        place,
        local,
        [(cot_b, one, every), (near_b[0], one, low), (near_b[1], one, high)]
        + [down_of(j, which) for j, which, _ in late]
        + [unit_of(array, j) for j, _, array in late],
        [
            (array.shape[1:], BF16, (1,) + array.shape[2:], lambda i, p: (i, 0, 0, 0))
            for _, _, array in late
        ],
        20,
    )

    at_lo = lambda i, p: (0, least(i, half - 1), 0, 0)
    at_hi = lambda i, p: (0, most(i - half, 0), 0, 0)
    near_up = lambda j: (weights, (1, 1, 1, feat, rows), lambda i, p: (0, j, i, 0, 0))
    near_grads = call_once(
        near_grads_body,
        place,
        local,
        [
            near_up(0),
            near_up(1),
            (slope_lo_s, strip, at_lo),
            (slope_lo_n, strip, at_lo),
            (slope_hi_s, strip, at_hi),
            (slope_hi_n, strip, at_hi),
        ],
        [(blocks, BF16, one, every)],
        16,
    )[0]
    got_grads = send(near_grads, 2)

    x_b = after((x,), near_grads)[0]
    give_lo, give_hi, keep_u = up_terms(
        up_terms_body,
        [(x_b, one, every), (x_lo, one, low), (x_hi, one, high), (slope_sn, strip, at_i)]
        + [(slope_lo_s, strip, at_lo), (slope_lo_n, strip, at_lo)]
        + [(slope_hi_s, strip, at_hi), (slope_hi_n, strip, at_hi)],
        3,
        [lambda i: least(i, half - 1), lambda i: most(i - half, 0)],
        16.0,
    )
    send_u, far_u, mine_u = up_meet(3, keep_u, [send_core(give_lo), send_core(give_hi)])
    got_u, far_u = send_z(send_u, 1), send_z(far_u, 1)

    got_d = after((got_d,), send_u)[0]
    send_d, mine_d = call(
        down_again_body,
        place,
        (1,),
        [whole(mine_d), whole(got_d)],
        [whole_out(shard[2:], BF16), whole_out(shard[2:], F32)],
        16,
    )
    got_d = send_z(send_d, 2)

    up_b = after((up_blocks,), send_d)[0]
    own_grads = call_once(
        grads_body,
        place,
        local,
        [
            (up_b, (1, feat, rows), lambda i, p: (i, 0, p[0])),
            (up_b, (1, feat, rows), lambda i, p: (i, 0, p[0] ^ 1)),
            (slope_ss, strip, at_i),
            (slope_sn, strip, at_i),
        ],
        [(blocks, F32, one, every)],
        16,
        span=4.0,
    )[0]

    own_out = outputs_of(0, after((hid,), own_grads)[0], F32)
    far_u = after((far_u,), own_out)[0]
    send_u = up_again(mine_u, far_u)
    last_u = send_z(send_u, 2)

    got_d = after((got_d,), send_u)[0]
    sum_d = call(
        functools.partial(down_sum_body, factor),
        place,
        (1,),
        [whole(mine_d), whole(got_d)],
        [whole_out(shard[2:], BF16)],
        8,
    )[0]
    swaps = []
    for device in range(n_dp * n_tensor):
        dp, t = device // n_tensor, device % n_tensor
        z_low, x_at = dp // 2 % 2, t % 2
        home = (dp // 4 * 4 + x_at * 2 + dp % 2) * n_tensor + t // 2 * 2 + z_low
        swaps.append((device, home))
    home_d = lax.ppermute(sum_d, ("dp", "tensor"), swaps)

    got_out = after((got_out,), sum_d)[0]
    outputs = added(own_out, got_out)

    got_u, last_u = after((got_u, last_u), outputs)
    send_u, mine_u = call(
        functools.partial(up_sum_body, factor),
        place,
        (1,),
        [whole(v) for v in (mine_e, got_e, last_e, mine_u, got_u, last_u)],
        [whole_out((2,) + shard_u[1:], BF16), whole_out((2,) + shard_u[1:], F32)],
        8,
    )
    got_u = send(send_u, 2)

    home_d = after((home_d,), send_u)[0]
    held, down_grads = call(
        place_own_body,
        place,
        (1,),
        [whole(mine_u), whole(home_d)],
        [
            whole_out((local, feat // n_dp, block_hidden), F32),
            whole_out((local, part, feat), F32),
        ],
        8,
    )
    got_grads = after((got_grads,), held)[0]
    feature_grads = added(own_grads, got_grads)

    got_u = after((got_u,), feature_grads)[0]
    up_grads = call(
        place_near_body,
        place,
        (2,),
        [
            (got_u, (1,) + shard_u[1:], lambda a, p: (a, 0, 0)),
            (held, None, None),
        ],
        [
            (
                (local, feat // n_dp, block_hidden),
                F32,
                (local, feat // n_dp, rows),
                lambda a, p: (0, 0, p[0] ^ 2 ^ a),
            )
        ],
        8,
        alias={2: 0},
    )[0]
    wide = (local * feat, tokens)
    return (outputs.reshape(wide), feature_grads.reshape(wide), up_grads, down_grads)


def solution(mesh):
    in_specs = (
        P("tensor", "dp"),
        P("tensor", "dp"),
        P("tensor", None, None),
        P("tensor", None, None),
    )
    out_specs = (
        P("tensor", "dp"),
        P("tensor", "dp"),
        P("tensor", "dp", None),
        P("tensor", "dp", None),
    )
    small = mesh.shape["tensor"] == 4 and mesh.shape["dp"] == 8
    return jax.shard_map(
        square_device if small else generic_device,
        mesh=mesh,
        in_specs=in_specs,
        out_specs=out_specs,
        check_vma=False,
    )
```

```python
import functools
import math

import jax
import jax.numpy as jnp
from jax import lax
from jax.experimental import pallas as pl
from jax.experimental.pallas import tpu as pltpu
from jax.sharding import PartitionSpec as P

BF16 = jnp.bfloat16
F32 = jnp.float32
INV_ROOT2 = 0.7071067811865476
INV_ROOT2PI = 0.3989422804014327
MIB = 1024 * 1024


def gelu_value(value):
    return 0.5 * value * (1.0 + lax.erf(value * INV_ROOT2))


def gelu_slope(value):
    return (
        0.5 * (1.0 + lax.erf(value * INV_ROOT2))
        + value * jnp.exp(-0.5 * value * value) * INV_ROOT2PI
    )


def generic_device(features, cotangent, up_blocks, down_blocks):
    local_blocks, block_feat, block_hidden = up_blocks.shape
    blocks = local_blocks * lax.axis_size("tensor")
    sub = block_hidden // blocks
    tokens_here = features.shape[1]
    factor = 1.0 / math.sqrt(tokens_here * lax.axis_size("dp"))
    x_local = features.reshape(local_blocks, block_feat, tokens_here)
    dy_local = cotangent.reshape(local_blocks, block_feat, tokens_here)
    down_four = down_blocks.reshape(local_blocks, blocks, sub, block_feat)
    preact = jnp.einsum("bdn,bdf->bfn", x_local, up_blocks, preferred_element_type=F32)
    pre_wide = preact.astype(BF16).astype(F32)
    hidden = gelu_value(pre_wide).astype(BF16).reshape(local_blocks, blocks, sub, tokens_here)
    mixed = lax.all_to_all(hidden, "tensor", split_axis=1, concat_axis=0, tiled=True)
    out_three = jnp.einsum("ijsn,jise->jen", mixed, down_four, preferred_element_type=F32)
    outputs = out_three.astype(BF16).reshape(local_blocks * block_feat, tokens_here)
    down_term = jnp.einsum("ijsn,jen->isje", mixed, dy_local, preferred_element_type=F32)
    down_term = down_term.reshape(block_hidden, local_blocks, block_feat)
    back = jnp.einsum("jen,jise->ijsn", dy_local, down_four, preferred_element_type=F32)
    back_home = lax.all_to_all(
        back.astype(BF16), "tensor", split_axis=0, concat_axis=1, tiled=True
    ).reshape(local_blocks, block_hidden, tokens_here)
    slope = (back_home.astype(F32) * gelu_slope(pre_wide)).astype(BF16)
    up_term = jnp.einsum("bdn,bfn->dbf", x_local, slope, preferred_element_type=F32)
    up_share = lax.psum_scatter(up_term, "dp", scatter_dimension=0, tiled=True)
    down_share = lax.psum_scatter(down_term, "dp", scatter_dimension=0, tiled=True)
    dx_three = jnp.einsum("bfn,bdf->bdn", slope, up_blocks, preferred_element_type=F32)
    feature_grads = dx_three.astype(BF16).reshape(local_blocks * block_feat, tokens_here)
    up_grads = jnp.transpose(up_share, (1, 0, 2)) * factor
    down_grads = jnp.transpose(down_share, (1, 0, 2)) * factor
    return (outputs, feature_grads, up_grads, down_grads)


def dot_tn(a, b):
    return lax.dot_general(a, b, (((0,), (0,)), ((), ())), preferred_element_type=F32)


def dot_nn(a, b):
    return lax.dot_general(a, b, (((1,), (0,)), ((), ())), preferred_element_type=F32)


def dot_nt(a, b):
    return lax.dot_general(a, b, (((1,), (1,)), ((), ())), preferred_element_type=F32)


def call(body, place, grid, ins, outs, mib, scratch=(), span=0.0, alias=None):
    return pl.pallas_call(
        body,
        grid_spec=pltpu.PrefetchScalarGridSpec(
            num_scalar_prefetch=1,
            grid=grid,
            in_specs=[
                pl.BlockSpec(b, m) if b else pl.BlockSpec(memory_space=pl.ANY) for _, b, m in ins
            ],
            out_specs=[pl.BlockSpec(b, m) for _, _, b, m in outs],
            scratch_shapes=list(scratch),
        ),
        out_shape=[jax.ShapeDtypeStruct(s, d) for s, d, _, _ in outs],
        input_output_aliases=alias or {},
        compiler_params=pltpu.CompilerParams(vmem_limit_bytes=mib * MIB),
        cost_estimate=pl.CostEstimate(
            flops=int(span * 1e9), bytes_accessed=0, transcendentals=0
        ),
    )(place, *[a for a, _, _ in ins])


def block_of(ref, block, where):
    at = []
    for size, extent, index in zip(block, ref.shape, where):
        if size == extent:
            at.append(slice(None))
        elif isinstance(index, int):
            at.append(slice(index * size, (index + 1) * size))
        else:
            at.append(pl.ds(pl.multiple_of(index * size, size), size))
    return ref.at[tuple(at)]


def call_once(body, place, steps, ins, outs, mib, scratch=(), span=0.0):
    def every_step(place, *refs):
        blocks = [(b, m) for _, b, m in ins] + [(b, m) for _, _, b, m in outs]
        held, rest = refs[: len(blocks)], refs[len(blocks) :]
        for step in range(steps):
            views = [block_of(ref, b, m(step, place)) for ref, (b, m) in zip(held, blocks)]
            body(step, steps, place, *views, *rest)

    return call(
        every_step,
        place,
        (1,),
        [whole(a) for a, _, _ in ins],
        [whole_out(s, d) for s, d, _, _ in outs],
        mib,
        scratch=scratch,
        span=span,
    )


def whole(array):
    rank = array.ndim
    return (array, array.shape, lambda *at: (0,) * rank)


def whole_out(shape, kind):
    rank = len(shape)
    return (shape, kind, shape, lambda *at: (0,) * rank)


def after(values, *earlier):
    return lax.optimization_barrier((tuple(values), earlier))[0]


def square(ref):
    block = ref[...]
    width = block.shape[-1]
    return block.reshape(block.size // width, width)


def hidden_body(place, x_ref, up_ref, hidden_ref, gate_ref):
    pre = dot_tn(square(up_ref), square(x_ref)).astype(BF16).astype(F32)
    half_cdf = 0.5 + 0.5 * lax.erf(pre * INV_ROOT2)
    gate = half_cdf + pre * jnp.exp(-0.5 * pre * pre) * INV_ROOT2PI
    hidden_ref[...] = (pre * half_cdf).astype(BF16).reshape(hidden_ref.shape)
    gate_ref[...] = gate.astype(BF16).reshape(gate_ref.shape)


def weights_body(place, *refs):
    low, core, out_ref = place[1] % 2, place[2], refs[-1]
    for at in range(2):
        out_ref[:, :, :, core * 2 + (low ^ at)] = refs[at][...]
        out_ref[:, :, :, (1 - core) * 2 + (low ^ at)] = refs[2 + at][...]


def halves(step, steps, work, lo, hi):
    work(*(lo if step < steps // 2 else hi))


def stacked(refs, axis=0):
    return jnp.concatenate([square(ref) for ref in refs], axis)


def put_slopes(cot, downs, gates, slopes):
    back = dot_nn(stacked(downs), cot).astype(BF16)
    base = 0
    for gate_ref, slope_ref in zip(gates, slopes):
        gate = square(gate_ref).astype(F32)
        mine = back[base : base + gate.shape[0]].astype(F32)
        slope_ref[...] = (mine * gate).astype(BF16).reshape(slope_ref.shape)
        base += gate.shape[0]


def slope_body(step, steps, place, cot_ref, down_ref, gate_ref, slope_ref):
    put_slopes(square(cot_ref), [down_ref], [gate_ref], [slope_ref])


def near_slopes_body(step, steps, place, own_ref, near_ref, *refs):
    downs, gates, slopes = refs[:3], refs[3:6], refs[6:]
    put_slopes(square(own_ref), downs[:1], gates[:1], slopes[:1])
    put_slopes(square(near_ref), downs[1:], gates[1:], slopes[1:])


def own_terms_body(step, steps, place, cot_ref, hid_ref, x_ref, slope_ref, give_ref, keep_ref, down_s, up_s):
    core = place[2]
    up_s[...] = dot_nt(square(x_ref), square(slope_ref)).astype(BF16).reshape(up_s.shape)
    count = up_s.shape[2]
    strip = slice(step * count, (step + 1) * count)
    give_ref[0, :, strip] = up_s[:, 1 - core]
    keep_ref[0, :, strip] = up_s[:, core]
    down_s[...] = dot_nt(square(hid_ref), square(cot_ref)).astype(BF16).reshape(down_s.shape)
    give_ref[1, step] = down_s[1 - core]
    keep_ref[1, step] = down_s[core]


def down_terms_body(step, steps, place, own_ref, near_0, near_1, sn, ns_0, ns_1, nn_0, nn_1, give_own, give_near, keep_ref, term_s):
    core = place[2]

    def put(pair, terms, give):
        term_s[pair] = terms.astype(BF16).reshape(term_s.shape[1:])
        give[...] = term_s[pair, 1 - core].reshape(give.shape)
        keep_ref[pair, 0] = term_s[pair, core]

    rows = 2 * term_s.shape[2]
    hidden = jnp.concatenate([square(sn), stacked((nn_0, nn_1), 1)])
    mixed = dot_nt(hidden, stacked((near_0, near_1), 1))
    put(0, mixed[:rows], give_own)
    put(1, dot_nt(stacked((ns_0, ns_1), 1), square(own_ref)), give_near.at[0])
    put(2, mixed[rows:], give_near.at[1])


def up_terms_body(step, steps, place, x_ref, x_0, x_1, sn_0, sn_1, ns_0, ns_1, nn_0, nn_1, give_lo, give_hi, keep_ref, term_s):
    core, near = place[2], stacked((x_0, x_1), 1)
    give_ref = give_lo if step < steps // 2 else give_hi
    slopes = ((sn_0, sn_1), (ns_0, ns_1), (nn_0, nn_1))
    for pair, (x, refs) in enumerate(zip((square(x_ref), near, near), slopes)):
        term_s[...] = dot_nt(x, stacked(refs, 1)).astype(BF16).reshape(term_s.shape)
        give_ref[pair] = term_s[:, 1 - core]
        keep_ref[pair] = term_s[:, core]


def outputs_body(step, steps, place, d_own, d_near, hid_ref, *refs):
    *nears, out_ref = refs

    def work(near_ref):
        total = dot_tn(stacked((d_own, d_near)), stacked((hid_ref, near_ref)))
        out_ref[0] = total.astype(out_ref.dtype)

    halves(step, steps, work, nears[:1], nears[-1:])


def grads_body(step, steps, place, up_own, up_near, slope_own, *refs):
    *nears, out_ref = refs

    def work(near_ref):
        total = dot_nn(stacked((up_own, up_near), 1), stacked((slope_own, near_ref)))
        out_ref[0] = total.astype(out_ref.dtype)

    halves(step, steps, work, nears[:1], nears[-1:])


def add_body(place, own_ref, got_0, got_1, out_ref):
    width = got_0.shape[-1]
    for at, ref in enumerate((got_0, got_1)):
        lanes = slice(at * width, (at + 1) * width)
        out_ref[:, :, lanes] = (own_ref[:, :, lanes] + ref[...].astype(F32)).astype(BF16)


def down_meet_body(place, first, first_got, keep_ref, got_own, got_near, send_ref, mine_ref, total_s):
    stay = (place[0] ^ place[1]) & 1
    total_s[0, 0] = first[1].astype(F32) + first_got[1].astype(F32)
    total_s[0, 1] = keep_ref[0].astype(F32) + got_own[...].astype(F32)
    total_s[1] = keep_ref[1:].astype(F32) + got_near[...].astype(F32)
    mine_ref[...] = total_s[:, stay]
    send_ref[...] = total_s[:, 1 - stay].astype(BF16)


def down_again_body(place, mine_ref, got_ref, send_ref, own_ref):
    stay = (place[0] // 2) ^ (place[1] // 2)
    own_ref[...] = mine_ref[stay] + got_ref[stay].astype(F32)
    send_ref[...] = (mine_ref[1 - stay] + got_ref[1 - stay].astype(F32)).astype(BF16)


def down_sum_body(factor, place, own_ref, got_ref, out_ref):
    out_ref[...] = ((own_ref[...] + got_ref[...].astype(F32)) * factor).astype(BF16)


def up_meet_body(parts, place, keep_ref, *refs):
    gots, sends, mine_ref = refs[:parts], refs[parts:-1], refs[-1]
    rows = gots[0].shape[2]
    for hop in range(4):
        there = place[1] ^ hop
        for at, got_ref in enumerate(gots):
            strip = slice(at * rows, (at + 1) * rows)
            total = keep_ref[:, there, strip].astype(F32) + got_ref[:, there].astype(F32)
            if hop % 2:
                sends[hop // 2][:, strip] = total.astype(BF16)
            else:
                mine_ref[hop // 2, :, strip] = total


def up_again_body(place, mine_ref, far_ref, send_ref):
    send_ref[...] = (mine_ref[1] + far_ref[...].astype(F32)).astype(BF16)


def up_sum_body(factor, place, *refs):
    ins, (send_ref, mine_ref) = refs[:6], refs[6:]
    first, total = (
        (own[0] + near[...].astype(F32) + far[...].astype(F32)) * factor
        for own, near, far in (ins[:3], ins[3:])
    )
    mine_ref[0] = first[0]
    mine_ref[1] = total[0]
    send_ref[...] = total[1:].astype(BF16)


def place_own_body(place, mine_ref, down_in, up_ref, down_ref):
    down_ref[...] = down_in[...].astype(F32)
    width = mine_ref.shape[-1]
    for at in range(2):
        lanes = pl.ds(pl.multiple_of((place[0] ^ at) * width, width), width)
        up_ref[:, :, lanes] = mine_ref[at].reshape(*up_ref.shape[:2], width)


def place_near_body(place, got_ref, held_ref, up_ref):
    up_ref[...] = got_ref[0].astype(F32).reshape(up_ref.shape)


def square_device(features, cotangent, up_blocks, down_blocks):
    local, feat, block_hidden = up_blocks.shape
    tokens = features.shape[1]
    n_dp, n_tensor = lax.axis_size("dp"), lax.axis_size("tensor")
    sub = block_hidden // (local * n_tensor)
    rows = local * sub
    part, span_t = rows // 2, tokens // 2
    factor = 1.0 / math.sqrt(tokens * n_dp)
    me = lax.axis_index("tensor").astype(jnp.int32)
    rank = lax.axis_index("dp").astype(jnp.int32)
    z, core = rank >> 1, rank & 1
    place = jnp.stack([me, z, core])
    x = features.reshape(local, feat, tokens)
    cot = cotangent.reshape(local, feat, tokens)
    one = (1, feat, tokens)
    blocks = (local, feat, tokens)
    half_one = (1, feat, span_t)
    every = lambda i, p: (i, 0, 0)

    def send(value, hop):
        return lax.ppermute(value, "tensor", [(t, t ^ hop) for t in range(n_tensor)])

    def send_z(value, hop):
        return lax.ppermute(value, "dp", [(d, d ^ (2 * hop)) for d in range(n_dp)])

    def send_core(value):
        return lax.ppermute(value, "dp", [(d, d ^ 1) for d in range(n_dp)])

    quarter = rows // 4
    at = (core * 2 + (z & 1)) * quarter
    to_i = jnp.stack(
        [
            lax.dynamic_slice(up_blocks, (0, at, (me ^ k) * rows), (local, quarter, rows))
            for k in (2, 3)
        ]
    )
    down_b = after((down_blocks,), to_i)[0]
    to_j = jnp.stack(
        [
            lax.dynamic_slice(down_b, (0, (me ^ k) * rows + at, 0), (local, quarter, feat))
            for k in (1, 3)
        ]
    )
    from_i, from_j = send(to_i, 2), send(to_j, 1)
    firsts = after([v[..., t] for v in (x, cot) for t in (slice(span_t), slice(span_t, tokens))], to_i, to_j)
    x_0, cot_0 = send(firsts[0], 2), send(firsts[2], 1)
    x_1, cot_1 = send(firsts[1], 2), send(firsts[3], 1)

    def hidden_of(source, up):
        width = source.shape[-1]
        unit = (2, local, local, sub, width)
        block = (1, local, 1, sub, width)
        where = lambda j, i, p: (j, 0, i, 0, 0)
        return call(
            hidden_body,
            place,
            (2, local),
            [(source, (1, feat, width), lambda j, i, p: (i, 0, 0)), up],
            [(unit, BF16, block, where), (unit, BF16, block, where)],
            16,
        )

    hid, gate = hidden_of(x, (up_blocks, (1, feat, rows), lambda j, i, p: (i, 0, p[0] ^ j)))
    from_i, from_j = after((from_i, from_j), hid)
    share = jnp.stack([from_i, from_j])
    share_z = send_z(share, 1)

    def unit_of(array, j, t=0):
        if t is None:
            return (array, (1, 1) + array.shape[2:], lambda i, p: (j, i, 0, 0, 0))
        return (array, (1, 1) + array.shape[2:4] + (span_t,), lambda i, p: (j, i, 0, 0, t))

    def down_of(j, near):
        if j == 0:
            return (down_blocks, (1, rows, feat), lambda i, p: (i, p[0] ^ (2 * near), 0))
        return (weights, (1, 1, 1, rows, feat), lambda i, p: (1, near, i, 0, 0))

    slope_ss = call_once(
        slope_body,
        place,
        local,
        [(cot, one, every), down_of(0, 0), unit_of(gate, 0, None)],
        [(gate.shape[1:], BF16, (1,) + gate.shape[2:], lambda i, p: (i, 0, 0, 0))],
        20,
    )[0]

    at_i = lambda i, p: (0, i, 0, 0)
    strip = (local, 1, sub, tokens)
    shard_u = (n_dp // 2, local * feat // n_dp, rows)
    up_block = (3, n_dp // 2, feat // n_dp, rows)

    def up_meet(count, keep, gots):
        piece = (count,) + shard_u[1:]
        return call(
            functools.partial(up_meet_body, len(gots)),
            place,
            (1,),
            [(v, (count,) + v.shape[1:], lambda i, p: (0, 0, 0, 0)) for v in (keep, *gots)],
            [whole_out(piece, BF16)] * 2 + [whole_out((2,) + piece, F32)],
            16,
        )

    def up_again(mine, far):
        piece = mine.shape[1:]
        return call(
            up_again_body, place, (1,), [whole(mine), whole(far)], [whole_out(piece, BF16)], 16
        )[0]

    give_e, keep_e = call_once(
        own_terms_body,
        place,
        local,
        [
            (cot, one, every),
            unit_of(hid, 0, None),
            (x, one, every),
            (slope_ss, strip, at_i),
        ],
        [whole_out((2,) + shard_u, BF16)] * 2,
        20,
        scratch=[
            pltpu.VMEM((2, part, feat), BF16),
            pltpu.VMEM((n_dp // 2, 2, feat // n_dp, rows), BF16),
        ],
    )
    share, share_z, x_0, cot_0 = after((share, share_z, x_0, cot_0), give_e)
    core_parts = after((share, share_z), x_0, cot_0)
    weights = call(
        weights_body,
        place,
        (1,),
        [whole(v) for v in (share, share_z, *map(send_core, core_parts))],
        [whole_out((2, 2, local, 4, quarter, feat), BF16)],
        16,
    )[0].reshape(2, 2, local, rows, feat)

    give_e = after((give_e,), x_0, cot_0)[0]
    first_got = send_core(give_e)
    send_e, far_e, mine_e = up_meet(1, keep_e, [first_got])
    got_e, far_e = send_z(send_e, 1), send_z(far_e, 1)

    near_up = lambda j: (weights, (1, 1, 1, feat, rows), lambda i, p: (0, j, i, 0, 0))
    at_i = lambda i, p: (0, i, 0, 0)
    strip_t = (local, 1, sub, span_t)

    def near_hidden(source):
        up = (weights, (1, 1, 1, feat, rows), lambda j, i, p: (0, j, i, 0, 0))
        return hidden_of(source, up)

    def near_slopes(t, near_cot, near_gate):
        kind = (local, local, sub, span_t)
        return call_once(
            near_slopes_body,
            place,
            local,
            [(cot, half_one, lambda i, p: (i, 0, t)), (near_cot, half_one, every)]
            + [down_of(0, 1), down_of(1, 0), down_of(1, 1)]
            + [unit_of(near_gate, 0), unit_of(gate, 1, t), unit_of(near_gate, 1)],
            [(kind, BF16, (1,) + kind[1:], lambda i, p: (i, 0, 0, 0))] * 3,
            20,
        )

    def near_outputs(t, own_hid, near_hid):
        return call_once(
            outputs_body,
            place,
            local,
            [down_of(1, 0), down_of(1, 1), unit_of(own_hid, 1, t), unit_of(near_hid, 1)],
            [((local, feat, span_t), BF16, half_one, every)],
            16,
        )[0]

    def near_grads(from_own, from_near):
        return call_once(
            grads_body,
            place,
            local,
            [near_up(0), near_up(1), (from_own, strip_t, at_i), (from_near, strip_t, at_i)],
            [((local, feat, span_t), BF16, half_one, every)],
            16,
        )[0]

    def added(own, got_0, got_1):
        pairs_at = lambda i, p: (i, 0, 0)
        two, two_t = (2, feat, tokens), (2, feat, span_t)
        return call(
            add_body,
            place,
            (local // 2,),
            [(own, two, pairs_at), (got_0, two_t, pairs_at), (got_1, two_t, pairs_at)],
            [(blocks, BF16, two, pairs_at)],
            20,
        )[0]

    x_0 = after((x_0,), weights, send_e)[0]
    hid_0, gate_0 = near_hidden(x_0)
    ns_0, sn_0, nn_0 = near_slopes(0, cot_0, gate_0)
    out_0 = near_outputs(0, hid, hid_0)
    got_out_0 = send(out_0, 1)
    ns_b = after((ns_0,), out_0)[0]
    dx_0 = near_grads(ns_b, nn_0)
    got_dx_0 = send(dx_0, 2)

    got_e, far_e = after((got_e, far_e), dx_0)
    send_e = up_again(mine_e, far_e)
    last_e = send_z(send_e, 2)

    x_1 = after((x_1,), send_e)[0]
    hid_1, gate_1 = near_hidden(x_1)
    cot_1, last_e = after((cot_1, last_e), hid_1)

    shard = (2, 2, local, part, feat)
    strip_d = (1, part, feat)
    give_own, give_near, keep_d = call_once(
        down_terms_body,
        place,
        local,
        [(cot, one, every), (cot_0, half_one, every), (cot_1, half_one, every)]
        + [unit_of(hid, 1, None)]
        + [unit_of(array, j) for j in (0, 1) for array in (hid_0, hid_1)],
        [
            (shard[2:], BF16, strip_d, every),
            (shard[1:], BF16, (2,) + strip_d, lambda i, p: (0, i, 0, 0)),
            ((3,) + shard[2:], BF16, (3,) + strip_d, lambda i, p: (0, i, 0, 0)),
        ],
        16,
        scratch=[pltpu.VMEM((3, 2, part, feat), BF16)],
    )
    core_own, core_near = send_core(give_own), send_core(give_near)
    hid_b = after((hid,), give_own)[0]
    out_1 = near_outputs(1, hid_b, hid_1)
    core_own, core_near = after((core_own, core_near), out_1)
    parts_d = (keep_e, first_got, keep_d, core_own, core_near)
    send_d, mine_d = call(
        down_meet_body,
        place,
        (1,),
        [whole(v) for v in parts_d],
        [whole_out(shard[1:], BF16), whole_out(shard[1:], F32)],
        16,
        scratch=[pltpu.VMEM(shard, F32)],
    )
    got_d = send_z(send_d, 1)
    cot_1 = after((cot_1,), send_d)[0]
    ns_1, sn_1, nn_1 = near_slopes(1, cot_1, gate_1)
    dx_1 = near_grads(ns_1, nn_1)

    x_b = after((x,), dx_1)[0]
    strips = [(v, strip_t, at_i) for v in (sn_0, sn_1, ns_0, ns_1, nn_0, nn_1)]
    give_lo, give_hi, keep_u = call_once(
        up_terms_body,
        place,
        local,
        [(x_b, one, every), (x_0, half_one, every), (x_1, half_one, every)] + strips,
        [
            ((3, n_dp // 2, shard_u[1] // 2, rows), BF16, up_block, lambda i, p: (0, 0, min(i, local // 2 - 1), 0)),
            ((3, n_dp // 2, shard_u[1] // 2, rows), BF16, up_block, lambda i, p: (0, 0, max(i - local // 2, 0), 0)),
            ((3,) + shard_u, BF16, up_block, lambda i, p: (0, 0, i, 0)),
        ],
        20,
        scratch=[pltpu.VMEM((n_dp // 2, 2, feat // n_dp, rows), BF16)],
        span=16.0,
    )
    send_u, far_u, mine_u = up_meet(3, keep_u, [send_core(give_lo), send_core(give_hi)])
    got_u, far_u = send_z(send_u, 1), send_z(far_u, 1)


    got_d = after((got_d,), send_u)[0]
    send_d, mine_d = call(
        down_again_body,
        place,
        (1,),
        [whole(mine_d), whole(got_d)],
        [whole_out(shard[2:], BF16), whole_out(shard[2:], F32)],
        16,
    )
    got_d = send_z(send_d, 2)

    got_out_0, got_dx_0 = after((got_out_0, got_dx_0), send_d)
    out_1, dx_1 = after((out_1, dx_1), got_out_0, got_dx_0)
    got_out_1, got_dx_1 = send(out_1, 1), send(dx_1, 2)

    up_b = after((up_blocks,), send_d)[0]
    at_half = lambda i, p: (0, i % local, 0, 0)
    own_grads = call_once(
        grads_body,
        place,
        2 * local,
        [
            (up_b, (1, feat, rows), lambda i, p: (i % local, 0, p[0])),
            (up_b, (1, feat, rows), lambda i, p: (i % local, 0, p[0] ^ 1)),
            (slope_ss, strip_t, lambda i, p: (0, i % local, 0, i // local)),
            (sn_0, strip_t, at_half),
            (sn_1, strip_t, at_half),
        ],
        [(blocks, F32, half_one, lambda i, p: (i % local, 0, i // local))],
        16,
        span=8.0,
    )[0]

    hid_c = after((hid,), own_grads)[0]
    in_turn = lambda spec: (spec[0], spec[1], lambda i, p: spec[2](i % local, p))
    own_out = call_once(
        outputs_body,
        place,
        2 * local,
        [
            in_turn(down_of(0, 0)),
            in_turn(down_of(0, 1)),
            (hid_c, (1, 1, local, sub, span_t), lambda i, p: (0, i % local, 0, 0, i // local)),
            in_turn(unit_of(hid_0, 0)),
            in_turn(unit_of(hid_1, 0)),
        ],
        [(blocks, F32, half_one, lambda i, p: (i % local, 0, i // local))],
        16,
    )[0]
    far_u = after((far_u,), own_out)[0]
    send_u = up_again(mine_u, far_u)
    last_u = send_z(send_u, 2)

    got_d = after((got_d,), send_u)[0]
    sum_d = call(
        functools.partial(down_sum_body, factor),
        place,
        (1,),
        [whole(mine_d), whole(got_d)],
        [whole_out(shard[2:], BF16)],
        8,
    )[0]
    swaps = []
    for device in range(n_dp * n_tensor):
        dp, t = device // n_tensor, device % n_tensor
        z_low, x_at = dp // 2 % 2, t % 2
        home = (dp // 4 * 4 + x_at * 2 + dp % 2) * n_tensor + t // 2 * 2 + z_low
        swaps.append((device, home))
    home_d = lax.ppermute(sum_d, ("dp", "tensor"), swaps)

    got_out_1 = after((got_out_1,), sum_d)[0]
    outputs = added(own_out, got_out_0, got_out_1)

    got_u, last_u = after((got_u, last_u), outputs)
    send_u, mine_u = call(
        functools.partial(up_sum_body, factor),
        place,
        (1,),
        [whole(v) for v in (mine_e, got_e, last_e, mine_u, got_u, last_u)],
        [whole_out((2,) + shard_u[1:], BF16), whole_out((2,) + shard_u[1:], F32)],
        8,
    )
    got_u = send(send_u, 2)

    home_d = after((home_d,), send_u)[0]
    held, down_grads = call(
        place_own_body,
        place,
        (1,),
        [whole(mine_u), whole(home_d)],
        [
            whole_out((local, feat // n_dp, block_hidden), F32),
            whole_out((local, part, feat), F32),
        ],
        8,
    )
    got_dx_1 = after((got_dx_1,), held)[0]
    feature_grads = added(own_grads, got_dx_0, got_dx_1)

    got_u = after((got_u,), feature_grads)[0]
    up_grads = call(
        place_near_body,
        place,
        (2,),
        [
            (got_u, (1,) + shard_u[1:], lambda a, p: (a, 0, 0)),
            (held, None, None),
        ],
        [
            (
                (local, feat // n_dp, block_hidden),
                F32,
                (local, feat // n_dp, rows),
                lambda a, p: (0, 0, p[0] ^ 2 ^ a),
            )
        ],
        8,
        alias={2: 0},
    )[0]
    wide = (local * feat, tokens)
    return (outputs.reshape(wide), feature_grads.reshape(wide), up_grads, down_grads)


def solution(mesh):
    in_specs = (
        P("tensor", "dp"),
        P("tensor", "dp"),
        P("tensor", None, None),
        P("tensor", None, None),
    )
    out_specs = (
        P("tensor", "dp"),
        P("tensor", "dp"),
        P("tensor", "dp", None),
        P("tensor", "dp", None),
    )
    small = mesh.shape["tensor"] == 4 and mesh.shape["dp"] == 8
    return jax.shard_map(
        square_device if small else generic_device,
        mesh=mesh,
        in_specs=in_specs,
        out_specs=out_specs,
        check_vma=False,
    )
```

```python
import functools
import math

import jax
import jax.numpy as jnp
from jax import lax
from jax.experimental import pallas as pl
from jax.experimental.pallas import tpu as pltpu
from jax.sharding import PartitionSpec as P

BF16 = jnp.bfloat16
F32 = jnp.float32
INV_ROOT2 = 0.7071067811865476
INV_ROOT2PI = 0.3989422804014327
MIB = 1024 * 1024


def gelu_value(value):
    return 0.5 * value * (1.0 + lax.erf(value * INV_ROOT2))


def gelu_slope(value):
    return (
        0.5 * (1.0 + lax.erf(value * INV_ROOT2))
        + value * jnp.exp(-0.5 * value * value) * INV_ROOT2PI
    )


def generic_device(features, cotangent, up_blocks, down_blocks):
    local_blocks, block_feat, block_hidden = up_blocks.shape
    blocks = local_blocks * lax.axis_size("tensor")
    sub = block_hidden // blocks
    tokens_here = features.shape[1]
    factor = 1.0 / math.sqrt(tokens_here * lax.axis_size("dp"))
    x_local = features.reshape(local_blocks, block_feat, tokens_here)
    dy_local = cotangent.reshape(local_blocks, block_feat, tokens_here)
    down_four = down_blocks.reshape(local_blocks, blocks, sub, block_feat)
    preact = jnp.einsum("bdn,bdf->bfn", x_local, up_blocks, preferred_element_type=F32)
    pre_wide = preact.astype(BF16).astype(F32)
    hidden = gelu_value(pre_wide).astype(BF16).reshape(local_blocks, blocks, sub, tokens_here)
    mixed = lax.all_to_all(hidden, "tensor", split_axis=1, concat_axis=0, tiled=True)
    out_three = jnp.einsum("ijsn,jise->jen", mixed, down_four, preferred_element_type=F32)
    outputs = out_three.astype(BF16).reshape(local_blocks * block_feat, tokens_here)
    down_term = jnp.einsum("ijsn,jen->isje", mixed, dy_local, preferred_element_type=F32)
    down_term = down_term.reshape(block_hidden, local_blocks, block_feat)
    back = jnp.einsum("jen,jise->ijsn", dy_local, down_four, preferred_element_type=F32)
    back_home = lax.all_to_all(
        back.astype(BF16), "tensor", split_axis=0, concat_axis=1, tiled=True
    ).reshape(local_blocks, block_hidden, tokens_here)
    slope = (back_home.astype(F32) * gelu_slope(pre_wide)).astype(BF16)
    up_term = jnp.einsum("bdn,bfn->dbf", x_local, slope, preferred_element_type=F32)
    up_share = lax.psum_scatter(up_term, "dp", scatter_dimension=0, tiled=True)
    down_share = lax.psum_scatter(down_term, "dp", scatter_dimension=0, tiled=True)
    dx_three = jnp.einsum("bfn,bdf->bdn", slope, up_blocks, preferred_element_type=F32)
    feature_grads = dx_three.astype(BF16).reshape(local_blocks * block_feat, tokens_here)
    up_grads = jnp.transpose(up_share, (1, 0, 2)) * factor
    down_grads = jnp.transpose(down_share, (1, 0, 2)) * factor
    return (outputs, feature_grads, up_grads, down_grads)


def dot_tn(a, b):
    return lax.dot_general(a, b, (((0,), (0,)), ((), ())), preferred_element_type=F32)


def dot_nn(a, b):
    return lax.dot_general(a, b, (((1,), (0,)), ((), ())), preferred_element_type=F32)


def dot_nt(a, b):
    return lax.dot_general(a, b, (((1,), (1,)), ((), ())), preferred_element_type=F32)


def call(body, place, grid, ins, outs, mib, scratch=(), span=0.0, alias=None):
    return pl.pallas_call(
        body,
        grid_spec=pltpu.PrefetchScalarGridSpec(
            num_scalar_prefetch=1,
            grid=grid,
            in_specs=[
                pl.BlockSpec(b, m) if b else pl.BlockSpec(memory_space=pl.ANY) for _, b, m in ins
            ],
            out_specs=[pl.BlockSpec(b, m) for _, _, b, m in outs],
            scratch_shapes=list(scratch),
        ),
        out_shape=[jax.ShapeDtypeStruct(s, d) for s, d, _, _ in outs],
        input_output_aliases=alias or {},
        compiler_params=pltpu.CompilerParams(vmem_limit_bytes=mib * MIB),
        cost_estimate=pl.CostEstimate(
            flops=int(span * 1e9), bytes_accessed=0, transcendentals=0
        ),
    )(place, *[a for a, _, _ in ins])


def block_of(ref, block, where):
    at = []
    for size, extent, index in zip(block, ref.shape, where):
        if size == extent:
            at.append(slice(None))
        elif isinstance(index, int):
            at.append(slice(index * size, (index + 1) * size))
        else:
            at.append(pl.ds(pl.multiple_of(index * size, size), size))
    return ref.at[tuple(at)]


def call_once(body, place, steps, ins, outs, mib, scratch=(), span=0.0):
    def every_step(place, *refs):
        blocks = [(b, m) for _, b, m in ins] + [(b, m) for _, _, b, m in outs]
        held, rest = refs[: len(blocks)], refs[len(blocks) :]
        for step in range(steps):
            views = [block_of(ref, b, m(step, place)) for ref, (b, m) in zip(held, blocks)]
            body(step, steps, place, *views, *rest)

    return call(
        every_step,
        place,
        (1,),
        [whole(a) for a, _, _ in ins],
        [whole_out(s, d) for s, d, _, _ in outs],
        mib,
        scratch=scratch,
        span=span,
    )


def by_grid(body):
    return lambda place, *refs: body(pl.program_id(0), pl.num_programs(0), place, *refs)


def whole(array):
    rank = array.ndim
    return (array, array.shape, lambda *at: (0,) * rank)


def whole_out(shape, kind):
    rank = len(shape)
    return (shape, kind, shape, lambda *at: (0,) * rank)


def after(values, *earlier):
    return lax.optimization_barrier((tuple(values), earlier))[0]


def square(ref):
    block = ref[...]
    width = block.shape[-1]
    return block.reshape(block.size // width, width)


def hidden_body(place, x_ref, up_ref, hidden_ref, gate_ref):
    pre = dot_tn(square(up_ref), square(x_ref)).astype(BF16).astype(F32)
    half_cdf = 0.5 + 0.5 * lax.erf(pre * INV_ROOT2)
    gate = half_cdf + pre * jnp.exp(-0.5 * pre * pre) * INV_ROOT2PI
    hidden_ref[...] = (pre * half_cdf).astype(BF16).reshape(hidden_ref.shape)
    gate_ref[...] = gate.astype(BF16).reshape(gate_ref.shape)


def weights_body(place, *refs):
    low, core, out_ref = place[1] % 2, place[2], refs[-1]
    for at in range(2):
        out_ref[:, :, :, core * 2 + (low ^ at)] = refs[at][...]
        out_ref[:, :, :, (1 - core) * 2 + (low ^ at)] = refs[2 + at][...]


def halves(step, steps, work, lo, hi):
    if isinstance(step, int):
        work(*(lo if step < steps // 2 else hi))
        return
    pl.when(step < steps // 2)(functools.partial(work, *lo))
    pl.when(step >= steps // 2)(functools.partial(work, *hi))


def stacked(refs, axis=0):
    return jnp.concatenate([square(ref) for ref in refs], axis)


def put_slopes(cot, downs, gates, slopes):
    back = dot_nn(stacked(downs), cot).astype(BF16)
    base = 0
    for gate_ref, slope_ref in zip(gates, slopes):
        gate = square(gate_ref).astype(F32)
        mine = back[base : base + gate.shape[0]].astype(F32)
        slope_ref[...] = (mine * gate).astype(BF16).reshape(slope_ref.shape)
        base += gate.shape[0]


def slope_body(step, steps, place, cot_ref, down_ref, gate_ref, slope_ref):
    put_slopes(square(cot_ref), [down_ref], [gate_ref], [slope_ref])


def late_body(step, steps, place, own_ref, near_lo, near_hi, *refs):
    downs, gates, (up_own, up_near, lo_s), slopes, out_ref = (
        refs[:4],
        refs[4:8],
        refs[8:11],
        refs[11:15],
        refs[15],
    )
    count = steps // 2
    if step < count:
        here = [ref.at[step] for ref in slopes]
        put_slopes(square(own_ref), downs[3:], gates[3:], here[3:])
        near_ref = near_lo if step < count // 2 else near_hi
        put_slopes(square(near_ref), downs[:3], gates[:3], here[:3])
        return
    sn, lo_n, hi_n, hi_s = slopes
    pair = (lo_s, lo_n) if step - count < count // 2 else (hi_s, hi_n)
    strips = [ref.at[:, (step - count) % (count // 2)] for ref in pair]
    out_ref[0] = dot_nn(stacked((up_own, up_near), 1), stacked(strips)).astype(BF16)


def own_terms_body(step, steps, place, cot_ref, hid_ref, x_ref, slope_ref, give_ref, keep_ref, down_s, up_s):
    core = place[2]
    up_s[...] = dot_nt(square(x_ref), square(slope_ref)).astype(BF16).reshape(up_s.shape)
    count = up_s.shape[2]
    strip = slice(step * count, (step + 1) * count)
    give_ref[0, :, strip] = up_s[:, 1 - core]
    keep_ref[0, :, strip] = up_s[:, core]
    down_s[...] = dot_nt(square(hid_ref), square(cot_ref)).astype(BF16).reshape(down_s.shape)
    give_ref[1, step] = down_s[1 - core]
    keep_ref[1, step] = down_s[core]


def down_terms_body(step, steps, place, own_ref, near_lo, near_hi, sn, ns_lo, ns_hi, nn_lo, nn_hi, give_own, give_near, keep_ref, term_s):
    core = place[2]

    def put(pair, terms, give):
        term_s[pair] = terms.astype(BF16).reshape(term_s.shape[1:])
        give[...] = term_s[pair, 1 - core].reshape(give.shape)
        keep_ref[pair, 0] = term_s[pair, core]

    def work(near_ref):
        rows = 2 * term_s.shape[2]
        mixed = dot_nt(stacked((sn, nn_lo, nn_hi)), square(near_ref))
        put(0, mixed[:rows], give_own)
        put(1, dot_nt(stacked((ns_lo, ns_hi)), square(own_ref)), give_near.at[0])
        put(2, mixed[rows:], give_near.at[1])

    halves(step, steps, work, (near_lo,), (near_hi,))


def put_up_term(pair, core, x, slope_ref, give_ref, keep_ref, term_s):
    term_s[...] = dot_nt(x, square(slope_ref)).astype(BF16).reshape(term_s.shape)
    give_ref[pair] = term_s[:, 1 - core]
    keep_ref[pair] = term_s[:, core]


def up_terms_body(step, steps, place, x_ref, x_lo, x_hi, sn, lo_s, lo_n, hi_s, hi_n, give_lo, give_hi, keep_ref, term_s):
    def work(x_near, from_own, from_near, give_ref):
        near = square(x_near)
        for pair, (x, ref) in enumerate(((square(x_ref), sn), (near, from_own), (near, from_near))):
            put_up_term(pair, place[2], x, ref, give_ref, keep_ref, term_s)

    lo, hi = (x_lo, lo_s, lo_n, give_lo), (x_hi, hi_s, hi_n, give_hi)
    halves(step, steps, work, lo, hi)


def outputs_body(step, steps, place, d_own, d_lo, d_hi, hid_ref, lo_ref, hi_ref, out_ref):
    total = dot_tn(stacked((d_own, d_lo, d_hi)), stacked((hid_ref, lo_ref, hi_ref)))
    out_ref[0] = total.astype(out_ref.dtype)


def grads_body(step, steps, place, up_own, up_near, slope_own, slope_near, out_ref):
    out_ref[0] = dot_nn(stacked((up_own, up_near), 1), stacked((slope_own, slope_near)))


def add_body(place, own_ref, got_ref, out_ref):
    out_ref[...] = (own_ref[...] + got_ref[...].astype(F32)).astype(BF16)


def down_meet_body(place, first, first_got, keep_ref, got_own, got_near, far_ref, near_ref, mine_ref):
    stay_j = (place[0] ^ place[1]) & 1
    stay_i = (place[0] // 2) ^ (place[1] // 2)
    kept = ((first.at[1], keep_ref.at[0]), (keep_ref.at[1], keep_ref.at[2]))
    got = ((first_got.at[1], got_own), (got_near.at[0], got_near.at[1]))
    for i in range(2):
        for j in range(2):

            @pl.when(jnp.logical_and(stay_i == i, stay_j == j))
            def _():
                total = lambda a, b: kept[a][b][...].astype(F32) + got[a][b][...].astype(F32)
                far_ref[...] = total(1 - i, 1 - j).astype(BF16)
                near_ref[...] = total(i, 1 - j).astype(BF16)
                mine_ref[0] = total(i, j)
                mine_ref[1] = total(1 - i, j)


def down_sum_body(factor, place, mine_ref, near_ref, got_ref, out_ref):
    total = mine_ref[0] + near_ref[...].astype(F32) + got_ref[...].astype(F32)
    out_ref[...] = (total * factor).astype(BF16)


def up_meet_body(parts, place, keep_ref, *refs):
    gots, sends, mine_ref = refs[:parts], refs[parts:-1], refs[-1]
    rows = gots[0].shape[2]
    for hop in range(4):
        there = place[1] ^ hop
        for at, got_ref in enumerate(gots):
            strip = slice(at * rows, (at + 1) * rows)
            total = keep_ref[:, there, strip].astype(F32) + got_ref[:, there].astype(F32)
            if hop % 2:
                sends[hop // 2][:, strip] = total.astype(BF16)
            else:
                mine_ref[hop // 2, :, strip] = total


def up_again_body(place, mine_ref, far_ref, send_ref):
    send_ref[...] = (mine_ref[1] + far_ref[...].astype(F32)).astype(BF16)


def up_sum_body(factor, place, *refs):
    ins, (send_ref, mine_ref) = refs[:6], refs[6:]
    first, total = (
        (own[0] + near[...].astype(F32) + far[...].astype(F32)) * factor
        for own, near, far in (ins[:3], ins[3:])
    )
    mine_ref[0] = first[0]
    mine_ref[1] = total[0]
    send_ref[...] = total[1:].astype(BF16)


def place_own_body(place, mine_ref, down_in, up_ref, down_ref):
    down_ref[...] = down_in[...].astype(F32)
    width = mine_ref.shape[-1]
    for at in range(2):
        lanes = pl.ds(pl.multiple_of((place[0] ^ at) * width, width), width)
        up_ref[:, :, lanes] = mine_ref[at].reshape(*up_ref.shape[:2], width)


def place_near_body(place, got_ref, held_ref, up_ref):
    up_ref[...] = got_ref[0].astype(F32).reshape(up_ref.shape)


def square_device(features, cotangent, up_blocks, down_blocks):
    local, feat, block_hidden = up_blocks.shape
    tokens = features.shape[1]
    n_dp, n_tensor = lax.axis_size("dp"), lax.axis_size("tensor")
    sub = block_hidden // (local * n_tensor)
    rows = local * sub
    half, part = local // 2, rows // 2
    factor = 1.0 / math.sqrt(tokens * n_dp)
    me = lax.axis_index("tensor").astype(jnp.int32)
    rank = lax.axis_index("dp").astype(jnp.int32)
    z, core = rank >> 1, rank & 1
    place = jnp.stack([me, z, core])
    x = features.reshape(local, feat, tokens)
    cot = cotangent.reshape(local, feat, tokens)
    one = (1, feat, tokens)
    blocks = (local, feat, tokens)
    every = lambda i, p: (i, 0, 0)
    least = lambda a, b: min(a, b) if isinstance(a, int) else jnp.minimum(a, b)
    most = lambda a, b: max(a, b) if isinstance(a, int) else jnp.maximum(a, b)
    low = lambda i, p: (least(i, half - 1), 0, 0)
    high = lambda i, p: (most(i - half, 0), 0, 0)

    def send(value, hop):
        return lax.ppermute(value, "tensor", [(t, t ^ hop) for t in range(n_tensor)])

    def send_z(value, hop):
        return lax.ppermute(value, "dp", [(d, d ^ (2 * hop)) for d in range(n_dp)])

    def send_core(value):
        return lax.ppermute(value, "dp", [(d, d ^ 1) for d in range(n_dp)])

    quarter = rows // 4
    at = (core * 2 + (z & 1)) * quarter
    to_i = jnp.stack(
        [
            lax.dynamic_slice(up_blocks, (0, at, (me ^ k) * rows), (local, quarter, rows))
            for k in (2, 3)
        ]
    )
    down_b = after((down_blocks,), to_i)[0]
    to_j = jnp.stack(
        [
            lax.dynamic_slice(down_b, (0, (me ^ k) * rows + at, 0), (local, quarter, feat))
            for k in (1, 3)
        ]
    )
    from_i, from_j = send(to_i, 2), send(to_j, 1)
    firsts = after((x[:half], x[half:], cot[:half], cot[half:]), to_i, to_j)
    x_lo, cot_lo = send(firsts[0], 2), send(firsts[2], 1)
    x_hi, cot_hi = send(firsts[1], 2), send(firsts[3], 1)

    def hidden_of(source, count, up, span):
        unit = (2, local, count, sub, tokens)
        block = (1, local, 1, sub, tokens)
        where = lambda j, i, p: (j, 0, i, 0, 0)
        return call(
            hidden_body,
            place,
            (2, count),
            [(source, one, lambda j, i, p: (i, 0, 0)), up],
            [(unit, BF16, block, where), (unit, BF16, block, where)],
            16,
        )

    hid, gate = hidden_of(
        x, local, (up_blocks, (1, feat, rows), lambda j, i, p: (i, 0, p[0] ^ j)), 0.0
    )
    from_i, from_j = after((from_i, from_j), hid)
    share = jnp.stack([from_i, from_j])
    share_z = send_z(share, 1)

    def unit_of(array, j):
        return (array, (1, 1) + array.shape[2:], lambda i, p: (j, i, 0, 0, 0))

    def down_of(j, which):
        if j == 0:
            if which == 0:
                return (down_blocks, (1, rows, feat), lambda i, p: (i, p[0], 0))
            return (
                down_blocks,
                (1, part, feat),
                lambda i, p: (i, 2 * (p[0] ^ 2) + which - 1, 0),
            )
        if which == 0:
            return (weights, (1, 1, 1, rows, feat), lambda i, p: (1, 0, i, 0, 0))
        return (weights, (1, 1, 1, part, feat), lambda i, p: (1, 1, i, which - 1, 0))

    def own_slope(which, array):
        return call_once(
            slope_body,
            place,
            local,
            [(cot, one, every), down_of(0, which), unit_of(array, 0)],
            [(array.shape[1:], BF16, (1,) + array.shape[2:], lambda i, p: (i, 0, 0, 0))],
            20,
        )[0]

    slope_ss = own_slope(0, gate)
    at_i = lambda i, p: (0, i, 0, 0)
    strip = (local, 1, sub, tokens)
    shard_u = (n_dp // 2, local * feat // n_dp, rows)

    def up_terms(body, ins, count, gives, span):
        block = (count, n_dp // 2, feat // n_dp, rows)
        wide = (count,) + shard_u
        part_u = (count, n_dp // 2, shard_u[1] // len(gives), rows)
        return call_once(
            body,
            place,
            local,
            ins,
            [
                (part_u, BF16, block, functools.partial(lambda m, i, p: (0, 0, m(i), 0), m))
                for m in gives
            ]
            + [(wide, BF16, block, lambda i, p: (0, 0, i, 0))],
            20,
            scratch=[pltpu.VMEM((n_dp // 2, 2, feat // n_dp, rows), BF16)],
            span=span,
        )

    def up_meet(count, keep, gots):
        piece = (count,) + shard_u[1:]
        return call(
            functools.partial(up_meet_body, len(gots)),
            place,
            (1,),
            [(v, (count,) + v.shape[1:], lambda i, p: (0, 0, 0, 0)) for v in (keep, *gots)],
            [whole_out(piece, BF16)] * 2 + [whole_out((2,) + piece, F32)],
            16,
        )

    def up_again(mine, far):
        piece = mine.shape[1:]
        return call(
            up_again_body, place, (1,), [whole(mine), whole(far)], [whole_out(piece, BF16)], 16
        )[0]

    give_e, keep_e = call_once(
        own_terms_body,
        place,
        local,
        [
            (cot, one, every),
            unit_of(hid, 0),
            (x, one, every),
            (slope_ss, strip, at_i),
        ],
        [whole_out((2,) + shard_u, BF16)] * 2,
        20,
        scratch=[
            pltpu.VMEM((2, part, feat), BF16),
            pltpu.VMEM((n_dp // 2, 2, feat // n_dp, rows), BF16),
        ],
    )
    share, share_z, x_lo, cot_lo = after((share, share_z, x_lo, cot_lo), give_e)
    core_parts = after((share, share_z), x_lo, cot_lo)
    weights = call(
        weights_body,
        place,
        (1,),
        [whole(v) for v in (share, share_z, *map(send_core, core_parts))],
        [whole_out((2, 2, local, 4, quarter, feat), BF16)],
        16,
    )[0].reshape(2, 2, local, rows, feat)

    def near_hidden(source, which):
        up = (
            weights,
            (1, 1, 1, feat, rows),
            lambda j, i, p: (0, j, which * half + i, 0, 0),
        )
        return hidden_of(source, half, up, 0.0)

    give_e = after((give_e,), x_lo, cot_lo)[0]
    first_got = send_core(give_e)
    send_e, far_e, mine_e = up_meet(1, keep_e, [first_got])
    got_e, far_e = send_z(send_e, 1), send_z(far_e, 1)
    x_lo = after((x_lo,), weights, send_e)[0]
    hid_lo, gate_lo = near_hidden(x_lo, 0)
    slope_lo_s = own_slope(1, gate_lo)

    got_e, far_e = after((got_e, far_e), slope_lo_s)
    send_e = up_again(mine_e, far_e)
    last_e = send_z(send_e, 2)

    x_hi = after((x_hi,), send_e)[0]
    hid_hi, gate_hi = near_hidden(x_hi, 1)
    cot_hi, last_e = after((cot_hi, last_e), hid_hi)

    def outputs_of(j, hid, kind):
        return call_once(
            outputs_body,
            place,
            local,
            [down_of(j, which) for which in range(3)]
            + [unit_of(array, j) for array in (hid, hid_lo, hid_hi)],
            [(blocks, kind, one, every)],
            16,
        )[0]

    def added(own, got):
        pairs_at = lambda i, p: (i, 0, 0)
        two = (2, feat, tokens)
        return call(
            add_body,
            place,
            (local // 2,),
            [(own, two, pairs_at), (got, two, pairs_at)],
            [(blocks, BF16, two, pairs_at)],
            20,
        )[0]

    shard = (2, 2, local, part, feat)
    strip_d = (1, part, feat)
    give_own, give_near, keep_d = call_once(
        down_terms_body,
        place,
        local,
        [(cot, one, every), (cot_lo, one, low), (cot_hi, one, high)]
        + [unit_of(hid, 1)]
        + [unit_of(array, j) for j in (0, 1) for array in (hid_lo, hid_hi)],
        [
            (shard[2:], BF16, strip_d, every),
            (shard[1:], BF16, (2,) + strip_d, lambda i, p: (0, i, 0, 0)),
            ((3,) + shard[2:], BF16, (3,) + strip_d, lambda i, p: (0, i, 0, 0)),
        ],
        16,
        scratch=[pltpu.VMEM((3, 2, part, feat), BF16)],
    )
    core_own, core_near = send_core(give_own), send_core(give_near)
    hid_b = after((hid,), give_own)[0]
    near_out = outputs_of(1, hid_b, BF16)
    got_out = send(near_out, 1)
    core_own, core_near = after((core_own, core_near), near_out)
    parts_d = (keep_e, first_got, keep_d, core_own, core_near)
    far_d, near_d, mine_d = call(
        down_meet_body,
        place,
        (1,),
        [whole(v) for v in parts_d],
        [whole_out(shard[2:], BF16)] * 2 + [whole_out(shard[1:], F32)],
        16,
    )
    got_far = send_z(far_d, 1)
    cot_b, *near_b = after((cot, cot_lo, cot_hi), far_d)
    late = [(1, 0, gate), (1, 1, gate_lo), (1, 2, gate_hi), (0, 2, gate_hi)]
    at_lo = lambda i, p: (0, least(i, half - 1), 0, 0)
    at_hi = lambda i, p: (0, most(i - half, 0), 0, 0)
    turn = lambda spec: (spec[0], spec[1], lambda i, p: spec[2](i % local, p))
    near_up = lambda j: (weights, (1, 1, 1, feat, rows), lambda i, p: (0, j, i, 0, 0))
    slope_sn, slope_lo_n, slope_hi_n, slope_hi_s, near_grads = call_once(
        late_body,
        place,
        2 * local,
        [
            turn(spec)
            for spec in [(cot_b, one, every), (near_b[0], one, low), (near_b[1], one, high)]
            + [down_of(j, which) for j, which, _ in late]
            + [unit_of(array, j) for j, _, array in late]
            + [near_up(0), near_up(1)]
        ]
        + [whole(slope_lo_s)],
        [whole_out(array.shape[1:], BF16) for _, _, array in late]
        + [(blocks, BF16, one, lambda i, p: (i % local, 0, 0))],
        20,
    )
    got_grads = send(near_grads, 2)

    x_b = after((x,), near_grads)[0]
    give_lo, give_hi, keep_u = up_terms(
        up_terms_body,
        [(x_b, one, every), (x_lo, one, low), (x_hi, one, high), (slope_sn, strip, at_i)]
        + [(slope_lo_s, strip, at_lo), (slope_lo_n, strip, at_lo)]
        + [(slope_hi_s, strip, at_hi), (slope_hi_n, strip, at_hi)],
        3,
        [lambda i: least(i, half - 1), lambda i: most(i - half, 0)],
        16.0,
    )
    give_lo, give_hi = after((give_lo, give_hi), got_far)
    gots_u = [send_core(give_lo), send_core(give_hi)]
    send_u, far_u, mine_u = up_meet(3, keep_u, gots_u)
    far_u = send_z(far_u, 1)

    got_far = after((got_far,), send_u)[0]
    send_d = up_again(mine_d, got_far)
    last_d = send_z(send_d, 2)
    got_near_d = send_z(after((near_d,), send_d)[0], 1)

    up_b = after((up_blocks,), send_d)[0]
    own_grads = call_once(
        grads_body,
        place,
        local,
        [
            (up_b, (1, feat, rows), lambda i, p: (i, 0, p[0])),
            (up_b, (1, feat, rows), lambda i, p: (i, 0, p[0] ^ 1)),
            (slope_ss, strip, at_i),
            (slope_sn, strip, at_i),
        ],
        [(blocks, F32, one, every)],
        16,
        span=4.0,
    )[0]

    own_out = outputs_of(0, after((hid,), own_grads)[0], F32)
    far_u = after((far_u,), own_out)[0]
    next_u = up_again(mine_u, far_u)
    last_u = send_z(next_u, 2)
    got_u = send_z(after((send_u,), next_u)[0], 1)

    last_d, got_near_d = after((last_d, got_near_d), next_u)
    sum_d = call(
        functools.partial(down_sum_body, factor),
        place,
        (1,),
        [whole(v) for v in (mine_d, got_near_d, last_d)],
        [whole_out(shard[2:], BF16)],
        8,
    )[0]
    swaps = []
    for device in range(n_dp * n_tensor):
        dp, t = device // n_tensor, device % n_tensor
        z_low, x_at = dp // 2 % 2, t % 2
        home = (dp // 4 * 4 + x_at * 2 + dp % 2) * n_tensor + t // 2 * 2 + z_low
        swaps.append((device, home))
    home_d = lax.ppermute(sum_d, ("dp", "tensor"), swaps)

    got_out = after((got_out,), sum_d)[0]
    outputs = added(own_out, got_out)

    got_u, last_u = after((got_u, last_u), outputs)
    send_u, mine_u = call(
        functools.partial(up_sum_body, factor),
        place,
        (1,),
        [whole(v) for v in (mine_e, got_e, last_e, mine_u, got_u, last_u)],
        [whole_out((2,) + shard_u[1:], BF16), whole_out((2,) + shard_u[1:], F32)],
        8,
    )
    got_u = send(send_u, 2)

    home_d = after((home_d,), send_u)[0]
    held, down_grads = call(
        place_own_body,
        place,
        (1,),
        [whole(mine_u), whole(home_d)],
        [
            whole_out((local, feat // n_dp, block_hidden), F32),
            whole_out((local, part, feat), F32),
        ],
        8,
    )
    got_grads = after((got_grads,), held)[0]
    feature_grads = added(own_grads, got_grads)

    got_u = after((got_u,), feature_grads)[0]
    up_grads = call(
        place_near_body,
        place,
        (2,),
        [
            (got_u, (1,) + shard_u[1:], lambda a, p: (a, 0, 0)),
            (held, None, None),
        ],
        [
            (
                (local, feat // n_dp, block_hidden),
                F32,
                (local, feat // n_dp, rows),
                lambda a, p: (0, 0, p[0] ^ 2 ^ a),
            )
        ],
        8,
        alias={2: 0},
    )[0]
    wide = (local * feat, tokens)
    return (outputs.reshape(wide), feature_grads.reshape(wide), up_grads, down_grads)


def solution(mesh):
    in_specs = (
        P("tensor", "dp"),
        P("tensor", "dp"),
        P("tensor", None, None),
        P("tensor", None, None),
    )
    out_specs = (
        P("tensor", "dp"),
        P("tensor", "dp"),
        P("tensor", "dp", None),
        P("tensor", "dp", None),
    )
    small = mesh.shape["tensor"] == 4 and mesh.shape["dp"] == 8
    return jax.shard_map(
        square_device if small else generic_device,
        mesh=mesh,
        in_specs=in_specs,
        out_specs=out_specs,
        check_vma=False,
    )
```

```python
import functools
import math

import jax
import jax.numpy as jnp
from jax import lax
from jax.experimental import pallas as pl
from jax.experimental.pallas import tpu as pltpu
from jax.sharding import PartitionSpec as P

BF16 = jnp.bfloat16
F32 = jnp.float32
INV_ROOT2 = 0.7071067811865476
INV_ROOT2PI = 0.3989422804014327
MIB = 1024 * 1024


def gelu_value(value):
    return 0.5 * value * (1.0 + lax.erf(value * INV_ROOT2))


def gelu_slope(value):
    return (
        0.5 * (1.0 + lax.erf(value * INV_ROOT2))
        + value * jnp.exp(-0.5 * value * value) * INV_ROOT2PI
    )


def generic_device(features, cotangent, up_blocks, down_blocks):
    local_blocks, block_feat, block_hidden = up_blocks.shape
    blocks = local_blocks * lax.axis_size("tensor")
    sub = block_hidden // blocks
    tokens_here = features.shape[1]
    factor = 1.0 / math.sqrt(tokens_here * lax.axis_size("dp"))
    x_local = features.reshape(local_blocks, block_feat, tokens_here)
    dy_local = cotangent.reshape(local_blocks, block_feat, tokens_here)
    down_four = down_blocks.reshape(local_blocks, blocks, sub, block_feat)
    preact = jnp.einsum("bdn,bdf->bfn", x_local, up_blocks, preferred_element_type=F32)
    pre_wide = preact.astype(BF16).astype(F32)
    hidden = gelu_value(pre_wide).astype(BF16).reshape(local_blocks, blocks, sub, tokens_here)
    mixed = lax.all_to_all(hidden, "tensor", split_axis=1, concat_axis=0, tiled=True)
    out_three = jnp.einsum("ijsn,jise->jen", mixed, down_four, preferred_element_type=F32)
    outputs = out_three.astype(BF16).reshape(local_blocks * block_feat, tokens_here)
    down_term = jnp.einsum("ijsn,jen->isje", mixed, dy_local, preferred_element_type=F32)
    down_term = down_term.reshape(block_hidden, local_blocks, block_feat)
    back = jnp.einsum("jen,jise->ijsn", dy_local, down_four, preferred_element_type=F32)
    back_home = lax.all_to_all(
        back.astype(BF16), "tensor", split_axis=0, concat_axis=1, tiled=True
    ).reshape(local_blocks, block_hidden, tokens_here)
    slope = (back_home.astype(F32) * gelu_slope(pre_wide)).astype(BF16)
    up_term = jnp.einsum("bdn,bfn->dbf", x_local, slope, preferred_element_type=F32)
    up_share = lax.psum_scatter(up_term, "dp", scatter_dimension=0, tiled=True)
    down_share = lax.psum_scatter(down_term, "dp", scatter_dimension=0, tiled=True)
    dx_three = jnp.einsum("bfn,bdf->bdn", slope, up_blocks, preferred_element_type=F32)
    feature_grads = dx_three.astype(BF16).reshape(local_blocks * block_feat, tokens_here)
    up_grads = jnp.transpose(up_share, (1, 0, 2)) * factor
    down_grads = jnp.transpose(down_share, (1, 0, 2)) * factor
    return (outputs, feature_grads, up_grads, down_grads)


def dot_tn(a, b):
    return lax.dot_general(a, b, (((0,), (0,)), ((), ())), preferred_element_type=F32)


def dot_nn(a, b):
    return lax.dot_general(a, b, (((1,), (0,)), ((), ())), preferred_element_type=F32)


def dot_nt(a, b):
    return lax.dot_general(a, b, (((1,), (1,)), ((), ())), preferred_element_type=F32)


def call(body, place, grid, ins, outs, mib, scratch=(), span=0.0, alias=None):
    return pl.pallas_call(
        body,
        grid_spec=pltpu.PrefetchScalarGridSpec(
            num_scalar_prefetch=1,
            grid=grid,
            in_specs=[
                pl.BlockSpec(b, m) if b else pl.BlockSpec(memory_space=pl.ANY) for _, b, m in ins
            ],
            out_specs=[pl.BlockSpec(b, m) for _, _, b, m in outs],
            scratch_shapes=list(scratch),
        ),
        out_shape=[jax.ShapeDtypeStruct(s, d) for s, d, _, _ in outs],
        input_output_aliases=alias or {},
        compiler_params=pltpu.CompilerParams(vmem_limit_bytes=mib * MIB),
        cost_estimate=pl.CostEstimate(
            flops=int(span * 1e9), bytes_accessed=0, transcendentals=0
        ),
    )(place, *[a for a, _, _ in ins])


def block_of(ref, block, where):
    at = []
    for size, extent, index in zip(block, ref.shape, where):
        if size == extent:
            at.append(slice(None))
        elif isinstance(index, int):
            at.append(slice(index * size, (index + 1) * size))
        else:
            at.append(pl.ds(pl.multiple_of(index * size, size), size))
    return ref.at[tuple(at)]


def call_once(body, place, steps, ins, outs, mib, scratch=(), span=0.0):
    def every_step(place, *refs):
        blocks = [(b, m) for _, b, m in ins] + [(b, m) for _, _, b, m in outs]
        held, rest = refs[: len(blocks)], refs[len(blocks) :]
        for step in range(steps):
            views = [block_of(ref, b, m(step, place)) for ref, (b, m) in zip(held, blocks)]
            body(step, steps, place, *views, *rest)

    return call(
        every_step,
        place,
        (1,),
        [whole(a) for a, _, _ in ins],
        [whole_out(s, d) for s, d, _, _ in outs],
        mib,
        scratch=scratch,
        span=span,
    )


def by_grid(body):
    return lambda place, *refs: body(pl.program_id(0), pl.num_programs(0), place, *refs)


def whole(array):
    rank = array.ndim
    return (array, array.shape, lambda *at: (0,) * rank)


def whole_out(shape, kind):
    rank = len(shape)
    return (shape, kind, shape, lambda *at: (0,) * rank)


def after(values, *earlier):
    return lax.optimization_barrier((tuple(values), earlier))[0]


def square(ref):
    block = ref[...]
    width = block.shape[-1]
    return block.reshape(block.size // width, width)


def hidden_body(place, x_ref, up_ref, hidden_ref, gate_ref):
    pre = dot_tn(square(up_ref), square(x_ref)).astype(BF16).astype(F32)
    half_cdf = 0.5 + 0.5 * lax.erf(pre * INV_ROOT2)
    gate = half_cdf + pre * jnp.exp(-0.5 * pre * pre) * INV_ROOT2PI
    hidden_ref[...] = (pre * half_cdf).astype(BF16).reshape(hidden_ref.shape)
    gate_ref[...] = gate.astype(BF16).reshape(gate_ref.shape)


def weights_body(place, *refs):
    low, core, out_ref = place[1] % 2, place[2], refs[-1]
    for at in range(2):
        out_ref[:, :, :, core * 2 + (low ^ at)] = refs[at][...]
        out_ref[:, :, :, (1 - core) * 2 + (low ^ at)] = refs[2 + at][...]


def halves(step, steps, work, lo, hi):
    if isinstance(step, int):
        work(*(lo if step < steps // 2 else hi))
        return
    pl.when(step < steps // 2)(functools.partial(work, *lo))
    pl.when(step >= steps // 2)(functools.partial(work, *hi))


def stacked(refs, axis=0):
    return jnp.concatenate([square(ref) for ref in refs], axis)


def put_slopes(cot, downs, gates, slopes):
    back = dot_nn(stacked(downs), cot).astype(BF16)
    base = 0
    for gate_ref, slope_ref in zip(gates, slopes):
        gate = square(gate_ref).astype(F32)
        mine = back[base : base + gate.shape[0]].astype(F32)
        slope_ref[...] = (mine * gate).astype(BF16).reshape(slope_ref.shape)
        base += gate.shape[0]


def slope_body(step, steps, place, cot_ref, down_ref, gate_ref, slope_ref):
    put_slopes(square(cot_ref), [down_ref], [gate_ref], [slope_ref])


def late_body(step, steps, place, own_ref, near_lo, near_hi, *refs):
    downs, gates, (up_own, up_near, lo_s), slopes, out_ref = (
        refs[:4],
        refs[4:8],
        refs[8:11],
        refs[11:15],
        refs[15],
    )
    count = steps // 2
    if step < count:
        here = [ref.at[step] for ref in slopes]
        put_slopes(square(own_ref), downs[3:], gates[3:], here[3:])
        near_ref = near_lo if step < count // 2 else near_hi
        put_slopes(square(near_ref), downs[:3], gates[:3], here[:3])
        return
    sn, lo_n, hi_n, hi_s = slopes
    pair = (lo_s, lo_n) if step - count < count // 2 else (hi_s, hi_n)
    strips = [ref.at[:, (step - count) % (count // 2)] for ref in pair]
    out_ref[0] = dot_nn(stacked((up_own, up_near), 1), stacked(strips)).astype(BF16)


def own_terms_body(step, steps, place, cot_ref, hid_ref, x_ref, slope_ref, give_ref, keep_ref, down_s, up_s):
    core = place[2]
    up_s[...] = dot_nt(square(x_ref), square(slope_ref)).astype(BF16).reshape(up_s.shape)
    count = up_s.shape[2]
    strip = slice(step * count, (step + 1) * count)
    give_ref[0, :, strip] = up_s[:, 1 - core]
    keep_ref[0, :, strip] = up_s[:, core]
    down_s[...] = dot_nt(square(hid_ref), square(cot_ref)).astype(BF16).reshape(down_s.shape)
    give_ref[1, step] = down_s[1 - core]
    keep_ref[1, step] = down_s[core]


def down_terms_body(step, steps, place, own_ref, near_lo, near_hi, sn, ns_lo, ns_hi, nn_lo, nn_hi, give_own, give_near, keep_ref, term_s):
    core = place[2]

    def put(pair, terms, give):
        term_s[pair] = terms.astype(BF16).reshape(term_s.shape[1:])
        give[...] = term_s[pair, 1 - core].reshape(give.shape)
        keep_ref[pair, 0] = term_s[pair, core]

    def work(near_ref):
        rows = 2 * term_s.shape[2]
        mixed = dot_nt(stacked((sn, nn_lo, nn_hi)), square(near_ref))
        put(0, mixed[:rows], give_own)
        put(1, dot_nt(stacked((ns_lo, ns_hi)), square(own_ref)), give_near.at[0])
        put(2, mixed[rows:], give_near.at[1])

    halves(step, steps, work, (near_lo,), (near_hi,))


def put_up_term(pair, core, x, slope_ref, give_ref, keep_ref, term_s):
    term_s[...] = dot_nt(x, square(slope_ref)).astype(BF16).reshape(term_s.shape)
    give_ref[pair] = term_s[:, 1 - core]
    keep_ref[pair] = term_s[:, core]


def up_terms_body(step, steps, place, x_ref, x_lo, x_hi, sn, lo_s, lo_n, hi_s, hi_n, give_lo, give_hi, keep_ref, term_s):
    def work(x_near, from_own, from_near, give_ref):
        near = square(x_near)
        for pair, (x, ref) in enumerate(((square(x_ref), sn), (near, from_own), (near, from_near))):
            put_up_term(pair, place[2], x, ref, give_ref, keep_ref, term_s)

    lo, hi = (x_lo, lo_s, lo_n, give_lo), (x_hi, hi_s, hi_n, give_hi)
    halves(step, steps, work, lo, hi)


def outputs_body(step, steps, place, d_own, d_lo, d_hi, hid_ref, lo_ref, hi_ref, out_ref):
    total = dot_tn(stacked((d_own, d_lo, d_hi)), stacked((hid_ref, lo_ref, hi_ref)))
    out_ref[0] = total.astype(out_ref.dtype)


def grads_body(step, steps, place, up_own, up_near, slope_own, slope_near, out_ref):
    out_ref[0] = dot_nn(stacked((up_own, up_near), 1), stacked((slope_own, slope_near)))


def add_body(place, own_ref, got_ref, out_ref):
    out_ref[...] = (own_ref[...] + got_ref[...].astype(F32)).astype(BF16)


def down_meet_body(place, first, first_got, keep_ref, got_own, got_near, send_ref, mine_ref):
    stay = (place[0] ^ place[1]) & 1
    kept = ((first.at[1], keep_ref.at[0]), (keep_ref.at[1], keep_ref.at[2]))
    got = ((first_got.at[1], got_own), (got_near.at[0], got_near.at[1]))
    for j in range(2):

        @pl.when(stay == j)
        def _():
            for i in range(2):
                total = lambda b: kept[i][b][...].astype(F32) + got[i][b][...].astype(F32)
                mine_ref[i] = total(j)
                send_ref[i] = total(1 - j).astype(BF16)


def down_again_body(place, mine_ref, got_ref, send_ref, own_ref):
    stay = (place[0] // 2) ^ (place[1] // 2)
    own_ref[...] = mine_ref[stay] + got_ref[stay].astype(F32)
    send_ref[...] = (mine_ref[1 - stay] + got_ref[1 - stay].astype(F32)).astype(BF16)


def down_sum_body(factor, place, own_ref, got_ref, out_ref):
    out_ref[...] = ((own_ref[...] + got_ref[...].astype(F32)) * factor).astype(BF16)


def up_meet_body(parts, place, keep_ref, *refs):
    gots, sends, mine_ref = refs[:parts], refs[parts:-1], refs[-1]
    rows = gots[0].shape[2]
    for hop in range(4):
        there = place[1] ^ hop
        for at, got_ref in enumerate(gots):
            strip = slice(at * rows, (at + 1) * rows)
            total = keep_ref[:, there, strip].astype(F32) + got_ref[:, there].astype(F32)
            if hop % 2:
                sends[hop // 2][:, strip] = total.astype(BF16)
            else:
                mine_ref[hop // 2, :, strip] = total


def up_again_body(place, mine_ref, far_ref, send_ref):
    send_ref[...] = (mine_ref[1] + far_ref[...].astype(F32)).astype(BF16)


def up_sum_body(factor, place, *refs):
    ins, (send_ref, mine_ref) = refs[:6], refs[6:]
    first, total = (
        (own[0] + near[...].astype(F32) + far[...].astype(F32)) * factor
        for own, near, far in (ins[:3], ins[3:])
    )
    mine_ref[0] = first[0]
    mine_ref[1] = total[0]
    send_ref[...] = total[1:].astype(BF16)


def place_own_body(place, mine_ref, down_in, up_ref, down_ref):
    down_ref[...] = down_in[...].astype(F32)
    width = mine_ref.shape[-1]
    for at in range(2):
        lanes = pl.ds(pl.multiple_of((place[0] ^ at) * width, width), width)
        up_ref[:, :, lanes] = mine_ref[at].reshape(*up_ref.shape[:2], width)


def place_near_body(place, got_ref, held_ref, up_ref):
    up_ref[...] = got_ref[0].astype(F32).reshape(up_ref.shape)


def square_device(features, cotangent, up_blocks, down_blocks):
    local, feat, block_hidden = up_blocks.shape
    tokens = features.shape[1]
    n_dp, n_tensor = lax.axis_size("dp"), lax.axis_size("tensor")
    sub = block_hidden // (local * n_tensor)
    rows = local * sub
    half, part = local // 2, rows // 2
    factor = 1.0 / math.sqrt(tokens * n_dp)
    me = lax.axis_index("tensor").astype(jnp.int32)
    rank = lax.axis_index("dp").astype(jnp.int32)
    z, core = rank >> 1, rank & 1
    place = jnp.stack([me, z, core])
    x = features.reshape(local, feat, tokens)
    cot = cotangent.reshape(local, feat, tokens)
    one = (1, feat, tokens)
    blocks = (local, feat, tokens)
    every = lambda i, p: (i, 0, 0)
    least = lambda a, b: min(a, b) if isinstance(a, int) else jnp.minimum(a, b)
    most = lambda a, b: max(a, b) if isinstance(a, int) else jnp.maximum(a, b)
    low = lambda i, p: (least(i, half - 1), 0, 0)
    high = lambda i, p: (most(i - half, 0), 0, 0)

    def send(value, hop):
        return lax.ppermute(value, "tensor", [(t, t ^ hop) for t in range(n_tensor)])

    def send_z(value, hop):
        return lax.ppermute(value, "dp", [(d, d ^ (2 * hop)) for d in range(n_dp)])

    def send_core(value):
        return lax.ppermute(value, "dp", [(d, d ^ 1) for d in range(n_dp)])

    quarter = rows // 4
    at = (core * 2 + (z & 1)) * quarter
    to_i = jnp.stack(
        [
            lax.dynamic_slice(up_blocks, (0, at, (me ^ k) * rows), (local, quarter, rows))
            for k in (2, 3)
        ]
    )
    down_b = after((down_blocks,), to_i)[0]
    to_j = jnp.stack(
        [
            lax.dynamic_slice(down_b, (0, (me ^ k) * rows + at, 0), (local, quarter, feat))
            for k in (1, 3)
        ]
    )
    from_i, from_j = send(to_i, 2), send(to_j, 1)
    firsts = after((x[:half], x[half:], cot[:half], cot[half:]), to_i, to_j)
    x_lo, cot_lo = send(firsts[0], 2), send(firsts[2], 1)
    x_hi, cot_hi = send(firsts[1], 2), send(firsts[3], 1)

    def hidden_of(source, count, up, span):
        unit = (2, local, count, sub, tokens)
        block = (1, local, 1, sub, tokens)
        where = lambda j, i, p: (j, 0, i, 0, 0)
        return call(
            hidden_body,
            place,
            (2, count),
            [(source, one, lambda j, i, p: (i, 0, 0)), up],
            [(unit, BF16, block, where), (unit, BF16, block, where)],
            16,
        )

    hid, gate = hidden_of(
        x, local, (up_blocks, (1, feat, rows), lambda j, i, p: (i, 0, p[0] ^ j)), 0.0
    )
    from_i, from_j = after((from_i, from_j), hid)
    share = jnp.stack([from_i, from_j])
    share_z = send_z(share, 1)

    def unit_of(array, j):
        return (array, (1, 1) + array.shape[2:], lambda i, p: (j, i, 0, 0, 0))

    def down_of(j, which):
        if j == 0:
            if which == 0:
                return (down_blocks, (1, rows, feat), lambda i, p: (i, p[0], 0))
            return (
                down_blocks,
                (1, part, feat),
                lambda i, p: (i, 2 * (p[0] ^ 2) + which - 1, 0),
            )
        if which == 0:
            return (weights, (1, 1, 1, rows, feat), lambda i, p: (1, 0, i, 0, 0))
        return (weights, (1, 1, 1, part, feat), lambda i, p: (1, 1, i, which - 1, 0))

    def own_slope(which, array):
        return call_once(
            slope_body,
            place,
            local,
            [(cot, one, every), down_of(0, which), unit_of(array, 0)],
            [(array.shape[1:], BF16, (1,) + array.shape[2:], lambda i, p: (i, 0, 0, 0))],
            20,
        )[0]

    slope_ss = own_slope(0, gate)
    at_i = lambda i, p: (0, i, 0, 0)
    strip = (local, 1, sub, tokens)
    shard_u = (n_dp // 2, local * feat // n_dp, rows)

    def up_terms(body, ins, count, gives, span):
        block = (count, n_dp // 2, feat // n_dp, rows)
        wide = (count,) + shard_u
        part_u = (count, n_dp // 2, shard_u[1] // len(gives), rows)
        return call_once(
            body,
            place,
            local,
            ins,
            [
                (part_u, BF16, block, functools.partial(lambda m, i, p: (0, 0, m(i), 0), m))
                for m in gives
            ]
            + [(wide, BF16, block, lambda i, p: (0, 0, i, 0))],
            20,
            scratch=[pltpu.VMEM((n_dp // 2, 2, feat // n_dp, rows), BF16)],
            span=span,
        )

    def up_meet(count, keep, gots):
        piece = (count,) + shard_u[1:]
        return call(
            functools.partial(up_meet_body, len(gots)),
            place,
            (1,),
            [(v, (count,) + v.shape[1:], lambda i, p: (0, 0, 0, 0)) for v in (keep, *gots)],
            [whole_out(piece, BF16)] * 2 + [whole_out((2,) + piece, F32)],
            16,
        )

    def up_again(mine, far):
        piece = mine.shape[1:]
        return call(
            up_again_body, place, (1,), [whole(mine), whole(far)], [whole_out(piece, BF16)], 16
        )[0]

    give_e, keep_e = call_once(
        own_terms_body,
        place,
        local,
        [
            (cot, one, every),
            unit_of(hid, 0),
            (x, one, every),
            (slope_ss, strip, at_i),
        ],
        [whole_out((2,) + shard_u, BF16)] * 2,
        20,
        scratch=[
            pltpu.VMEM((2, part, feat), BF16),
            pltpu.VMEM((n_dp // 2, 2, feat // n_dp, rows), BF16),
        ],
    )
    share, share_z, x_lo, cot_lo = after((share, share_z, x_lo, cot_lo), give_e)
    core_parts = after((share, share_z), x_lo, cot_lo)
    weights = call(
        weights_body,
        place,
        (1,),
        [whole(v) for v in (share, share_z, *map(send_core, core_parts))],
        [whole_out((2, 2, local, 4, quarter, feat), BF16)],
        16,
    )[0].reshape(2, 2, local, rows, feat)

    def near_hidden(source, which):
        up = (
            weights,
            (1, 1, 1, feat, rows),
            lambda j, i, p: (0, j, which * half + i, 0, 0),
        )
        return hidden_of(source, half, up, 0.0)

    give_e = after((give_e,), x_lo, cot_lo)[0]
    first_got = send_core(give_e)
    send_e, far_e, mine_e = up_meet(1, keep_e, [first_got])
    got_e, far_e = send_z(send_e, 1), send_z(far_e, 1)
    x_lo = after((x_lo,), weights, send_e)[0]
    hid_lo, gate_lo = near_hidden(x_lo, 0)
    slope_lo_s = own_slope(1, gate_lo)

    got_e, far_e = after((got_e, far_e), slope_lo_s)
    send_e = up_again(mine_e, far_e)
    last_e = send_z(send_e, 2)

    x_hi = after((x_hi,), send_e)[0]
    hid_hi, gate_hi = near_hidden(x_hi, 1)
    cot_hi, last_e = after((cot_hi, last_e), hid_hi)

    def outputs_of(j, hid, kind):
        return call_once(
            outputs_body,
            place,
            local,
            [down_of(j, which) for which in range(3)]
            + [unit_of(array, j) for array in (hid, hid_lo, hid_hi)],
            [(blocks, kind, one, every)],
            16,
        )[0]

    def added(own, got):
        pairs_at = lambda i, p: (i, 0, 0)
        two = (2, feat, tokens)
        return call(
            add_body,
            place,
            (local // 2,),
            [(own, two, pairs_at), (got, two, pairs_at)],
            [(blocks, BF16, two, pairs_at)],
            20,
        )[0]

    shard = (2, 2, local, part, feat)
    strip_d = (1, part, feat)
    give_own, give_near, keep_d = call_once(
        down_terms_body,
        place,
        local,
        [(cot, one, every), (cot_lo, one, low), (cot_hi, one, high)]
        + [unit_of(hid, 1)]
        + [unit_of(array, j) for j in (0, 1) for array in (hid_lo, hid_hi)],
        [
            (shard[2:], BF16, strip_d, every),
            (shard[1:], BF16, (2,) + strip_d, lambda i, p: (0, i, 0, 0)),
            ((3,) + shard[2:], BF16, (3,) + strip_d, lambda i, p: (0, i, 0, 0)),
        ],
        16,
        scratch=[pltpu.VMEM((3, 2, part, feat), BF16)],
    )
    core_own, core_near = send_core(give_own), send_core(give_near)
    hid_b = after((hid,), give_own)[0]
    near_out = outputs_of(1, hid_b, BF16)
    got_out = send(near_out, 1)
    core_own, core_near = after((core_own, core_near), near_out)
    parts_d = (keep_e, first_got, keep_d, core_own, core_near)
    send_d, mine_d = call(
        down_meet_body,
        place,
        (1,),
        [whole(v) for v in parts_d],
        [whole_out(shard[1:], BF16), whole_out(shard[1:], F32)],
        16,
    )
    got_d = send_z(send_d, 1)
    cot_b, *near_b = after((cot, cot_lo, cot_hi), send_d)
    late = [(1, 0, gate), (1, 1, gate_lo), (1, 2, gate_hi), (0, 2, gate_hi)]
    at_lo = lambda i, p: (0, least(i, half - 1), 0, 0)
    at_hi = lambda i, p: (0, most(i - half, 0), 0, 0)
    turn = lambda spec: (spec[0], spec[1], lambda i, p: spec[2](i % local, p))
    near_up = lambda j: (weights, (1, 1, 1, feat, rows), lambda i, p: (0, j, i, 0, 0))
    slope_sn, slope_lo_n, slope_hi_n, slope_hi_s, near_grads = call_once(
        late_body,
        place,
        2 * local,
        [
            turn(spec)
            for spec in [(cot_b, one, every), (near_b[0], one, low), (near_b[1], one, high)]
            + [down_of(j, which) for j, which, _ in late]
            + [unit_of(array, j) for j, _, array in late]
            + [near_up(0), near_up(1)]
        ]
        + [whole(slope_lo_s)],
        [whole_out(array.shape[1:], BF16) for _, _, array in late]
        + [(blocks, BF16, one, lambda i, p: (i % local, 0, 0))],
        20,
    )
    got_grads = send(near_grads, 2)

    x_b = after((x,), near_grads)[0]
    give_lo, give_hi, keep_u = up_terms(
        up_terms_body,
        [(x_b, one, every), (x_lo, one, low), (x_hi, one, high), (slope_sn, strip, at_i)]
        + [(slope_lo_s, strip, at_lo), (slope_lo_n, strip, at_lo)]
        + [(slope_hi_s, strip, at_hi), (slope_hi_n, strip, at_hi)],
        3,
        [lambda i: least(i, half - 1), lambda i: most(i - half, 0)],
        16.0,
    )
    send_u, far_u, mine_u = up_meet(3, keep_u, [send_core(give_lo), send_core(give_hi)])
    got_u, far_u = send_z(send_u, 1), send_z(far_u, 1)

    got_d = after((got_d,), send_u)[0]
    send_d, mine_d = call(
        down_again_body,
        place,
        (1,),
        [whole(mine_d), whole(got_d)],
        [whole_out(shard[2:], BF16), whole_out(shard[2:], F32)],
        16,
    )
    got_d = send_z(send_d, 2)

    up_b = after((up_blocks,), send_d)[0]
    own_grads = call_once(
        grads_body,
        place,
        local,
        [
            (up_b, (1, feat, rows), lambda i, p: (i, 0, p[0])),
            (up_b, (1, feat, rows), lambda i, p: (i, 0, p[0] ^ 1)),
            (slope_ss, strip, at_i),
            (slope_sn, strip, at_i),
        ],
        [(blocks, F32, one, every)],
        16,
        span=4.0,
    )[0]

    own_out = outputs_of(0, after((hid,), own_grads)[0], F32)
    far_u = after((far_u,), own_out)[0]
    send_u = up_again(mine_u, far_u)
    last_u = send_z(send_u, 2)

    got_d = after((got_d,), send_u)[0]
    sum_d = call(
        functools.partial(down_sum_body, factor),
        place,
        (1,),
        [whole(mine_d), whole(got_d)],
        [whole_out(shard[2:], BF16)],
        8,
    )[0]
    swaps = []
    for device in range(n_dp * n_tensor):
        dp, t = device // n_tensor, device % n_tensor
        z_low, x_at = dp // 2 % 2, t % 2
        home = (dp // 4 * 4 + x_at * 2 + dp % 2) * n_tensor + t // 2 * 2 + z_low
        swaps.append((device, home))
    home_d = lax.ppermute(sum_d, ("dp", "tensor"), swaps)

    got_out = after((got_out,), sum_d)[0]
    outputs = added(own_out, got_out)

    got_u, last_u = after((got_u, last_u), outputs)
    send_u, mine_u = call(
        functools.partial(up_sum_body, factor),
        place,
        (1,),
        [whole(v) for v in (mine_e, got_e, last_e, mine_u, got_u, last_u)],
        [whole_out((2,) + shard_u[1:], BF16), whole_out((2,) + shard_u[1:], F32)],
        8,
    )
    got_u = send(send_u, 2)

    home_d = after((home_d,), send_u)[0]
    held, down_grads = call(
        place_own_body,
        place,
        (1,),
        [whole(mine_u), whole(home_d)],
        [
            whole_out((local, feat // n_dp, block_hidden), F32),
            whole_out((local, part, feat), F32),
        ],
        8,
    )
    got_grads = after((got_grads,), held)[0]
    feature_grads = added(own_grads, got_grads)

    got_u = after((got_u,), feature_grads)[0]
    up_grads = call(
        place_near_body,
        place,
        (2,),
        [
            (got_u, (1,) + shard_u[1:], lambda a, p: (a, 0, 0)),
            (held, None, None),
        ],
        [
            (
                (local, feat // n_dp, block_hidden),
                F32,
                (local, feat // n_dp, rows),
                lambda a, p: (0, 0, p[0] ^ 2 ^ a),
            )
        ],
        8,
        alias={2: 0},
    )[0]
    wide = (local * feat, tokens)
    return (outputs.reshape(wide), feature_grads.reshape(wide), up_grads, down_grads)


def solution(mesh):
    in_specs = (
        P("tensor", "dp"),
        P("tensor", "dp"),
        P("tensor", None, None),
        P("tensor", None, None),
    )
    out_specs = (
        P("tensor", "dp"),
        P("tensor", "dp"),
        P("tensor", "dp", None),
        P("tensor", "dp", None),
    )
    small = mesh.shape["tensor"] == 4 and mesh.shape["dp"] == 8
    return jax.shard_map(
        square_device if small else generic_device,
        mesh=mesh,
        in_specs=in_specs,
        out_specs=out_specs,
        check_vma=False,
    )
```

```python
import functools
import math

import jax
import jax.numpy as jnp
from jax import lax
from jax.experimental import pallas as pl
from jax.experimental.pallas import tpu as pltpu
from jax.sharding import PartitionSpec as P

BF16 = jnp.bfloat16
F32 = jnp.float32
INV_ROOT2 = 0.7071067811865476
INV_ROOT2PI = 0.3989422804014327
MIB = 1024 * 1024


def gelu_value(value):
    return 0.5 * value * (1.0 + lax.erf(value * INV_ROOT2))


def gelu_slope(value):
    return (
        0.5 * (1.0 + lax.erf(value * INV_ROOT2))
        + value * jnp.exp(-0.5 * value * value) * INV_ROOT2PI
    )


def generic_device(features, cotangent, up_blocks, down_blocks):
    local_blocks, block_feat, block_hidden = up_blocks.shape
    blocks = local_blocks * lax.axis_size("tensor")
    sub = block_hidden // blocks
    tokens_here = features.shape[1]
    factor = 1.0 / math.sqrt(tokens_here * lax.axis_size("dp"))
    x_local = features.reshape(local_blocks, block_feat, tokens_here)
    dy_local = cotangent.reshape(local_blocks, block_feat, tokens_here)
    down_four = down_blocks.reshape(local_blocks, blocks, sub, block_feat)
    preact = jnp.einsum("bdn,bdf->bfn", x_local, up_blocks, preferred_element_type=F32)
    pre_wide = preact.astype(BF16).astype(F32)
    hidden = gelu_value(pre_wide).astype(BF16).reshape(local_blocks, blocks, sub, tokens_here)
    mixed = lax.all_to_all(hidden, "tensor", split_axis=1, concat_axis=0, tiled=True)
    out_three = jnp.einsum("ijsn,jise->jen", mixed, down_four, preferred_element_type=F32)
    outputs = out_three.astype(BF16).reshape(local_blocks * block_feat, tokens_here)
    down_term = jnp.einsum("ijsn,jen->isje", mixed, dy_local, preferred_element_type=F32)
    down_term = down_term.reshape(block_hidden, local_blocks, block_feat)
    back = jnp.einsum("jen,jise->ijsn", dy_local, down_four, preferred_element_type=F32)
    back_home = lax.all_to_all(
        back.astype(BF16), "tensor", split_axis=0, concat_axis=1, tiled=True
    ).reshape(local_blocks, block_hidden, tokens_here)
    slope = (back_home.astype(F32) * gelu_slope(pre_wide)).astype(BF16)
    up_term = jnp.einsum("bdn,bfn->dbf", x_local, slope, preferred_element_type=F32)
    up_share = lax.psum_scatter(up_term, "dp", scatter_dimension=0, tiled=True)
    down_share = lax.psum_scatter(down_term, "dp", scatter_dimension=0, tiled=True)
    dx_three = jnp.einsum("bfn,bdf->bdn", slope, up_blocks, preferred_element_type=F32)
    feature_grads = dx_three.astype(BF16).reshape(local_blocks * block_feat, tokens_here)
    up_grads = jnp.transpose(up_share, (1, 0, 2)) * factor
    down_grads = jnp.transpose(down_share, (1, 0, 2)) * factor
    return (outputs, feature_grads, up_grads, down_grads)


def dot_tn(a, b):
    return lax.dot_general(a, b, (((0,), (0,)), ((), ())), preferred_element_type=F32)


def dot_nn(a, b):
    return lax.dot_general(a, b, (((1,), (0,)), ((), ())), preferred_element_type=F32)


def dot_nt(a, b):
    return lax.dot_general(a, b, (((1,), (1,)), ((), ())), preferred_element_type=F32)


def call(body, place, grid, ins, outs, mib, scratch=(), span=0.0, alias=None):
    return pl.pallas_call(
        body,
        grid_spec=pltpu.PrefetchScalarGridSpec(
            num_scalar_prefetch=1,
            grid=grid,
            in_specs=[
                pl.BlockSpec(b, m) if b else pl.BlockSpec(memory_space=pl.ANY) for _, b, m in ins
            ],
            out_specs=[pl.BlockSpec(b, m) for _, _, b, m in outs],
            scratch_shapes=list(scratch),
        ),
        out_shape=[jax.ShapeDtypeStruct(s, d) for s, d, _, _ in outs],
        input_output_aliases=alias or {},
        compiler_params=pltpu.CompilerParams(vmem_limit_bytes=mib * MIB),
        cost_estimate=pl.CostEstimate(
            flops=int(span * 1e9), bytes_accessed=0, transcendentals=0
        ),
    )(place, *[a for a, _, _ in ins])


def block_of(ref, block, where):
    at = []
    for size, extent, index in zip(block, ref.shape, where):
        if size == extent:
            at.append(slice(None))
        elif isinstance(index, int):
            at.append(slice(index * size, (index + 1) * size))
        else:
            at.append(pl.ds(pl.multiple_of(index * size, size), size))
    return ref.at[tuple(at)]


def call_once(body, place, steps, ins, outs, mib, scratch=(), span=0.0):
    def every_step(place, *refs):
        blocks = [(b, m) for _, b, m in ins] + [(b, m) for _, _, b, m in outs]
        held, rest = refs[: len(blocks)], refs[len(blocks) :]
        for step in range(steps):
            views = [block_of(ref, b, m(step, place)) for ref, (b, m) in zip(held, blocks)]
            body(step, steps, place, *views, *rest)

    return call(
        every_step,
        place,
        (1,),
        [whole(a) for a, _, _ in ins],
        [whole_out(s, d) for s, d, _, _ in outs],
        mib,
        scratch=scratch,
        span=span,
    )


def by_grid(body):
    return lambda place, *refs: body(pl.program_id(0), pl.num_programs(0), place, *refs)


def whole(array):
    rank = array.ndim
    return (array, array.shape, lambda *at: (0,) * rank)


def whole_out(shape, kind):
    rank = len(shape)
    return (shape, kind, shape, lambda *at: (0,) * rank)


def after(values, *earlier):
    return lax.optimization_barrier((tuple(values), earlier))[0]


def square(ref):
    block = ref[...]
    width = block.shape[-1]
    return block.reshape(block.size // width, width)


def hidden_body(place, x_ref, up_ref, hidden_ref, gate_ref):
    pre = dot_tn(square(up_ref), square(x_ref)).astype(BF16).astype(F32)
    half_cdf = 0.5 + 0.5 * lax.erf(pre * INV_ROOT2)
    gate = half_cdf + pre * jnp.exp(-0.5 * pre * pre) * INV_ROOT2PI
    hidden_ref[...] = (pre * half_cdf).astype(BF16).reshape(hidden_ref.shape)
    gate_ref[...] = gate.astype(BF16).reshape(gate_ref.shape)


def weights_body(place, *refs):
    low, core, out_ref = place[1] % 2, place[2], refs[-1]
    for at in range(2):
        out_ref[:, :, :, core * 2 + (low ^ at)] = refs[at][...]
        out_ref[:, :, :, (1 - core) * 2 + (low ^ at)] = refs[2 + at][...]


def halves(step, steps, work, lo, hi):
    if isinstance(step, int):
        work(*(lo if step < steps // 2 else hi))
        return
    pl.when(step < steps // 2)(functools.partial(work, *lo))
    pl.when(step >= steps // 2)(functools.partial(work, *hi))


def stacked(refs, axis=0):
    return jnp.concatenate([square(ref) for ref in refs], axis)


def put_slopes(cot, downs, gates, slopes):
    back = dot_nn(stacked(downs), cot).astype(BF16)
    base = 0
    for gate_ref, slope_ref in zip(gates, slopes):
        gate = square(gate_ref).astype(F32)
        mine = back[base : base + gate.shape[0]].astype(F32)
        slope_ref[...] = (mine * gate).astype(BF16).reshape(slope_ref.shape)
        base += gate.shape[0]


def slope_body(step, steps, place, cot_ref, down_ref, gate_ref, slope_ref):
    put_slopes(square(cot_ref), [down_ref], [gate_ref], [slope_ref])


def late_body(step, steps, place, own_ref, near_lo, near_hi, *refs):
    downs, gates, (up_own, up_near, lo_s), slopes, out_ref = (
        refs[:4],
        refs[4:8],
        refs[8:11],
        refs[11:15],
        refs[15],
    )
    count = steps // 2
    if step < count:
        here = [ref.at[step] for ref in slopes]
        put_slopes(square(own_ref), downs[3:], gates[3:], here[3:])
        near_ref = near_lo if step < count // 2 else near_hi
        put_slopes(square(near_ref), downs[:3], gates[:3], here[:3])
        return
    sn, lo_n, hi_n, hi_s = slopes
    pair = (lo_s, lo_n) if step - count < count // 2 else (hi_s, hi_n)
    strips = [ref.at[:, (step - count) % (count // 2)] for ref in pair]
    out_ref[0] = dot_nn(stacked((up_own, up_near), 1), stacked(strips)).astype(BF16)


def own_terms_body(step, steps, place, cot_ref, hid_ref, x_ref, slope_ref, give_ref, keep_ref, down_s, up_s):
    core = place[2]
    up_s[...] = dot_nt(square(x_ref), square(slope_ref)).astype(BF16).reshape(up_s.shape)
    count = up_s.shape[2]
    strip = slice(step * count, (step + 1) * count)
    give_ref[0, :, strip] = up_s[:, 1 - core]
    keep_ref[0, :, strip] = up_s[:, core]
    down_s[...] = dot_nt(square(hid_ref), square(cot_ref)).astype(BF16).reshape(down_s.shape)
    give_ref[1, step] = down_s[1 - core]
    keep_ref[1, step] = down_s[core]


def down_terms_body(step, steps, place, own_ref, near_lo, near_hi, sn, ns_lo, ns_hi, nn_lo, nn_hi, give_own, give_near, keep_ref, term_s):
    core = place[2]

    def put(pair, terms, give):
        term_s[pair] = terms.astype(BF16).reshape(term_s.shape[1:])
        give[...] = term_s[pair, 1 - core].reshape(give.shape)
        keep_ref[pair, 0] = term_s[pair, core]

    def work(near_ref):
        rows = 2 * term_s.shape[2]
        mixed = dot_nt(stacked((sn, nn_lo, nn_hi)), square(near_ref))
        put(0, mixed[:rows], give_own)
        put(1, dot_nt(stacked((ns_lo, ns_hi)), square(own_ref)), give_near.at[0])
        put(2, mixed[rows:], give_near.at[1])

    halves(step, steps, work, (near_lo,), (near_hi,))


def put_up_term(pair, core, x, slope_ref, give_ref, keep_ref, term_s):
    term_s[...] = dot_nt(x, square(slope_ref)).astype(BF16).reshape(term_s.shape)
    give_ref[pair] = term_s[:, 1 - core]
    keep_ref[pair] = term_s[:, core]


def up_terms_body(step, steps, place, x_ref, x_lo, x_hi, sn, lo_s, lo_n, hi_s, hi_n, give_lo, give_hi, keep_ref, term_s):
    def work(x_near, from_own, from_near, give_ref):
        near = square(x_near)
        for pair, (x, ref) in enumerate(((square(x_ref), sn), (near, from_own), (near, from_near))):
            put_up_term(pair, place[2], x, ref, give_ref, keep_ref, term_s)

    lo, hi = (x_lo, lo_s, lo_n, give_lo), (x_hi, hi_s, hi_n, give_hi)
    halves(step, steps, work, lo, hi)


def outputs_body(step, steps, place, d_own, d_lo, d_hi, hid_ref, lo_ref, hi_ref, out_ref):
    total = dot_tn(stacked((d_own, d_lo, d_hi)), stacked((hid_ref, lo_ref, hi_ref)))
    out_ref[0] = total.astype(out_ref.dtype)


def grads_body(step, steps, place, up_own, up_near, slope_own, slope_near, out_ref):
    out_ref[0] = dot_nn(stacked((up_own, up_near), 1), stacked((slope_own, slope_near)))


def add_body(place, own_ref, got_ref, out_ref):
    out_ref[...] = (own_ref[...] + got_ref[...].astype(F32)).astype(BF16)


def down_meet_body(place, first, first_got, keep_ref, got_own, got_near, send_ref, mine_ref):
    stay = (place[0] ^ place[1]) & 1
    kept = ((first.at[1], keep_ref.at[0]), (keep_ref.at[1], keep_ref.at[2]))
    got = ((first_got.at[1], got_own), (got_near.at[0], got_near.at[1]))
    for j in range(2):

        @pl.when(stay == j)
        def _():
            for i in range(2):
                total = lambda b: kept[i][b][...].astype(F32) + got[i][b][...].astype(F32)
                mine_ref[i] = total(j)
                send_ref[i] = total(1 - j).astype(BF16)


def down_again_body(place, mine_ref, got_ref, send_ref, own_ref):
    stay = (place[0] // 2) ^ (place[1] // 2)
    own_ref[...] = mine_ref[stay] + got_ref[stay].astype(F32)
    send_ref[...] = (mine_ref[1 - stay] + got_ref[1 - stay].astype(F32)).astype(BF16)


def down_sum_body(factor, place, own_ref, got_ref, out_ref):
    out_ref[...] = ((own_ref[...] + got_ref[...].astype(F32)) * factor).astype(BF16)


def up_meet_body(parts, place, keep_ref, *refs):
    gots, sends, mine_ref = refs[:parts], refs[parts:-1], refs[-1]
    rows = gots[0].shape[2]
    for hop in range(4):
        there = place[1] ^ hop
        for at, got_ref in enumerate(gots):
            strip = slice(at * rows, (at + 1) * rows)
            total = keep_ref[:, there, strip].astype(F32) + got_ref[:, there].astype(F32)
            if hop % 2:
                sends[hop // 2][:, strip] = total.astype(BF16)
            else:
                mine_ref[hop // 2, :, strip] = total


def up_again_body(place, mine_ref, far_ref, send_ref):
    send_ref[...] = (mine_ref[1] + far_ref[...].astype(F32)).astype(BF16)


def up_sum_body(factor, place, *refs):
    ins, (send_ref, up_ref) = refs[:6], refs[6:]
    first, total = (
        (own[0] + near[...].astype(F32) + far[...].astype(F32)) * factor
        for own, near, far in (ins[:3], ins[3:])
    )
    send_ref[...] = total[1:].astype(BF16)
    width = send_ref.shape[-1]
    for at, mine in enumerate((first[0], total[0])):
        lanes = pl.ds(pl.multiple_of((place[0] ^ at) * width, width), width)
        up_ref[:, :, lanes] = mine.reshape(*up_ref.shape[:2], width)


def place_near_body(place, got_ref, held_ref, up_ref):
    up_ref[...] = got_ref[0].astype(F32).reshape(up_ref.shape)


def square_device(features, cotangent, up_blocks, down_blocks):
    local, feat, block_hidden = up_blocks.shape
    tokens = features.shape[1]
    n_dp, n_tensor = lax.axis_size("dp"), lax.axis_size("tensor")
    sub = block_hidden // (local * n_tensor)
    rows = local * sub
    half, part = local // 2, rows // 2
    factor = 1.0 / math.sqrt(tokens * n_dp)
    me = lax.axis_index("tensor").astype(jnp.int32)
    rank = lax.axis_index("dp").astype(jnp.int32)
    z, core = rank >> 1, rank & 1
    place = jnp.stack([me, z, core])
    x = features.reshape(local, feat, tokens)
    cot = cotangent.reshape(local, feat, tokens)
    one = (1, feat, tokens)
    blocks = (local, feat, tokens)
    every = lambda i, p: (i, 0, 0)
    least = lambda a, b: min(a, b) if isinstance(a, int) else jnp.minimum(a, b)
    most = lambda a, b: max(a, b) if isinstance(a, int) else jnp.maximum(a, b)
    low = lambda i, p: (least(i, half - 1), 0, 0)
    high = lambda i, p: (most(i - half, 0), 0, 0)

    def send(value, hop):
        return lax.ppermute(value, "tensor", [(t, t ^ hop) for t in range(n_tensor)])

    def send_z(value, hop):
        return lax.ppermute(value, "dp", [(d, d ^ (2 * hop)) for d in range(n_dp)])

    def send_core(value):
        return lax.ppermute(value, "dp", [(d, d ^ 1) for d in range(n_dp)])

    quarter = rows // 4
    at = (core * 2 + (z & 1)) * quarter
    to_i = jnp.stack(
        [
            lax.dynamic_slice(up_blocks, (0, at, (me ^ k) * rows), (local, quarter, rows))
            for k in (2, 3)
        ]
    )
    down_b = after((down_blocks,), to_i)[0]
    to_j = jnp.stack(
        [
            lax.dynamic_slice(down_b, (0, (me ^ k) * rows + at, 0), (local, quarter, feat))
            for k in (1, 3)
        ]
    )
    from_i, from_j = send(to_i, 2), send(to_j, 1)
    firsts = after((x[:half], x[half:], cot[:half], cot[half:]), to_i, to_j)
    x_lo, cot_lo = send(firsts[0], 2), send(firsts[2], 1)
    x_hi, cot_hi = send(firsts[1], 2), send(firsts[3], 1)

    def hidden_of(source, count, up, span):
        unit = (2, local, count, sub, tokens)
        block = (1, local, 1, sub, tokens)
        where = lambda j, i, p: (j, 0, i, 0, 0)
        return call(
            hidden_body,
            place,
            (2, count),
            [(source, one, lambda j, i, p: (i, 0, 0)), up],
            [(unit, BF16, block, where), (unit, BF16, block, where)],
            16,
        )

    hid, gate = hidden_of(
        x, local, (up_blocks, (1, feat, rows), lambda j, i, p: (i, 0, p[0] ^ j)), 0.0
    )
    from_i, from_j = after((from_i, from_j), hid)
    share = jnp.stack([from_i, from_j])
    share_z = send_z(share, 1)

    def unit_of(array, j):
        return (array, (1, 1) + array.shape[2:], lambda i, p: (j, i, 0, 0, 0))

    def down_of(j, which):
        if j == 0:
            if which == 0:
                return (down_blocks, (1, rows, feat), lambda i, p: (i, p[0], 0))
            return (
                down_blocks,
                (1, part, feat),
                lambda i, p: (i, 2 * (p[0] ^ 2) + which - 1, 0),
            )
        if which == 0:
            return (weights, (1, 1, 1, rows, feat), lambda i, p: (1, 0, i, 0, 0))
        return (weights, (1, 1, 1, part, feat), lambda i, p: (1, 1, i, which - 1, 0))

    def own_slope(which, array):
        return call_once(
            slope_body,
            place,
            local,
            [(cot, one, every), down_of(0, which), unit_of(array, 0)],
            [(array.shape[1:], BF16, (1,) + array.shape[2:], lambda i, p: (i, 0, 0, 0))],
            20,
        )[0]

    slope_ss = own_slope(0, gate)
    at_i = lambda i, p: (0, i, 0, 0)
    strip = (local, 1, sub, tokens)
    shard_u = (n_dp // 2, local * feat // n_dp, rows)

    def up_terms(body, ins, count, gives, span):
        block = (count, n_dp // 2, feat // n_dp, rows)
        wide = (count,) + shard_u
        part_u = (count, n_dp // 2, shard_u[1] // len(gives), rows)
        return call_once(
            body,
            place,
            local,
            ins,
            [
                (part_u, BF16, block, functools.partial(lambda m, i, p: (0, 0, m(i), 0), m))
                for m in gives
            ]
            + [(wide, BF16, block, lambda i, p: (0, 0, i, 0))],
            20,
            scratch=[pltpu.VMEM((n_dp // 2, 2, feat // n_dp, rows), BF16)],
            span=span,
        )

    def up_meet(count, keep, gots):
        piece = (count,) + shard_u[1:]
        return call(
            functools.partial(up_meet_body, len(gots)),
            place,
            (1,),
            [(v, (count,) + v.shape[1:], lambda i, p: (0, 0, 0, 0)) for v in (keep, *gots)],
            [whole_out(piece, BF16)] * 2 + [whole_out((2,) + piece, F32)],
            16,
        )

    def up_again(mine, far):
        piece = mine.shape[1:]
        return call(
            up_again_body, place, (1,), [whole(mine), whole(far)], [whole_out(piece, BF16)], 16
        )[0]

    give_e, keep_e = call_once(
        own_terms_body,
        place,
        local,
        [
            (cot, one, every),
            unit_of(hid, 0),
            (x, one, every),
            (slope_ss, strip, at_i),
        ],
        [whole_out((2,) + shard_u, BF16)] * 2,
        20,
        scratch=[
            pltpu.VMEM((2, part, feat), BF16),
            pltpu.VMEM((n_dp // 2, 2, feat // n_dp, rows), BF16),
        ],
    )
    share, share_z, x_lo, cot_lo = after((share, share_z, x_lo, cot_lo), give_e)
    core_parts = after((share, share_z), x_lo, cot_lo)
    weights = call(
        weights_body,
        place,
        (1,),
        [whole(v) for v in (share, share_z, *map(send_core, core_parts))],
        [whole_out((2, 2, local, 4, quarter, feat), BF16)],
        16,
    )[0].reshape(2, 2, local, rows, feat)

    def near_hidden(source, which):
        up = (
            weights,
            (1, 1, 1, feat, rows),
            lambda j, i, p: (0, j, which * half + i, 0, 0),
        )
        return hidden_of(source, half, up, 0.0)

    give_e = after((give_e,), x_lo, cot_lo)[0]
    first_got = send_core(give_e)
    send_e, far_e, mine_e = up_meet(1, keep_e, [first_got])
    got_e, far_e = send_z(send_e, 1), send_z(far_e, 1)
    x_lo = after((x_lo,), weights, send_e)[0]
    hid_lo, gate_lo = near_hidden(x_lo, 0)
    slope_lo_s = own_slope(1, gate_lo)

    got_e, far_e = after((got_e, far_e), slope_lo_s)
    send_e = up_again(mine_e, far_e)
    last_e = send_z(send_e, 2)

    x_hi = after((x_hi,), send_e)[0]
    hid_hi, gate_hi = near_hidden(x_hi, 1)
    cot_hi, last_e = after((cot_hi, last_e), hid_hi)

    def outputs_of(j, hid, kind):
        return call_once(
            outputs_body,
            place,
            local,
            [down_of(j, which) for which in range(3)]
            + [unit_of(array, j) for array in (hid, hid_lo, hid_hi)],
            [(blocks, kind, one, every)],
            16,
        )[0]

    def added(own, got):
        pairs_at = lambda i, p: (i, 0, 0)
        two = (2, feat, tokens)
        return call(
            add_body,
            place,
            (local // 2,),
            [(own, two, pairs_at), (got, two, pairs_at)],
            [(blocks, BF16, two, pairs_at)],
            20,
        )[0]

    shard = (2, 2, local, part, feat)
    strip_d = (1, part, feat)
    give_own, give_near, keep_d = call_once(
        down_terms_body,
        place,
        local,
        [(cot, one, every), (cot_lo, one, low), (cot_hi, one, high)]
        + [unit_of(hid, 1)]
        + [unit_of(array, j) for j in (0, 1) for array in (hid_lo, hid_hi)],
        [
            (shard[2:], BF16, strip_d, every),
            (shard[1:], BF16, (2,) + strip_d, lambda i, p: (0, i, 0, 0)),
            ((3,) + shard[2:], BF16, (3,) + strip_d, lambda i, p: (0, i, 0, 0)),
        ],
        16,
        scratch=[pltpu.VMEM((3, 2, part, feat), BF16)],
    )
    core_own, core_near = send_core(give_own), send_core(give_near)
    hid_b = after((hid,), give_own)[0]
    near_out = outputs_of(1, hid_b, BF16)
    got_out = send(near_out, 1)
    core_own, core_near = after((core_own, core_near), near_out)
    parts_d = (keep_e, first_got, keep_d, core_own, core_near)
    send_d, mine_d = call(
        down_meet_body,
        place,
        (1,),
        [whole(v) for v in parts_d],
        [whole_out(shard[1:], BF16), whole_out(shard[1:], F32)],
        16,
    )
    got_d = send_z(send_d, 1)
    cot_b, *near_b = after((cot, cot_lo, cot_hi), send_d)
    late = [(1, 0, gate), (1, 1, gate_lo), (1, 2, gate_hi), (0, 2, gate_hi)]
    at_lo = lambda i, p: (0, least(i, half - 1), 0, 0)
    at_hi = lambda i, p: (0, most(i - half, 0), 0, 0)
    turn = lambda spec: (spec[0], spec[1], lambda i, p: spec[2](i % local, p))
    near_up = lambda j: (weights, (1, 1, 1, feat, rows), lambda i, p: (0, j, i, 0, 0))
    slope_sn, slope_lo_n, slope_hi_n, slope_hi_s, near_grads = call_once(
        late_body,
        place,
        2 * local,
        [
            turn(spec)
            for spec in [(cot_b, one, every), (near_b[0], one, low), (near_b[1], one, high)]
            + [down_of(j, which) for j, which, _ in late]
            + [unit_of(array, j) for j, _, array in late]
            + [near_up(0), near_up(1)]
        ]
        + [whole(slope_lo_s)],
        [whole_out(array.shape[1:], BF16) for _, _, array in late]
        + [(blocks, BF16, one, lambda i, p: (i % local, 0, 0))],
        20,
    )
    got_grads = send(near_grads, 2)

    x_b = after((x,), near_grads)[0]
    give_lo, give_hi, keep_u = up_terms(
        up_terms_body,
        [(x_b, one, every), (x_lo, one, low), (x_hi, one, high), (slope_sn, strip, at_i)]
        + [(slope_lo_s, strip, at_lo), (slope_lo_n, strip, at_lo)]
        + [(slope_hi_s, strip, at_hi), (slope_hi_n, strip, at_hi)],
        3,
        [lambda i: least(i, half - 1), lambda i: most(i - half, 0)],
        16.0,
    )
    send_u, far_u, mine_u = up_meet(3, keep_u, [send_core(give_lo), send_core(give_hi)])
    far_u = send_z(far_u, 1)

    got_d = after((got_d,), send_u)[0]
    send_d, mine_d = call(
        down_again_body,
        place,
        (1,),
        [whole(mine_d), whole(got_d)],
        [whole_out(shard[2:], BF16), whole_out(shard[2:], F32)],
        16,
    )
    got_d = send_z(send_d, 2)
    got_u = send_z(after((send_u,), send_d)[0], 1)

    up_b = after((up_blocks,), send_d)[0]
    own_grads = call_once(
        grads_body,
        place,
        local,
        [
            (up_b, (1, feat, rows), lambda i, p: (i, 0, p[0])),
            (up_b, (1, feat, rows), lambda i, p: (i, 0, p[0] ^ 1)),
            (slope_ss, strip, at_i),
            (slope_sn, strip, at_i),
        ],
        [(blocks, F32, one, every)],
        16,
        span=4.0,
    )[0]

    own_out = outputs_of(0, after((hid,), own_grads)[0], F32)
    far_u = after((far_u,), own_out)[0]
    send_u = up_again(mine_u, far_u)
    last_u = send_z(send_u, 2)

    got_d = after((got_d,), send_u)[0]
    sum_d = call(
        functools.partial(down_sum_body, factor),
        place,
        (1,),
        [whole(mine_d), whole(got_d)],
        [whole_out(shard[2:], BF16)],
        8,
    )[0]
    swaps = []
    for device in range(n_dp * n_tensor):
        dp, t = device // n_tensor, device % n_tensor
        z_low, x_at = dp // 2 % 2, t % 2
        home = (dp // 4 * 4 + x_at * 2 + dp % 2) * n_tensor + t // 2 * 2 + z_low
        swaps.append((device, home))
    home_d = lax.ppermute(sum_d, ("dp", "tensor"), swaps)

    got_out = after((got_out,), sum_d)[0]
    outputs = added(own_out, got_out)

    got_u, last_u = after((got_u, last_u), outputs)
    send_u, held = call(
        functools.partial(up_sum_body, factor),
        place,
        (1,),
        [whole(v) for v in (mine_e, got_e, last_e, mine_u, got_u, last_u)],
        [
            whole_out((2,) + shard_u[1:], BF16),
            whole_out((local, feat // n_dp, block_hidden), F32),
        ],
        8,
    )
    got_u = send(send_u, 2)

    got_grads = after((got_grads,), held)[0]
    feature_grads = added(own_grads, got_grads)
    down_grads = after((home_d,), feature_grads)[0].astype(F32)

    got_u = after((got_u,), down_grads)[0]
    up_grads = call(
        place_near_body,
        place,
        (2,),
        [
            (got_u, (1,) + shard_u[1:], lambda a, p: (a, 0, 0)),
            (held, None, None),
        ],
        [
            (
                (local, feat // n_dp, block_hidden),
                F32,
                (local, feat // n_dp, rows),
                lambda a, p: (0, 0, p[0] ^ 2 ^ a),
            )
        ],
        8,
        alias={2: 0},
    )[0]
    wide = (local * feat, tokens)
    return (outputs.reshape(wide), feature_grads.reshape(wide), up_grads, down_grads)


def solution(mesh):
    in_specs = (
        P("tensor", "dp"),
        P("tensor", "dp"),
        P("tensor", None, None),
        P("tensor", None, None),
    )
    out_specs = (
        P("tensor", "dp"),
        P("tensor", "dp"),
        P("tensor", "dp", None),
        P("tensor", "dp", None),
    )
    small = mesh.shape["tensor"] == 4 and mesh.shape["dp"] == 8
    return jax.shard_map(
        square_device if small else generic_device,
        mesh=mesh,
        in_specs=in_specs,
        out_specs=out_specs,
        check_vma=False,
    )
```

```python
import functools
import math

import jax
import jax.numpy as jnp
from jax import lax
from jax.experimental import pallas as pl
from jax.experimental.pallas import tpu as pltpu
from jax.sharding import PartitionSpec as P

BF16 = jnp.bfloat16
F32 = jnp.float32
INV_ROOT2 = 0.7071067811865476
INV_ROOT2PI = 0.3989422804014327
MIB = 1024 * 1024


def gelu_value(value):
    return 0.5 * value * (1.0 + lax.erf(value * INV_ROOT2))


def gelu_slope(value):
    return (
        0.5 * (1.0 + lax.erf(value * INV_ROOT2))
        + value * jnp.exp(-0.5 * value * value) * INV_ROOT2PI
    )


def generic_device(features, cotangent, up_blocks, down_blocks):
    local_blocks, block_feat, block_hidden = up_blocks.shape
    blocks = local_blocks * lax.axis_size("tensor")
    sub = block_hidden // blocks
    tokens_here = features.shape[1]
    factor = 1.0 / math.sqrt(tokens_here * lax.axis_size("dp"))
    x_local = features.reshape(local_blocks, block_feat, tokens_here)
    dy_local = cotangent.reshape(local_blocks, block_feat, tokens_here)
    down_four = down_blocks.reshape(local_blocks, blocks, sub, block_feat)
    preact = jnp.einsum("bdn,bdf->bfn", x_local, up_blocks, preferred_element_type=F32)
    pre_wide = preact.astype(BF16).astype(F32)
    hidden = gelu_value(pre_wide).astype(BF16).reshape(local_blocks, blocks, sub, tokens_here)
    mixed = lax.all_to_all(hidden, "tensor", split_axis=1, concat_axis=0, tiled=True)
    out_three = jnp.einsum("ijsn,jise->jen", mixed, down_four, preferred_element_type=F32)
    outputs = out_three.astype(BF16).reshape(local_blocks * block_feat, tokens_here)
    down_term = jnp.einsum("ijsn,jen->isje", mixed, dy_local, preferred_element_type=F32)
    down_term = down_term.reshape(block_hidden, local_blocks, block_feat)
    back = jnp.einsum("jen,jise->ijsn", dy_local, down_four, preferred_element_type=F32)
    back_home = lax.all_to_all(
        back.astype(BF16), "tensor", split_axis=0, concat_axis=1, tiled=True
    ).reshape(local_blocks, block_hidden, tokens_here)
    slope = (back_home.astype(F32) * gelu_slope(pre_wide)).astype(BF16)
    up_term = jnp.einsum("bdn,bfn->dbf", x_local, slope, preferred_element_type=F32)
    up_share = lax.psum_scatter(up_term, "dp", scatter_dimension=0, tiled=True)
    down_share = lax.psum_scatter(down_term, "dp", scatter_dimension=0, tiled=True)
    dx_three = jnp.einsum("bfn,bdf->bdn", slope, up_blocks, preferred_element_type=F32)
    feature_grads = dx_three.astype(BF16).reshape(local_blocks * block_feat, tokens_here)
    up_grads = jnp.transpose(up_share, (1, 0, 2)) * factor
    down_grads = jnp.transpose(down_share, (1, 0, 2)) * factor
    return (outputs, feature_grads, up_grads, down_grads)


def dot_tn(a, b):
    return lax.dot_general(a, b, (((0,), (0,)), ((), ())), preferred_element_type=F32)


def dot_nn(a, b):
    return lax.dot_general(a, b, (((1,), (0,)), ((), ())), preferred_element_type=F32)


def dot_nt(a, b):
    return lax.dot_general(a, b, (((1,), (1,)), ((), ())), preferred_element_type=F32)


def call(body, place, grid, ins, outs, mib, scratch=(), span=0.0, alias=None):
    return pl.pallas_call(
        body,
        grid_spec=pltpu.PrefetchScalarGridSpec(
            num_scalar_prefetch=1,
            grid=grid,
            in_specs=[
                pl.BlockSpec(b, m) if b else pl.BlockSpec(memory_space=pl.ANY) for _, b, m in ins
            ],
            out_specs=[pl.BlockSpec(b, m) for _, _, b, m in outs],
            scratch_shapes=list(scratch),
        ),
        out_shape=[jax.ShapeDtypeStruct(s, d) for s, d, _, _ in outs],
        input_output_aliases=alias or {},
        compiler_params=pltpu.CompilerParams(vmem_limit_bytes=mib * MIB),
        cost_estimate=pl.CostEstimate(
            flops=int(span * 1e9), bytes_accessed=0, transcendentals=0
        ),
    )(place, *[a for a, _, _ in ins])


def block_of(ref, block, where):
    at = []
    for size, extent, index in zip(block, ref.shape, where):
        if size == extent:
            at.append(slice(None))
        elif isinstance(index, int):
            at.append(slice(index * size, (index + 1) * size))
        else:
            at.append(pl.ds(pl.multiple_of(index * size, size), size))
    return ref.at[tuple(at)]


def call_once(body, place, steps, ins, outs, mib, scratch=(), span=0.0):
    def every_step(place, *refs):
        blocks = [(b, m) for _, b, m in ins] + [(b, m) for _, _, b, m in outs]
        held, rest = refs[: len(blocks)], refs[len(blocks) :]
        for step in range(steps):
            views = [block_of(ref, b, m(step, place)) for ref, (b, m) in zip(held, blocks)]
            body(step, steps, place, *views, *rest)

    return call(
        every_step,
        place,
        (1,),
        [whole(a) for a, _, _ in ins],
        [whole_out(s, d) for s, d, _, _ in outs],
        mib,
        scratch=scratch,
        span=span,
    )


def by_grid(body):
    return lambda place, *refs: body(pl.program_id(0), pl.num_programs(0), place, *refs)


def whole(array):
    rank = array.ndim
    return (array, array.shape, lambda *at: (0,) * rank)


def whole_out(shape, kind):
    rank = len(shape)
    return (shape, kind, shape, lambda *at: (0,) * rank)


def after(values, *earlier):
    return lax.optimization_barrier((tuple(values), earlier))[0]


def square(ref):
    block = ref[...]
    width = block.shape[-1]
    return block.reshape(block.size // width, width)


def hidden_body(place, x_ref, up_ref, hidden_ref, gate_ref):
    pre = dot_tn(square(up_ref), square(x_ref)).astype(BF16).astype(F32)
    half_cdf = 0.5 + 0.5 * lax.erf(pre * INV_ROOT2)
    gate = half_cdf + pre * jnp.exp(-0.5 * pre * pre) * INV_ROOT2PI
    hidden_ref[...] = (pre * half_cdf).astype(BF16).reshape(hidden_ref.shape)
    gate_ref[...] = gate.astype(BF16).reshape(gate_ref.shape)


def weights_body(place, *refs):
    low, core, out_ref = place[1] % 2, place[2], refs[-1]
    for at in range(2):
        out_ref[:, :, :, core * 2 + (low ^ at)] = refs[at][...]
        out_ref[:, :, :, (1 - core) * 2 + (low ^ at)] = refs[2 + at][...]


def halves(step, steps, work, lo, hi):
    if isinstance(step, int):
        work(*(lo if step < steps // 2 else hi))
        return
    pl.when(step < steps // 2)(functools.partial(work, *lo))
    pl.when(step >= steps // 2)(functools.partial(work, *hi))


def stacked(refs, axis=0):
    return jnp.concatenate([square(ref) for ref in refs], axis)


def put_slopes(cot, downs, gates, slopes):
    back = dot_nn(stacked(downs), cot).astype(BF16)
    base = 0
    for gate_ref, slope_ref in zip(gates, slopes):
        gate = square(gate_ref).astype(F32)
        mine = back[base : base + gate.shape[0]].astype(F32)
        slope_ref[...] = (mine * gate).astype(BF16).reshape(slope_ref.shape)
        base += gate.shape[0]


def slope_body(step, steps, place, cot_ref, down_ref, gate_ref, slope_ref):
    put_slopes(square(cot_ref), [down_ref], [gate_ref], [slope_ref])


def late_body(step, steps, place, own_ref, near_lo, near_hi, *refs):
    downs, gates, (up_own, up_near, lo_s), slopes, out_ref = (
        refs[:4],
        refs[4:8],
        refs[8:11],
        refs[11:15],
        refs[15],
    )
    count = steps // 2
    if step < count:
        here = [ref.at[step] for ref in slopes]
        put_slopes(square(own_ref), downs[3:], gates[3:], here[3:])
        near_ref = near_lo if step < count // 2 else near_hi
        put_slopes(square(near_ref), downs[:3], gates[:3], here[:3])
        return
    sn, lo_n, hi_n, hi_s = slopes
    pair = (lo_s, lo_n) if step - count < count // 2 else (hi_s, hi_n)
    strips = [ref.at[:, (step - count) % (count // 2)] for ref in pair]
    out_ref[0] = dot_nn(stacked((up_own, up_near), 1), stacked(strips)).astype(BF16)


def own_terms_body(step, steps, place, cot_ref, hid_ref, x_ref, slope_ref, give_ref, keep_ref, down_s, up_s):
    core = place[2]
    up_s[...] = dot_nt(square(x_ref), square(slope_ref)).astype(BF16).reshape(up_s.shape)
    count = up_s.shape[2]
    strip = slice(step * count, (step + 1) * count)
    give_ref[0, :, strip] = up_s[:, 1 - core]
    keep_ref[0, :, strip] = up_s[:, core]
    down_s[...] = dot_nt(square(hid_ref), square(cot_ref)).astype(BF16).reshape(down_s.shape)
    give_ref[1, step] = down_s[1 - core]
    keep_ref[1, step] = down_s[core]


def down_terms_body(step, steps, place, own_ref, near_lo, near_hi, sn, ns_lo, ns_hi, nn_lo, nn_hi, give_own, give_near, keep_ref, term_s):
    core = place[2]

    def put(pair, terms, give):
        term_s[pair] = terms.astype(BF16).reshape(term_s.shape[1:])
        give[...] = term_s[pair, 1 - core].reshape(give.shape)
        keep_ref[pair, 0] = term_s[pair, core]

    def work(near_ref):
        rows = 2 * term_s.shape[2]
        mixed = dot_nt(stacked((sn, nn_lo, nn_hi)), square(near_ref))
        put(0, mixed[:rows], give_own)
        put(1, dot_nt(stacked((ns_lo, ns_hi)), square(own_ref)), give_near.at[0])
        put(2, mixed[rows:], give_near.at[1])

    halves(step, steps, work, (near_lo,), (near_hi,))


def put_up_term(pair, core, x, slope_ref, give_ref, keep_ref, term_s):
    term_s[...] = dot_nt(x, square(slope_ref)).astype(BF16).reshape(term_s.shape)
    give_ref[pair] = term_s[:, 1 - core]
    keep_ref[pair] = term_s[:, core]


def up_terms_body(step, steps, place, x_ref, x_lo, x_hi, sn, lo_s, lo_n, hi_s, hi_n, give_lo, give_hi, keep_ref, term_s):
    def work(x_near, from_own, from_near, give_ref):
        near = square(x_near)
        for pair, (x, ref) in enumerate(((square(x_ref), sn), (near, from_own), (near, from_near))):
            put_up_term(pair, place[2], x, ref, give_ref, keep_ref, term_s)

    lo, hi = (x_lo, lo_s, lo_n, give_lo), (x_hi, hi_s, hi_n, give_hi)
    halves(step, steps, work, lo, hi)


def outputs_body(step, steps, place, d_own, d_lo, d_hi, hid_ref, lo_ref, hi_ref, out_ref):
    total = dot_tn(stacked((d_own, d_lo, d_hi)), stacked((hid_ref, lo_ref, hi_ref)))
    out_ref[0] = total.astype(out_ref.dtype)


def grads_body(step, steps, place, up_own, up_near, slope_own, slope_near, out_ref):
    out_ref[0] = dot_nn(stacked((up_own, up_near), 1), stacked((slope_own, slope_near)))


def add_body(place, own_ref, got_ref, out_ref):
    out_ref[...] = (own_ref[...] + got_ref[...].astype(F32)).astype(BF16)


def down_meet_body(place, first, first_got, keep_ref, got_own, got_near, send_ref, mine_ref):
    stay = (place[0] ^ place[1]) & 1
    kept = ((first.at[1], keep_ref.at[0]), (keep_ref.at[1], keep_ref.at[2]))
    got = ((first_got.at[1], got_own), (got_near.at[0], got_near.at[1]))
    for j in range(2):

        @pl.when(stay == j)
        def _():
            for i in range(2):
                total = lambda b: kept[i][b][...].astype(F32) + got[i][b][...].astype(F32)
                mine_ref[i] = total(j)
                send_ref[i] = total(1 - j).astype(BF16)


def down_again_body(place, mine_ref, got_ref, send_ref, own_ref):
    stay = (place[0] // 2) ^ (place[1] // 2)
    own_ref[...] = mine_ref[stay] + got_ref[stay].astype(F32)
    send_ref[...] = (mine_ref[1 - stay] + got_ref[1 - stay].astype(F32)).astype(BF16)


def down_sum_body(factor, place, own_ref, got_ref, out_ref):
    out_ref[...] = ((own_ref[...] + got_ref[...].astype(F32)) * factor).astype(BF16)


def up_meet_body(parts, place, keep_ref, *refs):
    gots, sends, mine_ref = refs[:parts], refs[parts:-1], refs[-1]
    rows = gots[0].shape[2]
    for hop in range(4):
        there = place[1] ^ hop
        for at, got_ref in enumerate(gots):
            strip = slice(at * rows, (at + 1) * rows)
            total = keep_ref[:, there, strip].astype(F32) + got_ref[:, there].astype(F32)
            if hop % 2:
                sends[hop // 2][:, strip] = total.astype(BF16)
            else:
                mine_ref[hop // 2, :, strip] = total


def up_again_body(place, mine_ref, far_ref, send_ref):
    send_ref[...] = (mine_ref[1] + far_ref[...].astype(F32)).astype(BF16)


def up_sum_body(factor, place, *refs):
    ins, (send_ref, up_ref) = refs[:6], refs[6:]
    first, total = (
        (own[0] + near[...].astype(F32) + far[...].astype(F32)) * factor
        for own, near, far in (ins[:3], ins[3:])
    )
    send_ref[...] = total[1:].astype(BF16)
    width = send_ref.shape[-1]
    for at, mine in enumerate((first[0], total[0])):
        lanes = pl.ds(pl.multiple_of((place[0] ^ at) * width, width), width)
        up_ref[:, :, lanes] = mine.reshape(*up_ref.shape[:2], width)


def place_body(place, got_ref, home_ref, held_ref, up_ref, down_ref):
    up_ref[...] = got_ref[0].astype(F32).reshape(up_ref.shape)
    down_ref[...] = home_ref[...].astype(F32)


def square_device(features, cotangent, up_blocks, down_blocks):
    local, feat, block_hidden = up_blocks.shape
    tokens = features.shape[1]
    n_dp, n_tensor = lax.axis_size("dp"), lax.axis_size("tensor")
    sub = block_hidden // (local * n_tensor)
    rows = local * sub
    half, part = local // 2, rows // 2
    factor = 1.0 / math.sqrt(tokens * n_dp)
    me = lax.axis_index("tensor").astype(jnp.int32)
    rank = lax.axis_index("dp").astype(jnp.int32)
    z, core = rank >> 1, rank & 1
    place = jnp.stack([me, z, core])
    x = features.reshape(local, feat, tokens)
    cot = cotangent.reshape(local, feat, tokens)
    one = (1, feat, tokens)
    blocks = (local, feat, tokens)
    every = lambda i, p: (i, 0, 0)
    least = lambda a, b: min(a, b) if isinstance(a, int) else jnp.minimum(a, b)
    most = lambda a, b: max(a, b) if isinstance(a, int) else jnp.maximum(a, b)
    low = lambda i, p: (least(i, half - 1), 0, 0)
    high = lambda i, p: (most(i - half, 0), 0, 0)

    def send(value, hop):
        return lax.ppermute(value, "tensor", [(t, t ^ hop) for t in range(n_tensor)])

    def send_z(value, hop):
        return lax.ppermute(value, "dp", [(d, d ^ (2 * hop)) for d in range(n_dp)])

    def send_core(value):
        return lax.ppermute(value, "dp", [(d, d ^ 1) for d in range(n_dp)])

    quarter = rows // 4
    at = (core * 2 + (z & 1)) * quarter
    to_i = jnp.stack(
        [
            lax.dynamic_slice(up_blocks, (0, at, (me ^ k) * rows), (local, quarter, rows))
            for k in (2, 3)
        ]
    )
    down_b = after((down_blocks,), to_i)[0]
    to_j = jnp.stack(
        [
            lax.dynamic_slice(down_b, (0, (me ^ k) * rows + at, 0), (local, quarter, feat))
            for k in (1, 3)
        ]
    )
    from_i, from_j = send(to_i, 2), send(to_j, 1)
    firsts = after((x[:half], x[half:], cot[:half], cot[half:]), to_i, to_j)
    x_lo, cot_lo = send(firsts[0], 2), send(firsts[2], 1)
    x_hi, cot_hi = send(firsts[1], 2), send(firsts[3], 1)

    def hidden_of(source, count, up, span):
        unit = (2, local, count, sub, tokens)
        block = (1, local, 1, sub, tokens)
        where = lambda j, i, p: (j, 0, i, 0, 0)
        return call(
            hidden_body,
            place,
            (2, count),
            [(source, one, lambda j, i, p: (i, 0, 0)), up],
            [(unit, BF16, block, where), (unit, BF16, block, where)],
            16,
        )

    hid, gate = hidden_of(
        x, local, (up_blocks, (1, feat, rows), lambda j, i, p: (i, 0, p[0] ^ j)), 0.0
    )
    from_i, from_j = after((from_i, from_j), hid)
    share = jnp.stack([from_i, from_j])
    share_z = send_z(share, 1)

    def unit_of(array, j):
        return (array, (1, 1) + array.shape[2:], lambda i, p: (j, i, 0, 0, 0))

    def down_of(j, which):
        if j == 0:
            if which == 0:
                return (down_blocks, (1, rows, feat), lambda i, p: (i, p[0], 0))
            return (
                down_blocks,
                (1, part, feat),
                lambda i, p: (i, 2 * (p[0] ^ 2) + which - 1, 0),
            )
        if which == 0:
            return (weights, (1, 1, 1, rows, feat), lambda i, p: (1, 0, i, 0, 0))
        return (weights, (1, 1, 1, part, feat), lambda i, p: (1, 1, i, which - 1, 0))

    def own_slope(which, array):
        return call_once(
            slope_body,
            place,
            local,
            [(cot, one, every), down_of(0, which), unit_of(array, 0)],
            [(array.shape[1:], BF16, (1,) + array.shape[2:], lambda i, p: (i, 0, 0, 0))],
            20,
        )[0]

    slope_ss = own_slope(0, gate)
    at_i = lambda i, p: (0, i, 0, 0)
    strip = (local, 1, sub, tokens)
    shard_u = (n_dp // 2, local * feat // n_dp, rows)

    def up_terms(body, ins, count, gives, span):
        block = (count, n_dp // 2, feat // n_dp, rows)
        wide = (count,) + shard_u
        part_u = (count, n_dp // 2, shard_u[1] // len(gives), rows)
        return call_once(
            body,
            place,
            local,
            ins,
            [
                (part_u, BF16, block, functools.partial(lambda m, i, p: (0, 0, m(i), 0), m))
                for m in gives
            ]
            + [(wide, BF16, block, lambda i, p: (0, 0, i, 0))],
            20,
            scratch=[pltpu.VMEM((n_dp // 2, 2, feat // n_dp, rows), BF16)],
            span=span,
        )

    def up_meet(count, keep, gots):
        piece = (count,) + shard_u[1:]
        return call(
            functools.partial(up_meet_body, len(gots)),
            place,
            (1,),
            [(v, (count,) + v.shape[1:], lambda i, p: (0, 0, 0, 0)) for v in (keep, *gots)],
            [whole_out(piece, BF16)] * 2 + [whole_out((2,) + piece, F32)],
            16,
        )

    def up_again(mine, far):
        piece = mine.shape[1:]
        return call(
            up_again_body, place, (1,), [whole(mine), whole(far)], [whole_out(piece, BF16)], 16
        )[0]

    give_e, keep_e = call_once(
        own_terms_body,
        place,
        local,
        [
            (cot, one, every),
            unit_of(hid, 0),
            (x, one, every),
            (slope_ss, strip, at_i),
        ],
        [whole_out((2,) + shard_u, BF16)] * 2,
        20,
        scratch=[
            pltpu.VMEM((2, part, feat), BF16),
            pltpu.VMEM((n_dp // 2, 2, feat // n_dp, rows), BF16),
        ],
    )
    share, share_z, x_lo, cot_lo = after((share, share_z, x_lo, cot_lo), give_e)
    core_parts = after((share, share_z), x_lo, cot_lo)
    weights = call(
        weights_body,
        place,
        (1,),
        [whole(v) for v in (share, share_z, *map(send_core, core_parts))],
        [whole_out((2, 2, local, 4, quarter, feat), BF16)],
        16,
    )[0].reshape(2, 2, local, rows, feat)

    def near_hidden(source, which):
        up = (
            weights,
            (1, 1, 1, feat, rows),
            lambda j, i, p: (0, j, which * half + i, 0, 0),
        )
        return hidden_of(source, half, up, 0.0)

    give_e = after((give_e,), x_lo, cot_lo)[0]
    first_got = send_core(give_e)
    send_e, far_e, mine_e = up_meet(1, keep_e, [first_got])
    got_e, far_e = send_z(send_e, 1), send_z(far_e, 1)
    x_lo = after((x_lo,), weights, send_e)[0]
    hid_lo, gate_lo = near_hidden(x_lo, 0)
    slope_lo_s = own_slope(1, gate_lo)

    got_e, far_e = after((got_e, far_e), slope_lo_s)
    send_e = up_again(mine_e, far_e)
    last_e = send_z(send_e, 2)

    x_hi = after((x_hi,), send_e)[0]
    hid_hi, gate_hi = near_hidden(x_hi, 1)
    cot_hi, last_e = after((cot_hi, last_e), hid_hi)

    def outputs_of(j, hid, kind):
        return call_once(
            outputs_body,
            place,
            local,
            [down_of(j, which) for which in range(3)]
            + [unit_of(array, j) for array in (hid, hid_lo, hid_hi)],
            [(blocks, kind, one, every)],
            16,
        )[0]

    def added(own, got):
        pairs_at = lambda i, p: (i, 0, 0)
        two = (2, feat, tokens)
        return call(
            add_body,
            place,
            (local // 2,),
            [(own, two, pairs_at), (got, two, pairs_at)],
            [(blocks, BF16, two, pairs_at)],
            20,
        )[0]

    shard = (2, 2, local, part, feat)
    strip_d = (1, part, feat)
    give_own, give_near, keep_d = call_once(
        down_terms_body,
        place,
        local,
        [(cot, one, every), (cot_lo, one, low), (cot_hi, one, high)]
        + [unit_of(hid, 1)]
        + [unit_of(array, j) for j in (0, 1) for array in (hid_lo, hid_hi)],
        [
            (shard[2:], BF16, strip_d, every),
            (shard[1:], BF16, (2,) + strip_d, lambda i, p: (0, i, 0, 0)),
            ((3,) + shard[2:], BF16, (3,) + strip_d, lambda i, p: (0, i, 0, 0)),
        ],
        16,
        scratch=[pltpu.VMEM((3, 2, part, feat), BF16)],
    )
    core_own, core_near = send_core(give_own), send_core(give_near)
    hid_b = after((hid,), give_own)[0]
    near_out = outputs_of(1, hid_b, BF16)
    got_out = send(near_out, 1)
    core_own, core_near = after((core_own, core_near), near_out)
    parts_d = (keep_e, first_got, keep_d, core_own, core_near)
    send_d, mine_d = call(
        down_meet_body,
        place,
        (1,),
        [whole(v) for v in parts_d],
        [whole_out(shard[1:], BF16), whole_out(shard[1:], F32)],
        16,
    )
    got_d = send_z(send_d, 1)
    cot_b, *near_b = after((cot, cot_lo, cot_hi), send_d)
    late = [(1, 0, gate), (1, 1, gate_lo), (1, 2, gate_hi), (0, 2, gate_hi)]
    at_lo = lambda i, p: (0, least(i, half - 1), 0, 0)
    at_hi = lambda i, p: (0, most(i - half, 0), 0, 0)
    turn = lambda spec: (spec[0], spec[1], lambda i, p: spec[2](i % local, p))
    near_up = lambda j: (weights, (1, 1, 1, feat, rows), lambda i, p: (0, j, i, 0, 0))
    slope_sn, slope_lo_n, slope_hi_n, slope_hi_s, near_grads = call_once(
        late_body,
        place,
        2 * local,
        [
            turn(spec)
            for spec in [(cot_b, one, every), (near_b[0], one, low), (near_b[1], one, high)]
            + [down_of(j, which) for j, which, _ in late]
            + [unit_of(array, j) for j, _, array in late]
            + [near_up(0), near_up(1)]
        ]
        + [whole(slope_lo_s)],
        [whole_out(array.shape[1:], BF16) for _, _, array in late]
        + [(blocks, BF16, one, lambda i, p: (i % local, 0, 0))],
        20,
    )
    got_grads = send(near_grads, 2)

    x_b = after((x,), near_grads)[0]
    give_lo, give_hi, keep_u = up_terms(
        up_terms_body,
        [(x_b, one, every), (x_lo, one, low), (x_hi, one, high), (slope_sn, strip, at_i)]
        + [(slope_lo_s, strip, at_lo), (slope_lo_n, strip, at_lo)]
        + [(slope_hi_s, strip, at_hi), (slope_hi_n, strip, at_hi)],
        3,
        [lambda i: least(i, half - 1), lambda i: most(i - half, 0)],
        16.0,
    )
    send_u, far_u, mine_u = up_meet(3, keep_u, [send_core(give_lo), send_core(give_hi)])
    far_u = send_z(far_u, 1)

    got_d = after((got_d,), send_u)[0]
    send_d, mine_d = call(
        down_again_body,
        place,
        (1,),
        [whole(mine_d), whole(got_d)],
        [whole_out(shard[2:], BF16), whole_out(shard[2:], F32)],
        16,
    )
    got_d = send_z(send_d, 2)
    got_u = send_z(after((send_u,), send_d)[0], 1)

    up_b = after((up_blocks,), send_d)[0]
    own_grads = call_once(
        grads_body,
        place,
        local,
        [
            (up_b, (1, feat, rows), lambda i, p: (i, 0, p[0])),
            (up_b, (1, feat, rows), lambda i, p: (i, 0, p[0] ^ 1)),
            (slope_ss, strip, at_i),
            (slope_sn, strip, at_i),
        ],
        [(blocks, F32, one, every)],
        16,
        span=4.0,
    )[0]

    own_out = outputs_of(0, after((hid,), own_grads)[0], F32)
    far_u = after((far_u,), own_out)[0]
    send_u = up_again(mine_u, far_u)
    last_u = send_z(send_u, 2)

    got_out = after((got_out,), send_u)[0]
    outputs = added(own_out, got_out)

    got_d = after((got_d,), outputs)[0]
    sum_d = call(
        functools.partial(down_sum_body, factor),
        place,
        (1,),
        [whole(mine_d), whole(got_d)],
        [whole_out(shard[2:], BF16)],
        8,
    )[0]
    swaps = []
    for device in range(n_dp * n_tensor):
        dp, t = device // n_tensor, device % n_tensor
        z_low, x_at = dp // 2 % 2, t % 2
        home = (dp // 4 * 4 + x_at * 2 + dp % 2) * n_tensor + t // 2 * 2 + z_low
        swaps.append((device, home))
    home_d = lax.ppermute(sum_d, ("dp", "tensor"), swaps)

    got_u, last_u = after((got_u, last_u), sum_d)
    send_u, held = call(
        functools.partial(up_sum_body, factor),
        place,
        (1,),
        [whole(v) for v in (mine_e, got_e, last_e, mine_u, got_u, last_u)],
        [
            whole_out((2,) + shard_u[1:], BF16),
            whole_out((local, feat // n_dp, block_hidden), F32),
        ],
        8,
    )
    got_u = send(send_u, 2)

    got_grads = after((got_grads,), held)[0]
    feature_grads = added(own_grads, got_grads)
    got_u, home_d = after((got_u, home_d), feature_grads)
    pair_d = (local // 2,) + shard[3:]
    up_grads, down_grads = call(
        place_body,
        place,
        (2,),
        [
            (got_u, (1,) + shard_u[1:], lambda a, p: (a, 0, 0)),
            (home_d, pair_d, lambda a, p: (a, 0, 0)),
            (held, None, None),
        ],
        [
            (
                (local, feat // n_dp, block_hidden),
                F32,
                (local, feat // n_dp, rows),
                lambda a, p: (0, 0, p[0] ^ 2 ^ a),
            ),
            ((local,) + shard[3:], F32, pair_d, lambda a, p: (a, 0, 0)),
        ],
        8,
        alias={3: 0},
    )
    wide = (local * feat, tokens)
    return (outputs.reshape(wide), feature_grads.reshape(wide), up_grads, down_grads)


def solution(mesh):
    in_specs = (
        P("tensor", "dp"),
        P("tensor", "dp"),
        P("tensor", None, None),
        P("tensor", None, None),
    )
    out_specs = (
        P("tensor", "dp"),
        P("tensor", "dp"),
        P("tensor", "dp", None),
        P("tensor", "dp", None),
    )
    small = mesh.shape["tensor"] == 4 and mesh.shape["dp"] == 8
    return jax.shard_map(
        square_device if small else generic_device,
        mesh=mesh,
        in_specs=in_specs,
        out_specs=out_specs,
        check_vma=False,
    )
```

```python
import functools
import math

import jax
import jax.numpy as jnp
from jax import lax
from jax.experimental import pallas as pl
from jax.experimental.pallas import tpu as pltpu
from jax.sharding import PartitionSpec as P

BF16 = jnp.bfloat16
F32 = jnp.float32
INV_ROOT2 = 0.7071067811865476
INV_ROOT2PI = 0.3989422804014327
MIB = 1024 * 1024


def gelu_value(value):
    return 0.5 * value * (1.0 + lax.erf(value * INV_ROOT2))


def gelu_slope(value):
    return (
        0.5 * (1.0 + lax.erf(value * INV_ROOT2))
        + value * jnp.exp(-0.5 * value * value) * INV_ROOT2PI
    )


def generic_device(features, cotangent, up_blocks, down_blocks):
    local_blocks, block_feat, block_hidden = up_blocks.shape
    blocks = local_blocks * lax.axis_size("tensor")
    sub = block_hidden // blocks
    tokens_here = features.shape[1]
    factor = 1.0 / math.sqrt(tokens_here * lax.axis_size("dp"))
    x_local = features.reshape(local_blocks, block_feat, tokens_here)
    dy_local = cotangent.reshape(local_blocks, block_feat, tokens_here)
    down_four = down_blocks.reshape(local_blocks, blocks, sub, block_feat)
    preact = jnp.einsum("bdn,bdf->bfn", x_local, up_blocks, preferred_element_type=F32)
    pre_wide = preact.astype(BF16).astype(F32)
    hidden = gelu_value(pre_wide).astype(BF16).reshape(local_blocks, blocks, sub, tokens_here)
    mixed = lax.all_to_all(hidden, "tensor", split_axis=1, concat_axis=0, tiled=True)
    out_three = jnp.einsum("ijsn,jise->jen", mixed, down_four, preferred_element_type=F32)
    outputs = out_three.astype(BF16).reshape(local_blocks * block_feat, tokens_here)
    down_term = jnp.einsum("ijsn,jen->isje", mixed, dy_local, preferred_element_type=F32)
    down_term = down_term.reshape(block_hidden, local_blocks, block_feat)
    back = jnp.einsum("jen,jise->ijsn", dy_local, down_four, preferred_element_type=F32)
    back_home = lax.all_to_all(
        back.astype(BF16), "tensor", split_axis=0, concat_axis=1, tiled=True
    ).reshape(local_blocks, block_hidden, tokens_here)
    slope = (back_home.astype(F32) * gelu_slope(pre_wide)).astype(BF16)
    up_term = jnp.einsum("bdn,bfn->dbf", x_local, slope, preferred_element_type=F32)
    up_share = lax.psum_scatter(up_term, "dp", scatter_dimension=0, tiled=True)
    down_share = lax.psum_scatter(down_term, "dp", scatter_dimension=0, tiled=True)
    dx_three = jnp.einsum("bfn,bdf->bdn", slope, up_blocks, preferred_element_type=F32)
    feature_grads = dx_three.astype(BF16).reshape(local_blocks * block_feat, tokens_here)
    up_grads = jnp.transpose(up_share, (1, 0, 2)) * factor
    down_grads = jnp.transpose(down_share, (1, 0, 2)) * factor
    return (outputs, feature_grads, up_grads, down_grads)


def dot_tn(a, b):
    return lax.dot_general(a, b, (((0,), (0,)), ((), ())), preferred_element_type=F32)


def dot_nn(a, b):
    return lax.dot_general(a, b, (((1,), (0,)), ((), ())), preferred_element_type=F32)


def dot_nt(a, b):
    return lax.dot_general(a, b, (((1,), (1,)), ((), ())), preferred_element_type=F32)


def call(body, place, grid, ins, outs, mib, scratch=(), span=0.0, alias=None):
    return pl.pallas_call(
        body,
        grid_spec=pltpu.PrefetchScalarGridSpec(
            num_scalar_prefetch=1,
            grid=grid,
            in_specs=[
                pl.BlockSpec(b, m) if b else pl.BlockSpec(memory_space=pl.ANY) for _, b, m in ins
            ],
            out_specs=[pl.BlockSpec(b, m) for _, _, b, m in outs],
            scratch_shapes=list(scratch),
        ),
        out_shape=[jax.ShapeDtypeStruct(s, d) for s, d, _, _ in outs],
        input_output_aliases=alias or {},
        compiler_params=pltpu.CompilerParams(vmem_limit_bytes=mib * MIB),
        cost_estimate=pl.CostEstimate(
            flops=int(span * 1e9), bytes_accessed=0, transcendentals=0
        ),
    )(place, *[a for a, _, _ in ins])


def block_of(ref, block, where):
    at = []
    for size, extent, index in zip(block, ref.shape, where):
        if size == extent:
            at.append(slice(None))
        elif isinstance(index, int):
            at.append(slice(index * size, (index + 1) * size))
        else:
            at.append(pl.ds(pl.multiple_of(index * size, size), size))
    return ref.at[tuple(at)]


def call_once(body, place, steps, ins, outs, mib, scratch=(), span=0.0):
    def every_step(place, *refs):
        blocks = [(b, m) for _, b, m in ins] + [(b, m) for _, _, b, m in outs]
        held, rest = refs[: len(blocks)], refs[len(blocks) :]
        for step in range(steps):
            views = [block_of(ref, b, m(step, place)) for ref, (b, m) in zip(held, blocks)]
            body(step, steps, place, *views, *rest)

    return call(
        every_step,
        place,
        (1,),
        [whole(a) for a, _, _ in ins],
        [whole_out(s, d) for s, d, _, _ in outs],
        mib,
        scratch=scratch,
        span=span,
    )


def by_grid(body):
    return lambda place, *refs: body(pl.program_id(0), pl.num_programs(0), place, *refs)


def whole(array):
    rank = array.ndim
    return (array, array.shape, lambda *at: (0,) * rank)


def whole_out(shape, kind):
    rank = len(shape)
    return (shape, kind, shape, lambda *at: (0,) * rank)


def after(values, *earlier):
    return lax.optimization_barrier((tuple(values), earlier))[0]


def square(ref):
    block = ref[...]
    width = block.shape[-1]
    return block.reshape(block.size // width, width)


def hidden_body(place, x_ref, up_ref, hidden_ref, gate_ref):
    pre = dot_tn(square(up_ref), square(x_ref)).astype(BF16).astype(F32)
    half_cdf = 0.5 + 0.5 * lax.erf(pre * INV_ROOT2)
    gate = half_cdf + pre * jnp.exp(-0.5 * pre * pre) * INV_ROOT2PI
    hidden_ref[...] = (pre * half_cdf).astype(BF16).reshape(hidden_ref.shape)
    gate_ref[...] = gate.astype(BF16).reshape(gate_ref.shape)


def weights_body(place, *refs):
    low, core, out_ref = place[1] % 2, place[2], refs[-1]
    for at in range(2):
        out_ref[:, :, :, core * 2 + (low ^ at)] = refs[at][...]
        out_ref[:, :, :, (1 - core) * 2 + (low ^ at)] = refs[2 + at][...]


def halves(step, steps, work, lo, hi):
    if isinstance(step, int):
        work(*(lo if step < steps // 2 else hi))
        return
    pl.when(step < steps // 2)(functools.partial(work, *lo))
    pl.when(step >= steps // 2)(functools.partial(work, *hi))


def stacked(refs, axis=0):
    return jnp.concatenate([square(ref) for ref in refs], axis)


def put_slopes(cot, downs, gates, slopes):
    back = dot_nn(stacked(downs), cot).astype(BF16)
    base = 0
    for gate_ref, slope_ref in zip(gates, slopes):
        gate = square(gate_ref).astype(F32)
        mine = back[base : base + gate.shape[0]].astype(F32)
        slope_ref[...] = (mine * gate).astype(BF16).reshape(slope_ref.shape)
        base += gate.shape[0]


def slope_body(step, steps, place, cot_ref, down_ref, gate_ref, slope_ref):
    put_slopes(square(cot_ref), [down_ref], [gate_ref], [slope_ref])


def late_body(step, steps, place, own_ref, near_lo, near_hi, *refs):
    downs, gates, (up_own, up_near, lo_s), slopes, out_ref = (
        refs[:4],
        refs[4:8],
        refs[8:11],
        refs[11:15],
        refs[15],
    )
    count = steps // 2
    if step < count:
        here = [ref.at[step] for ref in slopes]
        put_slopes(square(own_ref), downs[3:], gates[3:], here[3:])
        near_ref = near_lo if step < count // 2 else near_hi
        put_slopes(square(near_ref), downs[:3], gates[:3], here[:3])
        return
    sn, lo_n, hi_n, hi_s = slopes
    pair = (lo_s, lo_n) if step - count < count // 2 else (hi_s, hi_n)
    strips = [ref.at[:, (step - count) % (count // 2)] for ref in pair]
    out_ref[0] = dot_nn(stacked((up_own, up_near), 1), stacked(strips)).astype(BF16)


def own_terms_body(step, steps, place, cot_ref, hid_ref, x_ref, slope_ref, give_ref, keep_ref, down_s, up_s):
    core = place[2]
    up_s[...] = dot_nt(square(x_ref), square(slope_ref)).astype(BF16).reshape(up_s.shape)
    count = up_s.shape[2]
    strip = slice(step * count, (step + 1) * count)
    give_ref[0, :, strip] = up_s[:, 1 - core]
    keep_ref[0, :, strip] = up_s[:, core]
    down_s[...] = dot_nt(square(hid_ref), square(cot_ref)).astype(BF16).reshape(down_s.shape)
    give_ref[1, step] = down_s[1 - core]
    keep_ref[1, step] = down_s[core]


def down_terms_body(step, steps, place, own_ref, near_lo, near_hi, sn, ns_lo, ns_hi, nn_lo, nn_hi, give_own, give_near, keep_ref, term_s):
    core = place[2]

    def put(pair, terms, give):
        term_s[pair] = terms.astype(BF16).reshape(term_s.shape[1:])
        give[...] = term_s[pair, 1 - core].reshape(give.shape)
        keep_ref[pair, 0] = term_s[pair, core]

    def work(near_ref):
        rows = 2 * term_s.shape[2]
        mixed = dot_nt(stacked((sn, nn_lo, nn_hi)), square(near_ref))
        put(0, mixed[:rows], give_own)
        put(1, dot_nt(stacked((ns_lo, ns_hi)), square(own_ref)), give_near.at[0])
        put(2, mixed[rows:], give_near.at[1])

    halves(step, steps, work, (near_lo,), (near_hi,))


def put_up_term(pair, core, x, slope_ref, give_ref, keep_ref, term_s):
    term_s[...] = dot_nt(x, square(slope_ref)).astype(BF16).reshape(term_s.shape)
    give_ref[pair] = term_s[:, 1 - core]
    keep_ref[pair] = term_s[:, core]


def up_terms_body(step, steps, place, x_ref, x_lo, x_hi, sn, lo_s, lo_n, hi_s, hi_n, give_lo, give_hi, keep_ref, term_s):
    def work(x_near, from_own, from_near, give_ref):
        near = square(x_near)
        for pair, (x, ref) in enumerate(((square(x_ref), sn), (near, from_own), (near, from_near))):
            put_up_term(pair, place[2], x, ref, give_ref, keep_ref, term_s)

    lo, hi = (x_lo, lo_s, lo_n, give_lo), (x_hi, hi_s, hi_n, give_hi)
    halves(step, steps, work, lo, hi)


def outputs_body(step, steps, place, d_own, d_lo, d_hi, hid_ref, lo_ref, hi_ref, out_ref):
    total = dot_tn(stacked((d_own, d_lo, d_hi)), stacked((hid_ref, lo_ref, hi_ref)))
    out_ref[0] = total.astype(out_ref.dtype)


def grads_body(step, steps, place, up_own, up_near, slope_own, slope_near, out_ref):
    out_ref[0] = dot_nn(stacked((up_own, up_near), 1), stacked((slope_own, slope_near)))


def add_body(place, own_ref, got_ref, out_ref):
    out_ref[...] = (own_ref[...] + got_ref[...].astype(F32)).astype(BF16)


def down_meet_body(place, first, first_got, keep_ref, got_own, got_near, send_ref, mine_ref):
    stay = (place[0] ^ place[1]) & 1
    kept = ((first.at[1], keep_ref.at[0]), (keep_ref.at[1], keep_ref.at[2]))
    got = ((first_got.at[1], got_own), (got_near.at[0], got_near.at[1]))
    for j in range(2):

        @pl.when(stay == j)
        def _():
            for i in range(2):
                total = lambda b: kept[i][b][...].astype(F32) + got[i][b][...].astype(F32)
                mine_ref[i] = total(j)
                send_ref[i] = total(1 - j).astype(BF16)


def down_again_body(place, mine_ref, got_ref, send_ref, own_ref):
    stay = (place[0] // 2) ^ (place[1] // 2)
    own_ref[...] = mine_ref[stay] + got_ref[stay].astype(F32)
    send_ref[...] = (mine_ref[1 - stay] + got_ref[1 - stay].astype(F32)).astype(BF16)


def down_sum_body(factor, place, own_ref, got_ref, out_ref):
    out_ref[...] = ((own_ref[...] + got_ref[...].astype(F32)) * factor).astype(BF16)


def up_meet_body(parts, place, keep_ref, *refs):
    gots, sends, mine_ref = refs[:parts], refs[parts:-1], refs[-1]
    rows = gots[0].shape[2]
    for hop in range(4):
        there = place[1] ^ hop
        for at, got_ref in enumerate(gots):
            strip = slice(at * rows, (at + 1) * rows)
            total = keep_ref[:, there, strip].astype(F32) + got_ref[:, there].astype(F32)
            if hop % 2:
                sends[hop // 2][:, strip] = total.astype(BF16)
            else:
                mine_ref[hop // 2, :, strip] = total


def up_again_body(place, mine_ref, far_ref, send_ref):
    send_ref[...] = (mine_ref[1] + far_ref[...].astype(F32)).astype(BF16)


def up_sum_body(factor, place, *refs):
    ins, (send_ref, up_ref) = refs[:6], refs[6:]
    first, total = (
        (own[0] + near[...].astype(F32) + far[...].astype(F32)) * factor
        for own, near, far in (ins[:3], ins[3:])
    )
    send_ref[...] = total[1:].astype(BF16)
    width = send_ref.shape[-1]
    for at, mine in enumerate((first[0], total[0])):
        lanes = pl.ds(pl.multiple_of((place[0] ^ at) * width, width), width)
        up_ref[:, :, lanes] = mine.reshape(*up_ref.shape[:2], width)


def place_body(place, got_ref, home_ref, held_ref, up_ref, down_ref):
    up_ref[...] = got_ref[0].astype(F32).reshape(up_ref.shape)
    down_ref[...] = home_ref[...].astype(F32)


def square_device(features, cotangent, up_blocks, down_blocks):
    local, feat, block_hidden = up_blocks.shape
    tokens = features.shape[1]
    n_dp, n_tensor = lax.axis_size("dp"), lax.axis_size("tensor")
    sub = block_hidden // (local * n_tensor)
    rows = local * sub
    half, part = local // 2, rows // 2
    factor = 1.0 / math.sqrt(tokens * n_dp)
    me = lax.axis_index("tensor").astype(jnp.int32)
    rank = lax.axis_index("dp").astype(jnp.int32)
    z, core = rank >> 1, rank & 1
    place = jnp.stack([me, z, core])
    x = features.reshape(local, feat, tokens)
    cot = cotangent.reshape(local, feat, tokens)
    one = (1, feat, tokens)
    blocks = (local, feat, tokens)
    every = lambda i, p: (i, 0, 0)
    least = lambda a, b: min(a, b) if isinstance(a, int) else jnp.minimum(a, b)
    most = lambda a, b: max(a, b) if isinstance(a, int) else jnp.maximum(a, b)
    low = lambda i, p: (least(i, half - 1), 0, 0)
    high = lambda i, p: (most(i - half, 0), 0, 0)

    def send(value, hop):
        return lax.ppermute(value, "tensor", [(t, t ^ hop) for t in range(n_tensor)])

    def send_z(value, hop):
        return lax.ppermute(value, "dp", [(d, d ^ (2 * hop)) for d in range(n_dp)])

    def send_core(value):
        return lax.ppermute(value, "dp", [(d, d ^ 1) for d in range(n_dp)])

    quarter = rows // 4
    at = (core * 2 + (z & 1)) * quarter
    to_i = jnp.stack(
        [
            lax.dynamic_slice(up_blocks, (0, at, (me ^ k) * rows), (local, quarter, rows))
            for k in (2, 3)
        ]
    )
    down_b = after((down_blocks,), to_i)[0]
    to_j = jnp.stack(
        [
            lax.dynamic_slice(down_b, (0, (me ^ k) * rows + at, 0), (local, quarter, feat))
            for k in (1, 3)
        ]
    )
    from_i, from_j = send(to_i, 2), send(to_j, 1)
    firsts = after((x[:half], x[half:], cot[:half], cot[half:]), to_i, to_j)
    x_lo, cot_lo = send(firsts[0], 2), send(firsts[2], 1)
    x_hi, cot_hi = send(firsts[1], 2), send(firsts[3], 1)

    def hidden_of(source, count, up, span):
        unit = (2, local, count, sub, tokens)
        block = (1, local, 1, sub, tokens)
        where = lambda j, i, p: (j, 0, i, 0, 0)
        return call(
            hidden_body,
            place,
            (2, count),
            [(source, one, lambda j, i, p: (i, 0, 0)), up],
            [(unit, BF16, block, where), (unit, BF16, block, where)],
            16,
        )

    hid, gate = hidden_of(
        x, local, (up_blocks, (1, feat, rows), lambda j, i, p: (i, 0, p[0] ^ j)), 0.0
    )
    from_i, from_j = after((from_i, from_j), hid)
    share = jnp.stack([from_i, from_j])
    share_z = send_z(share, 1)

    def unit_of(array, j):
        return (array, (1, 1) + array.shape[2:], lambda i, p: (j, i, 0, 0, 0))

    def down_of(j, which):
        if j == 0:
            if which == 0:
                return (down_blocks, (1, rows, feat), lambda i, p: (i, p[0], 0))
            return (
                down_blocks,
                (1, part, feat),
                lambda i, p: (i, 2 * (p[0] ^ 2) + which - 1, 0),
            )
        if which == 0:
            return (weights, (1, 1, 1, rows, feat), lambda i, p: (1, 0, i, 0, 0))
        return (weights, (1, 1, 1, part, feat), lambda i, p: (1, 1, i, which - 1, 0))

    def own_slope(which, array):
        return call_once(
            slope_body,
            place,
            local,
            [(cot, one, every), down_of(0, which), unit_of(array, 0)],
            [(array.shape[1:], BF16, (1,) + array.shape[2:], lambda i, p: (i, 0, 0, 0))],
            20,
        )[0]

    slope_ss = own_slope(0, gate)
    at_i = lambda i, p: (0, i, 0, 0)
    strip = (local, 1, sub, tokens)
    shard_u = (n_dp // 2, local * feat // n_dp, rows)

    def up_terms(body, ins, count, gives, span):
        block = (count, n_dp // 2, feat // n_dp, rows)
        wide = (count,) + shard_u
        part_u = (count, n_dp // 2, shard_u[1] // len(gives), rows)
        return call_once(
            body,
            place,
            local,
            ins,
            [
                (part_u, BF16, block, functools.partial(lambda m, i, p: (0, 0, m(i), 0), m))
                for m in gives
            ]
            + [(wide, BF16, block, lambda i, p: (0, 0, i, 0))],
            20,
            scratch=[pltpu.VMEM((n_dp // 2, 2, feat // n_dp, rows), BF16)],
            span=span,
        )

    def up_meet(count, keep, gots):
        piece = (count,) + shard_u[1:]
        return call(
            functools.partial(up_meet_body, len(gots)),
            place,
            (1,),
            [(v, (count,) + v.shape[1:], lambda i, p: (0, 0, 0, 0)) for v in (keep, *gots)],
            [whole_out(piece, BF16)] * 2 + [whole_out((2,) + piece, F32)],
            16,
        )

    def up_again(mine, far):
        piece = mine.shape[1:]
        return call(
            up_again_body, place, (1,), [whole(mine), whole(far)], [whole_out(piece, BF16)], 16
        )[0]

    give_e, keep_e = call_once(
        own_terms_body,
        place,
        local,
        [
            (cot, one, every),
            unit_of(hid, 0),
            (x, one, every),
            (slope_ss, strip, at_i),
        ],
        [whole_out((2,) + shard_u, BF16)] * 2,
        20,
        scratch=[
            pltpu.VMEM((2, part, feat), BF16),
            pltpu.VMEM((n_dp // 2, 2, feat // n_dp, rows), BF16),
        ],
    )
    share, share_z, x_lo, cot_lo = after((share, share_z, x_lo, cot_lo), give_e)
    core_parts = after((share, share_z), x_lo, cot_lo)
    weights = call(
        weights_body,
        place,
        (1,),
        [whole(v) for v in (share, share_z, *map(send_core, core_parts))],
        [whole_out((2, 2, local, 4, quarter, feat), BF16)],
        16,
    )[0].reshape(2, 2, local, rows, feat)

    def near_hidden(source, which):
        up = (
            weights,
            (1, 1, 1, feat, rows),
            lambda j, i, p: (0, j, which * half + i, 0, 0),
        )
        return hidden_of(source, half, up, 0.0)

    give_e = after((give_e,), x_lo, cot_lo)[0]
    first_got = send_core(give_e)
    send_e, far_e, mine_e = up_meet(1, keep_e, [first_got])
    got_e, far_e = send_z(send_e, 1), send_z(far_e, 1)
    x_lo = after((x_lo,), weights, send_e)[0]
    hid_lo, gate_lo = near_hidden(x_lo, 0)
    slope_lo_s = own_slope(1, gate_lo)

    got_e, far_e = after((got_e, far_e), slope_lo_s)
    send_e = up_again(mine_e, far_e)
    last_e = send_z(send_e, 2)

    x_hi = after((x_hi,), send_e)[0]
    hid_hi, gate_hi = near_hidden(x_hi, 1)
    cot_hi, last_e = after((cot_hi, last_e), hid_hi)

    def outputs_of(j, hid, kind):
        return call_once(
            outputs_body,
            place,
            local,
            [down_of(j, which) for which in range(3)]
            + [unit_of(array, j) for array in (hid, hid_lo, hid_hi)],
            [(blocks, kind, one, every)],
            16,
        )[0]

    def added(own, got):
        pairs_at = lambda i, p: (i, 0, 0)
        two = (2, feat, tokens)
        return call(
            add_body,
            place,
            (local // 2,),
            [(own, two, pairs_at), (got, two, pairs_at)],
            [(blocks, BF16, two, pairs_at)],
            20,
        )[0]

    shard = (2, 2, local, part, feat)
    strip_d = (1, part, feat)
    give_own, give_near, keep_d = call_once(
        down_terms_body,
        place,
        local,
        [(cot, one, every), (cot_lo, one, low), (cot_hi, one, high)]
        + [unit_of(hid, 1)]
        + [unit_of(array, j) for j in (0, 1) for array in (hid_lo, hid_hi)],
        [
            (shard[2:], BF16, strip_d, every),
            (shard[1:], BF16, (2,) + strip_d, lambda i, p: (0, i, 0, 0)),
            ((3,) + shard[2:], BF16, (3,) + strip_d, lambda i, p: (0, i, 0, 0)),
        ],
        16,
        scratch=[pltpu.VMEM((3, 2, part, feat), BF16)],
    )
    core_own, core_near = send_core(give_own), send_core(give_near)
    hid_b = after((hid,), give_own)[0]
    near_out = outputs_of(1, hid_b, BF16)
    got_out = send(near_out, 1)
    core_own, core_near = after((core_own, core_near), near_out)
    parts_d = (keep_e, first_got, keep_d, core_own, core_near)
    send_d, mine_d = call(
        down_meet_body,
        place,
        (1,),
        [whole(v) for v in parts_d],
        [whole_out(shard[1:], BF16), whole_out(shard[1:], F32)],
        16,
    )
    got_d = send_z(send_d, 1)
    cot_b, *near_b = after((cot, cot_lo, cot_hi), send_d)
    late = [(1, 0, gate), (1, 1, gate_lo), (1, 2, gate_hi), (0, 2, gate_hi)]
    at_lo = lambda i, p: (0, least(i, half - 1), 0, 0)
    at_hi = lambda i, p: (0, most(i - half, 0), 0, 0)
    turn = lambda spec: (spec[0], spec[1], lambda i, p: spec[2](i % local, p))
    near_up = lambda j: (weights, (1, 1, 1, feat, rows), lambda i, p: (0, j, i, 0, 0))
    slope_sn, slope_lo_n, slope_hi_n, slope_hi_s, near_grads = call_once(
        late_body,
        place,
        2 * local,
        [
            turn(spec)
            for spec in [(cot_b, one, every), (near_b[0], one, low), (near_b[1], one, high)]
            + [down_of(j, which) for j, which, _ in late]
            + [unit_of(array, j) for j, _, array in late]
            + [near_up(0), near_up(1)]
        ]
        + [whole(slope_lo_s)],
        [whole_out(array.shape[1:], BF16) for _, _, array in late]
        + [(blocks, BF16, one, lambda i, p: (i % local, 0, 0))],
        20,
    )
    got_grads = send(near_grads, 2)

    x_b = after((x,), near_grads)[0]
    give_lo, give_hi, keep_u = up_terms(
        up_terms_body,
        [(x_b, one, every), (x_lo, one, low), (x_hi, one, high), (slope_sn, strip, at_i)]
        + [(slope_lo_s, strip, at_lo), (slope_lo_n, strip, at_lo)]
        + [(slope_hi_s, strip, at_hi), (slope_hi_n, strip, at_hi)],
        3,
        [lambda i: least(i, half - 1), lambda i: most(i - half, 0)],
        16.0,
    )
    send_u, far_u, mine_u = up_meet(3, keep_u, [send_core(give_lo), send_core(give_hi)])
    far_u = send_z(far_u, 1)

    got_d = after((got_d,), send_u)[0]
    send_d, mine_d = call(
        down_again_body,
        place,
        (1,),
        [whole(mine_d), whole(got_d)],
        [whole_out(shard[2:], BF16), whole_out(shard[2:], F32)],
        16,
    )
    got_d = send_z(send_d, 2)
    got_u = send_z(after((send_u,), send_d)[0], 1)

    up_b = after((up_blocks,), send_d)[0]
    own_grads = call_once(
        grads_body,
        place,
        local,
        [
            (up_b, (1, feat, rows), lambda i, p: (i, 0, p[0])),
            (up_b, (1, feat, rows), lambda i, p: (i, 0, p[0] ^ 1)),
            (slope_ss, strip, at_i),
            (slope_sn, strip, at_i),
        ],
        [(blocks, F32, one, every)],
        16,
        span=4.0,
    )[0]

    own_out = outputs_of(0, after((hid,), own_grads)[0], F32)
    far_u = after((far_u,), own_out)[0]
    send_u = up_again(mine_u, far_u)
    last_u = send_z(send_u, 2)

    got_d = after((got_d,), send_u)[0]
    sum_d = call(
        functools.partial(down_sum_body, factor),
        place,
        (1,),
        [whole(mine_d), whole(got_d)],
        [whole_out(shard[2:], BF16)],
        8,
    )[0]
    swaps = []
    for device in range(n_dp * n_tensor):
        dp, t = device // n_tensor, device % n_tensor
        z_low, x_at = dp // 2 % 2, t % 2
        home = (dp // 4 * 4 + x_at * 2 + dp % 2) * n_tensor + t // 2 * 2 + z_low
        swaps.append((device, home))
    home_d = lax.ppermute(sum_d, ("dp", "tensor"), swaps)

    got_out = after((got_out,), sum_d)[0]
    outputs = added(own_out, got_out)

    got_u, last_u = after((got_u, last_u), outputs)
    send_u, held = call(
        functools.partial(up_sum_body, factor),
        place,
        (1,),
        [whole(v) for v in (mine_e, got_e, last_e, mine_u, got_u, last_u)],
        [
            whole_out((2,) + shard_u[1:], BF16),
            whole_out((local, feat // n_dp, block_hidden), F32),
        ],
        8,
    )
    got_u = send(send_u, 2)

    got_grads = after((got_grads,), held)[0]
    feature_grads = added(own_grads, got_grads)
    got_u, home_d = after((got_u, home_d), feature_grads)
    pair_d = (local // 2,) + shard[3:]
    up_grads, down_grads = call(
        place_body,
        place,
        (2,),
        [
            (got_u, (1,) + shard_u[1:], lambda a, p: (a, 0, 0)),
            (home_d, pair_d, lambda a, p: (a, 0, 0)),
            (held, None, None),
        ],
        [
            (
                (local, feat // n_dp, block_hidden),
                F32,
                (local, feat // n_dp, rows),
                lambda a, p: (0, 0, p[0] ^ 2 ^ a),
            ),
            ((local,) + shard[3:], F32, pair_d, lambda a, p: (a, 0, 0)),
        ],
        8,
        alias={3: 0},
    )
    wide = (local * feat, tokens)
    return (outputs.reshape(wide), feature_grads.reshape(wide), up_grads, down_grads)


def solution(mesh):
    in_specs = (
        P("tensor", "dp"),
        P("tensor", "dp"),
        P("tensor", None, None),
        P("tensor", None, None),
    )
    out_specs = (
        P("tensor", "dp"),
        P("tensor", "dp"),
        P("tensor", "dp", None),
        P("tensor", "dp", None),
    )
    small = mesh.shape["tensor"] == 4 and mesh.shape["dp"] == 8
    return jax.shard_map(
        square_device if small else generic_device,
        mesh=mesh,
        in_specs=in_specs,
        out_specs=out_specs,
        check_vma=False,
    )
```

```python
import functools
import math

import jax
import jax.numpy as jnp
from jax import lax
from jax.experimental import pallas as pl
from jax.experimental.pallas import tpu as pltpu
from jax.sharding import PartitionSpec as P

BF16 = jnp.bfloat16
F32 = jnp.float32
INV_ROOT2 = 0.7071067811865476
INV_ROOT2PI = 0.3989422804014327
MIB = 1024 * 1024


def gelu_value(value):
    return 0.5 * value * (1.0 + lax.erf(value * INV_ROOT2))


def gelu_slope(value):
    return (
        0.5 * (1.0 + lax.erf(value * INV_ROOT2))
        + value * jnp.exp(-0.5 * value * value) * INV_ROOT2PI
    )


def generic_device(features, cotangent, up_blocks, down_blocks):
    local_blocks, block_feat, block_hidden = up_blocks.shape
    blocks = local_blocks * lax.axis_size("tensor")
    sub = block_hidden // blocks
    tokens_here = features.shape[1]
    factor = 1.0 / math.sqrt(tokens_here * lax.axis_size("dp"))
    x_local = features.reshape(local_blocks, block_feat, tokens_here)
    dy_local = cotangent.reshape(local_blocks, block_feat, tokens_here)
    down_four = down_blocks.reshape(local_blocks, blocks, sub, block_feat)
    preact = jnp.einsum("bdn,bdf->bfn", x_local, up_blocks, preferred_element_type=F32)
    pre_wide = preact.astype(BF16).astype(F32)
    hidden = gelu_value(pre_wide).astype(BF16).reshape(local_blocks, blocks, sub, tokens_here)
    mixed = lax.all_to_all(hidden, "tensor", split_axis=1, concat_axis=0, tiled=True)
    out_three = jnp.einsum("ijsn,jise->jen", mixed, down_four, preferred_element_type=F32)
    outputs = out_three.astype(BF16).reshape(local_blocks * block_feat, tokens_here)
    down_term = jnp.einsum("ijsn,jen->isje", mixed, dy_local, preferred_element_type=F32)
    down_term = down_term.reshape(block_hidden, local_blocks, block_feat)
    back = jnp.einsum("jen,jise->ijsn", dy_local, down_four, preferred_element_type=F32)
    back_home = lax.all_to_all(
        back.astype(BF16), "tensor", split_axis=0, concat_axis=1, tiled=True
    ).reshape(local_blocks, block_hidden, tokens_here)
    slope = (back_home.astype(F32) * gelu_slope(pre_wide)).astype(BF16)
    up_term = jnp.einsum("bdn,bfn->dbf", x_local, slope, preferred_element_type=F32)
    up_share = lax.psum_scatter(up_term, "dp", scatter_dimension=0, tiled=True)
    down_share = lax.psum_scatter(down_term, "dp", scatter_dimension=0, tiled=True)
    dx_three = jnp.einsum("bfn,bdf->bdn", slope, up_blocks, preferred_element_type=F32)
    feature_grads = dx_three.astype(BF16).reshape(local_blocks * block_feat, tokens_here)
    up_grads = jnp.transpose(up_share, (1, 0, 2)) * factor
    down_grads = jnp.transpose(down_share, (1, 0, 2)) * factor
    return (outputs, feature_grads, up_grads, down_grads)


def dot_tn(a, b):
    return lax.dot_general(a, b, (((0,), (0,)), ((), ())), preferred_element_type=F32)


def dot_nn(a, b):
    return lax.dot_general(a, b, (((1,), (0,)), ((), ())), preferred_element_type=F32)


def dot_nt(a, b):
    return lax.dot_general(a, b, (((1,), (1,)), ((), ())), preferred_element_type=F32)


def call(body, place, grid, ins, outs, mib, scratch=(), span=0.0, alias=None):
    return pl.pallas_call(
        body,
        grid_spec=pltpu.PrefetchScalarGridSpec(
            num_scalar_prefetch=1,
            grid=grid,
            in_specs=[
                pl.BlockSpec(b, m) if b else pl.BlockSpec(memory_space=pl.ANY) for _, b, m in ins
            ],
            out_specs=[pl.BlockSpec(b, m) for _, _, b, m in outs],
            scratch_shapes=list(scratch),
        ),
        out_shape=[jax.ShapeDtypeStruct(s, d) for s, d, _, _ in outs],
        input_output_aliases=alias or {},
        compiler_params=pltpu.CompilerParams(vmem_limit_bytes=mib * MIB),
        cost_estimate=pl.CostEstimate(
            flops=int(span * 1e9), bytes_accessed=0, transcendentals=0
        ),
    )(place, *[a for a, _, _ in ins])


def block_of(ref, block, where):
    at = []
    for size, extent, index in zip(block, ref.shape, where):
        if size == extent:
            at.append(slice(None))
        elif isinstance(index, int):
            at.append(slice(index * size, (index + 1) * size))
        else:
            at.append(pl.ds(pl.multiple_of(index * size, size), size))
    return ref.at[tuple(at)]


def call_once(body, place, steps, ins, outs, mib, scratch=(), span=0.0):
    def every_step(place, *refs):
        blocks = [(b, m) for _, b, m in ins] + [(b, m) for _, _, b, m in outs]
        held, rest = refs[: len(blocks)], refs[len(blocks) :]
        for step in range(steps):
            views = [block_of(ref, b, m(step, place)) for ref, (b, m) in zip(held, blocks)]
            body(step, steps, place, *views, *rest)

    return call(
        every_step,
        place,
        (1,),
        [whole(a) for a, _, _ in ins],
        [whole_out(s, d) for s, d, _, _ in outs],
        mib,
        scratch=scratch,
        span=span,
    )


def by_grid(body):
    return lambda place, *refs: body(pl.program_id(0), pl.num_programs(0), place, *refs)


def whole(array):
    rank = array.ndim
    return (array, array.shape, lambda *at: (0,) * rank)


def whole_out(shape, kind):
    rank = len(shape)
    return (shape, kind, shape, lambda *at: (0,) * rank)


def after(values, *earlier):
    return lax.optimization_barrier((tuple(values), earlier))[0]


def square(ref):
    block = ref[...]
    width = block.shape[-1]
    return block.reshape(block.size // width, width)


def hidden_body(place, x_ref, up_ref, hidden_ref, gate_ref):
    pre = dot_tn(square(up_ref), square(x_ref)).astype(BF16).astype(F32)
    half_cdf = 0.5 + 0.5 * lax.erf(pre * INV_ROOT2)
    gate = half_cdf + pre * jnp.exp(-0.5 * pre * pre) * INV_ROOT2PI
    hidden_ref[...] = (pre * half_cdf).astype(BF16).reshape(hidden_ref.shape)
    gate_ref[...] = gate.astype(BF16).reshape(gate_ref.shape)


def weights_body(place, *refs):
    low, core, out_ref = place[1] % 2, place[2], refs[-1]
    for at in range(2):
        out_ref[:, :, :, core * 2 + (low ^ at)] = refs[at][...]
        out_ref[:, :, :, (1 - core) * 2 + (low ^ at)] = refs[2 + at][...]


def halves(step, steps, work, lo, hi):
    if isinstance(step, int):
        work(*(lo if step < steps // 2 else hi))
        return
    pl.when(step < steps // 2)(functools.partial(work, *lo))
    pl.when(step >= steps // 2)(functools.partial(work, *hi))


def stacked(refs, axis=0):
    return jnp.concatenate([square(ref) for ref in refs], axis)


def put_slopes(cot, downs, gates, slopes):
    back = dot_nn(stacked(downs), cot).astype(BF16)
    base = 0
    for gate_ref, slope_ref in zip(gates, slopes):
        gate = square(gate_ref).astype(F32)
        mine = back[base : base + gate.shape[0]].astype(F32)
        slope_ref[...] = (mine * gate).astype(BF16).reshape(slope_ref.shape)
        base += gate.shape[0]


def slope_body(step, steps, place, cot_ref, down_ref, gate_ref, slope_ref):
    put_slopes(square(cot_ref), [down_ref], [gate_ref], [slope_ref])


def late_body(step, steps, place, own_ref, near_lo, near_hi, *refs):
    downs, gates, (up_own, up_near, lo_s), slopes, out_ref = (
        refs[:4],
        refs[4:8],
        refs[8:11],
        refs[11:15],
        refs[15],
    )
    count = steps // 2
    if step < count:
        here = [ref.at[step] for ref in slopes]
        put_slopes(square(own_ref), downs[3:], gates[3:], here[3:])
        near_ref = near_lo if step < count // 2 else near_hi
        put_slopes(square(near_ref), downs[:3], gates[:3], here[:3])
        return
    sn, lo_n, hi_n, hi_s = slopes
    pair = (lo_s, lo_n) if step - count < count // 2 else (hi_s, hi_n)
    strips = [ref.at[:, (step - count) % (count // 2)] for ref in pair]
    out_ref[0] = dot_nn(stacked((up_own, up_near), 1), stacked(strips)).astype(BF16)


def own_terms_body(step, steps, place, cot_ref, hid_ref, x_ref, slope_ref, give_ref, keep_ref, down_s, up_s):
    core = place[2]
    up_s[...] = dot_nt(square(x_ref), square(slope_ref)).astype(BF16).reshape(up_s.shape)
    count = up_s.shape[2]
    strip = slice(step * count, (step + 1) * count)
    give_ref[0, :, strip] = up_s[:, 1 - core]
    keep_ref[0, :, strip] = up_s[:, core]
    down_s[...] = dot_nt(square(hid_ref), square(cot_ref)).astype(BF16).reshape(down_s.shape)
    give_ref[1, step] = down_s[1 - core]
    keep_ref[1, step] = down_s[core]


def down_terms_body(step, steps, place, own_ref, near_lo, near_hi, sn, ns_lo, ns_hi, nn_lo, nn_hi, give_own, give_near, keep_ref, term_s):
    core = place[2]

    def put(pair, terms, give):
        term_s[pair] = terms.astype(BF16).reshape(term_s.shape[1:])
        give[...] = term_s[pair, 1 - core].reshape(give.shape)
        keep_ref[pair, 0] = term_s[pair, core]

    def work(near_ref):
        rows = 2 * term_s.shape[2]
        mixed = dot_nt(stacked((sn, nn_lo, nn_hi)), square(near_ref))
        put(0, mixed[:rows], give_own)
        put(1, dot_nt(stacked((ns_lo, ns_hi)), square(own_ref)), give_near.at[0])
        put(2, mixed[rows:], give_near.at[1])

    halves(step, steps, work, (near_lo,), (near_hi,))


def put_up_term(pair, core, x, slope_ref, give_ref, keep_ref, term_s):
    term_s[...] = dot_nt(x, square(slope_ref)).astype(BF16).reshape(term_s.shape)
    give_ref[pair] = term_s[:, 1 - core]
    keep_ref[pair] = term_s[:, core]


def up_terms_body(step, steps, place, x_ref, x_lo, x_hi, sn, lo_s, lo_n, hi_s, hi_n, give_lo, give_hi, keep_ref, term_s):
    def work(x_near, from_own, from_near, give_ref):
        near = square(x_near)
        for pair, (x, ref) in enumerate(((square(x_ref), sn), (near, from_own), (near, from_near))):
            put_up_term(pair, place[2], x, ref, give_ref, keep_ref, term_s)

    lo, hi = (x_lo, lo_s, lo_n, give_lo), (x_hi, hi_s, hi_n, give_hi)
    halves(step, steps, work, lo, hi)


def outputs_body(step, steps, place, d_own, d_lo, d_hi, hid_ref, lo_ref, hi_ref, out_ref):
    total = dot_tn(stacked((d_own, d_lo, d_hi)), stacked((hid_ref, lo_ref, hi_ref)))
    out_ref[0] = total.astype(out_ref.dtype)


def grads_body(step, steps, place, up_own, up_near, slope_own, slope_near, out_ref):
    out_ref[0] = dot_nn(stacked((up_own, up_near), 1), stacked((slope_own, slope_near)))


def add_body(place, own_ref, got_ref, out_ref):
    out_ref[...] = (own_ref[...] + got_ref[...].astype(F32)).astype(BF16)


def down_meet_body(place, first, first_got, keep_ref, got_own, got_near, send_ref, mine_ref):
    stay = (place[0] ^ place[1]) & 1
    kept = ((first.at[1], keep_ref.at[0]), (keep_ref.at[1], keep_ref.at[2]))
    got = ((first_got.at[1], got_own), (got_near.at[0], got_near.at[1]))
    for j in range(2):

        @pl.when(stay == j)
        def _():
            for i in range(2):
                total = lambda b: kept[i][b][...].astype(F32) + got[i][b][...].astype(F32)
                mine_ref[i] = total(j)
                send_ref[i] = total(1 - j).astype(BF16)


def down_again_body(place, mine_ref, got_ref, send_ref, own_ref):
    stay = (place[0] // 2) ^ (place[1] // 2)
    own_ref[...] = mine_ref[stay] + got_ref[stay].astype(F32)
    send_ref[...] = (mine_ref[1 - stay] + got_ref[1 - stay].astype(F32)).astype(BF16)


def down_sum_body(factor, place, own_ref, got_ref, out_ref):
    out_ref[...] = ((own_ref[...] + got_ref[...].astype(F32)) * factor).astype(BF16)


def up_meet_body(parts, place, keep_ref, *refs):
    gots, sends, mine_ref = refs[:parts], refs[parts:-1], refs[-1]
    rows = gots[0].shape[2]
    for hop in range(4):
        there = place[1] ^ hop
        for at, got_ref in enumerate(gots):
            strip = slice(at * rows, (at + 1) * rows)
            total = keep_ref[:, there, strip].astype(F32) + got_ref[:, there].astype(F32)
            if hop % 2:
                sends[hop // 2][:, strip] = total.astype(BF16)
            else:
                mine_ref[hop // 2, :, strip] = total


def up_again_body(place, mine_ref, far_ref, send_ref):
    send_ref[...] = (mine_ref[1] + far_ref[...].astype(F32)).astype(BF16)


def up_sum_body(factor, place, *refs):
    ins, (send_ref, up_ref) = refs[:6], refs[6:]
    first, total = (
        (own[0] + near[...].astype(F32) + far[...].astype(F32)) * factor
        for own, near, far in (ins[:3], ins[3:])
    )
    send_ref[...] = total[1:].astype(BF16)
    width = send_ref.shape[-1]
    for at, mine in enumerate((first[0], total[0])):
        lanes = pl.ds(pl.multiple_of((place[0] ^ at) * width, width), width)
        up_ref[:, :, lanes] = mine.reshape(*up_ref.shape[:2], width)


def place_body(place, got_ref, home_ref, held_ref, up_ref, down_ref):
    up_ref[...] = got_ref[0].astype(F32).reshape(up_ref.shape)
    down_ref[...] = home_ref[...].astype(F32)


def square_device(features, cotangent, up_blocks, down_blocks):
    local, feat, block_hidden = up_blocks.shape
    tokens = features.shape[1]
    n_dp, n_tensor = lax.axis_size("dp"), lax.axis_size("tensor")
    sub = block_hidden // (local * n_tensor)
    rows = local * sub
    half, part = local // 2, rows // 2
    factor = 1.0 / math.sqrt(tokens * n_dp)
    me = lax.axis_index("tensor").astype(jnp.int32)
    rank = lax.axis_index("dp").astype(jnp.int32)
    z, core = rank >> 1, rank & 1
    place = jnp.stack([me, z, core])
    x = features.reshape(local, feat, tokens)
    cot = cotangent.reshape(local, feat, tokens)
    one = (1, feat, tokens)
    blocks = (local, feat, tokens)
    every = lambda i, p: (i, 0, 0)
    least = lambda a, b: min(a, b) if isinstance(a, int) else jnp.minimum(a, b)
    most = lambda a, b: max(a, b) if isinstance(a, int) else jnp.maximum(a, b)
    low = lambda i, p: (least(i, half - 1), 0, 0)
    high = lambda i, p: (most(i - half, 0), 0, 0)

    def send(value, hop):
        return lax.ppermute(value, "tensor", [(t, t ^ hop) for t in range(n_tensor)])

    def send_z(value, hop):
        return lax.ppermute(value, "dp", [(d, d ^ (2 * hop)) for d in range(n_dp)])

    def send_core(value):
        return lax.ppermute(value, "dp", [(d, d ^ 1) for d in range(n_dp)])

    quarter = rows // 4
    at = (core * 2 + (z & 1)) * quarter
    to_i = jnp.stack(
        [
            lax.dynamic_slice(up_blocks, (0, at, (me ^ k) * rows), (local, quarter, rows))
            for k in (2, 3)
        ]
    )
    down_b = after((down_blocks,), to_i)[0]
    to_j = jnp.stack(
        [
            lax.dynamic_slice(down_b, (0, (me ^ k) * rows + at, 0), (local, quarter, feat))
            for k in (1, 3)
        ]
    )
    from_i, from_j = send(to_i, 2), send(to_j, 1)
    firsts = after((x[:half], x[half:], cot[:half], cot[half:]), to_i, to_j)
    x_lo, cot_lo = send(firsts[0], 2), send(firsts[2], 1)
    x_hi, cot_hi = send(firsts[1], 2), send(firsts[3], 1)

    def hidden_of(source, count, up, span):
        unit = (2, local, count, sub, tokens)
        block = (1, local, 1, sub, tokens)
        where = lambda j, i, p: (j, 0, i, 0, 0)
        return call(
            hidden_body,
            place,
            (2, count),
            [(source, one, lambda j, i, p: (i, 0, 0)), up],
            [(unit, BF16, block, where), (unit, BF16, block, where)],
            16,
        )

    hid, gate = hidden_of(
        x, local, (up_blocks, (1, feat, rows), lambda j, i, p: (i, 0, p[0] ^ j)), 0.0
    )
    from_i, from_j = after((from_i, from_j), hid)
    share = jnp.stack([from_i, from_j])
    share_z = send_z(share, 1)

    def unit_of(array, j):
        return (array, (1, 1) + array.shape[2:], lambda i, p: (j, i, 0, 0, 0))

    def down_of(j, which):
        if j == 0:
            if which == 0:
                return (down_blocks, (1, rows, feat), lambda i, p: (i, p[0], 0))
            return (
                down_blocks,
                (1, part, feat),
                lambda i, p: (i, 2 * (p[0] ^ 2) + which - 1, 0),
            )
        if which == 0:
            return (weights, (1, 1, 1, rows, feat), lambda i, p: (1, 0, i, 0, 0))
        return (weights, (1, 1, 1, part, feat), lambda i, p: (1, 1, i, which - 1, 0))

    def own_slope(which, array):
        return call_once(
            slope_body,
            place,
            local,
            [(cot, one, every), down_of(0, which), unit_of(array, 0)],
            [(array.shape[1:], BF16, (1,) + array.shape[2:], lambda i, p: (i, 0, 0, 0))],
            20,
        )[0]

    slope_ss = own_slope(0, gate)
    at_i = lambda i, p: (0, i, 0, 0)
    strip = (local, 1, sub, tokens)
    shard_u = (n_dp // 2, local * feat // n_dp, rows)

    def up_terms(body, ins, count, gives, span):
        block = (count, n_dp // 2, feat // n_dp, rows)
        wide = (count,) + shard_u
        part_u = (count, n_dp // 2, shard_u[1] // len(gives), rows)
        return call_once(
            body,
            place,
            local,
            ins,
            [
                (part_u, BF16, block, functools.partial(lambda m, i, p: (0, 0, m(i), 0), m))
                for m in gives
            ]
            + [(wide, BF16, block, lambda i, p: (0, 0, i, 0))],
            20,
            scratch=[pltpu.VMEM((n_dp // 2, 2, feat // n_dp, rows), BF16)],
            span=span,
        )

    def up_meet(count, keep, gots):
        piece = (count,) + shard_u[1:]
        return call(
            functools.partial(up_meet_body, len(gots)),
            place,
            (1,),
            [(v, (count,) + v.shape[1:], lambda i, p: (0, 0, 0, 0)) for v in (keep, *gots)],
            [whole_out(piece, BF16)] * 2 + [whole_out((2,) + piece, F32)],
            16,
        )

    def up_again(mine, far):
        piece = mine.shape[1:]
        return call(
            up_again_body, place, (1,), [whole(mine), whole(far)], [whole_out(piece, BF16)], 16
        )[0]

    give_e, keep_e = call_once(
        own_terms_body,
        place,
        local,
        [
            (cot, one, every),
            unit_of(hid, 0),
            (x, one, every),
            (slope_ss, strip, at_i),
        ],
        [whole_out((2,) + shard_u, BF16)] * 2,
        20,
        scratch=[
            pltpu.VMEM((2, part, feat), BF16),
            pltpu.VMEM((n_dp // 2, 2, feat // n_dp, rows), BF16),
        ],
    )
    share, share_z, x_lo, cot_lo = after((share, share_z, x_lo, cot_lo), give_e)
    core_parts = after((share, share_z), x_lo, cot_lo)
    weights = call(
        weights_body,
        place,
        (1,),
        [whole(v) for v in (share, share_z, *map(send_core, core_parts))],
        [whole_out((2, 2, local, 4, quarter, feat), BF16)],
        16,
    )[0].reshape(2, 2, local, rows, feat)

    def near_hidden(source, which):
        up = (
            weights,
            (1, 1, 1, feat, rows),
            lambda j, i, p: (0, j, which * half + i, 0, 0),
        )
        return hidden_of(source, half, up, 0.0)

    give_e = after((give_e,), x_lo, cot_lo)[0]
    first_got = send_core(give_e)
    send_e, far_e, mine_e = up_meet(1, keep_e, [first_got])
    got_e, far_e = send_z(send_e, 1), send_z(far_e, 1)
    x_lo = after((x_lo,), weights, send_e)[0]
    hid_lo, gate_lo = near_hidden(x_lo, 0)
    slope_lo_s = own_slope(1, gate_lo)

    got_e, far_e = after((got_e, far_e), slope_lo_s)
    send_e = up_again(mine_e, far_e)
    last_e = send_z(send_e, 2)

    x_hi = after((x_hi,), send_e)[0]
    hid_hi, gate_hi = near_hidden(x_hi, 1)
    cot_hi, last_e = after((cot_hi, last_e), hid_hi)

    def outputs_of(j, hid, kind):
        return call_once(
            outputs_body,
            place,
            local,
            [down_of(j, which) for which in range(3)]
            + [unit_of(array, j) for array in (hid, hid_lo, hid_hi)],
            [(blocks, kind, one, every)],
            16,
        )[0]

    def added(own, got):
        return call(
            add_body,
            place,
            (local,),
            [(own, one, every), (got, one, every)],
            [(blocks, BF16, one, every)],
            20,
        )[0]

    shard = (2, 2, local, part, feat)
    strip_d = (1, part, feat)
    give_own, give_near, keep_d = call_once(
        down_terms_body,
        place,
        local,
        [(cot, one, every), (cot_lo, one, low), (cot_hi, one, high)]
        + [unit_of(hid, 1)]
        + [unit_of(array, j) for j in (0, 1) for array in (hid_lo, hid_hi)],
        [
            (shard[2:], BF16, strip_d, every),
            (shard[1:], BF16, (2,) + strip_d, lambda i, p: (0, i, 0, 0)),
            ((3,) + shard[2:], BF16, (3,) + strip_d, lambda i, p: (0, i, 0, 0)),
        ],
        16,
        scratch=[pltpu.VMEM((3, 2, part, feat), BF16)],
    )
    core_own, core_near = send_core(give_own), send_core(give_near)
    hid_b = after((hid,), give_own)[0]
    near_out = outputs_of(1, hid_b, BF16)
    got_out = send(near_out, 1)
    core_own, core_near = after((core_own, core_near), near_out)
    parts_d = (keep_e, first_got, keep_d, core_own, core_near)
    send_d, mine_d = call(
        down_meet_body,
        place,
        (1,),
        [whole(v) for v in parts_d],
        [whole_out(shard[1:], BF16), whole_out(shard[1:], F32)],
        16,
    )
    got_d = send_z(send_d, 1)
    cot_b, *near_b = after((cot, cot_lo, cot_hi), send_d)
    late = [(1, 0, gate), (1, 1, gate_lo), (1, 2, gate_hi), (0, 2, gate_hi)]
    at_lo = lambda i, p: (0, least(i, half - 1), 0, 0)
    at_hi = lambda i, p: (0, most(i - half, 0), 0, 0)
    turn = lambda spec: (spec[0], spec[1], lambda i, p: spec[2](i % local, p))
    near_up = lambda j: (weights, (1, 1, 1, feat, rows), lambda i, p: (0, j, i, 0, 0))
    slope_sn, slope_lo_n, slope_hi_n, slope_hi_s, near_grads = call_once(
        late_body,
        place,
        2 * local,
        [
            turn(spec)
            for spec in [(cot_b, one, every), (near_b[0], one, low), (near_b[1], one, high)]
            + [down_of(j, which) for j, which, _ in late]
            + [unit_of(array, j) for j, _, array in late]
            + [near_up(0), near_up(1)]
        ]
        + [whole(slope_lo_s)],
        [whole_out(array.shape[1:], BF16) for _, _, array in late]
        + [(blocks, BF16, one, lambda i, p: (i % local, 0, 0))],
        20,
    )
    got_grads = send(near_grads, 2)

    x_b = after((x,), near_grads)[0]
    give_lo, give_hi, keep_u = up_terms(
        up_terms_body,
        [(x_b, one, every), (x_lo, one, low), (x_hi, one, high), (slope_sn, strip, at_i)]
        + [(slope_lo_s, strip, at_lo), (slope_lo_n, strip, at_lo)]
        + [(slope_hi_s, strip, at_hi), (slope_hi_n, strip, at_hi)],
        3,
        [lambda i: least(i, half - 1), lambda i: most(i - half, 0)],
        16.0,
    )
    send_u, far_u, mine_u = up_meet(3, keep_u, [send_core(give_lo), send_core(give_hi)])
    far_u = send_z(far_u, 1)

    got_d = after((got_d,), send_u)[0]
    send_d, mine_d = call(
        down_again_body,
        place,
        (1,),
        [whole(mine_d), whole(got_d)],
        [whole_out(shard[2:], BF16), whole_out(shard[2:], F32)],
        16,
    )
    got_d = send_z(send_d, 2)

    up_b = after((up_blocks,), send_d)[0]
    own_grads = call_once(
        grads_body,
        place,
        local,
        [
            (up_b, (1, feat, rows), lambda i, p: (i, 0, p[0])),
            (up_b, (1, feat, rows), lambda i, p: (i, 0, p[0] ^ 1)),
            (slope_ss, strip, at_i),
            (slope_sn, strip, at_i),
        ],
        [(blocks, F32, one, every)],
        16,
        span=4.0,
    )[0]

    own_out = outputs_of(0, after((hid,), own_grads)[0], F32)
    far_u = after((far_u,), own_out)[0]
    next_u = up_again(mine_u, far_u)
    last_u = send_z(next_u, 2)
    got_u = send_z(after((send_u,), next_u)[0], 1)

    got_d = after((got_d,), send_u)[0]
    sum_d = call(
        functools.partial(down_sum_body, factor),
        place,
        (1,),
        [whole(mine_d), whole(got_d)],
        [whole_out(shard[2:], BF16)],
        8,
    )[0]
    swaps = []
    for device in range(n_dp * n_tensor):
        dp, t = device // n_tensor, device % n_tensor
        z_low, x_at = dp // 2 % 2, t % 2
        home = (dp // 4 * 4 + x_at * 2 + dp % 2) * n_tensor + t // 2 * 2 + z_low
        swaps.append((device, home))
    home_d = lax.ppermute(sum_d, ("dp", "tensor"), swaps)

    got_out = after((got_out,), sum_d)[0]
    outputs = added(own_out, got_out)

    got_u, last_u = after((got_u, last_u), outputs)
    send_u, held = call(
        functools.partial(up_sum_body, factor),
        place,
        (1,),
        [whole(v) for v in (mine_e, got_e, last_e, mine_u, got_u, last_u)],
        [
            whole_out((2,) + shard_u[1:], BF16),
            whole_out((local, feat // n_dp, block_hidden), F32),
        ],
        8,
    )
    got_u = send(send_u, 2)

    got_grads = after((got_grads,), held)[0]
    feature_grads = added(own_grads, got_grads)
    got_u, home_d = after((got_u, home_d), feature_grads)
    pair_d = (local // 2,) + shard[3:]
    up_grads, down_grads = call(
        place_body,
        place,
        (2,),
        [
            (got_u, (1,) + shard_u[1:], lambda a, p: (a, 0, 0)),
            (home_d, pair_d, lambda a, p: (a, 0, 0)),
            (held, None, None),
        ],
        [
            (
                (local, feat // n_dp, block_hidden),
                F32,
                (local, feat // n_dp, rows),
                lambda a, p: (0, 0, p[0] ^ 2 ^ a),
            ),
            ((local,) + shard[3:], F32, pair_d, lambda a, p: (a, 0, 0)),
        ],
        8,
        alias={3: 0},
    )
    wide = (local * feat, tokens)
    return (outputs.reshape(wide), feature_grads.reshape(wide), up_grads, down_grads)


def solution(mesh):
    in_specs = (
        P("tensor", "dp"),
        P("tensor", "dp"),
        P("tensor", None, None),
        P("tensor", None, None),
    )
    out_specs = (
        P("tensor", "dp"),
        P("tensor", "dp"),
        P("tensor", "dp", None),
        P("tensor", "dp", None),
    )
    small = mesh.shape["tensor"] == 4 and mesh.shape["dp"] == 8
    return jax.shard_map(
        square_device if small else generic_device,
        mesh=mesh,
        in_specs=in_specs,
        out_specs=out_specs,
        check_vma=False,
    )
```
